32 devices in a mesh: group: 4 (over y, x), dev: 8 (over z, core).
Axes of the slice: x: 2, y: 2, z: 4, core: 2. Of those that a mesh axis runs over, the one named last changes fastest.
Arguments:
- queries: bfloat16 [16384, 1024], P(('group', 'dev')), may hold values from -2.5 to 2.5
- passages: bfloat16 [512, 32, 1024], P(('group', 'dev')), may hold values from -2.5 to 2.5
- block_ids: int32 [32, 4], replicated, may hold values from 0 to 31, as said below
- positives: int32 [16384], P(('group', 'dev')), may hold values from 0 to 511
Outputs:
- query_loss: float32 [16384], P(('group', 'dev'))
- query_grad: bfloat16 [16384, 1024], P(('group', 'dev'))
- passage_grad: bfloat16 [512, 32, 1024], P(('group', 'dev'))
The draws below stay inside these ranges and needn't reach their ends.
Inputs may be any that keep to these rules, and one draw needn't show every extreme that they name: `block_ids`: row b names passage block b first (it holds the positives of query block b), then three other passage blocks, all four different.
All inputs are finite; a program needn't handle non-finite values.
Results may differ from the reference program's by a relative error of at most 0.0045.
Values may be sent and summed in bfloat16 or wider, within the bound.
No kernel may reach another device: no remote copies, remote signals or barrier semaphores. Data moves between devices by JAX's collectives and lax.ppermute only.
A program may use at most 64 MiB of HBM per device.

```python
import jax
import jax.numpy as jnp
from jax import lax

D = 1024
BLOCK = 512
REFS = 4
QBLOCKS = 32
NPB = 32
QUERIES = 16384


def make_ids(key):
    id_key = jax.random.fold_in(key, 2)
    key_picks, ordering_random_key = jax.random.split(id_key)
    count = QBLOCKS
    picks = jax.random.randint(key_picks, (count, 3, 3), 0, count)
    ranks = jnp.min(picks, axis=2)
    order = jax.random.permutation(ordering_random_key, count).astype(jnp.int32)
    hot_ids = order[ranks]
    own_ids = jnp.arange(count, dtype=jnp.int32)
    first = jnp.where(hot_ids[:, 0] == own_ids, (own_ids + 1) % count, hot_ids[:, 0])
    bad_second = (hot_ids[:, 1] == own_ids) | (hot_ids[:, 1] == first)
    spare_second = jnp.where(first == (own_ids + 2) % count, (own_ids + 3) % count, (own_ids + 2) % count)
    second = jnp.where(bad_second, spare_second, hot_ids[:, 1])
    bad_third = (hot_ids[:, 2] == own_ids) | (hot_ids[:, 2] == first) | (hot_ids[:, 2] == second)
    cand_five = (own_ids + 5) % count
    cand_six = (own_ids + 6) % count
    cand_seven = (own_ids + 7) % count
    five_free = (cand_five != first) & (cand_five != second)
    six_free = (cand_six != first) & (cand_six != second)
    spare_third = jnp.where(five_free, cand_five, jnp.where(six_free, cand_six, cand_seven))
    third = jnp.where(bad_third, spare_third, hot_ids[:, 2])
    return jnp.stack([own_ids, first, second, third], axis=1).astype(jnp.int32)


def make_passages(key):
    pass_key = jax.random.fold_in(key, 1)
    key_base = jax.random.fold_in(pass_key, 0)
    base = 0.25 * jax.random.truncated_normal(key_base, -10.0, 10.0, (BLOCK, NPB, D), jnp.float32)
    return base


def draw_block_ids(key, part):
    return make_ids(key)


def draw_passages(key, part):
    return make_passages(key).astype(jnp.bfloat16)


def draw_queries(key, part):
    query_key = jax.random.fold_in(key, 3)
    base = 0.25 * jax.random.truncated_normal(query_key, -10.0, 10.0, (QUERIES, D), jnp.float32)
    return base.astype(jnp.bfloat16)


def touch_ends(result, rng, least, high):
    index_at = [jax.random.randint(jax.random.fold_in(rng, axis), (), 0, length) for axis, length in enumerate(result.shape)]
    longest = result.shape.index(max(result.shape))
    beside = index_at[:longest] + [(index_at[longest] + 1) % result.shape[longest]] + index_at[longest + 1:]
    return result.at[tuple(index_at)].set(least).at[tuple(beside)].set(high)


def setup_inputs(seed: int = 0) -> dict:
    keys = jax.random.split(jax.random.key(seed), 5)
    queries = draw_queries(jax.random.fold_in(keys[4], 71), 0)
    passages = draw_passages(jax.random.fold_in(keys[4], 71), 0)
    block_ids = draw_block_ids(jax.random.fold_in(keys[4], 71), 0)
    positives = touch_ends(jax.random.randint(keys[3], (QUERIES,), 0, BLOCK), jax.random.fold_in(keys[3], 1), 0, BLOCK - 1).astype(jnp.int32)
    return {"queries": queries, "passages": passages, "block_ids": block_ids, "positives": positives}


SCORE_SCALE = 0.8


def reference(queries, passages, block_ids, positives):
    query_block_list = queries.reshape(QBLOCKS, BLOCK, D)
    positive_rows = positives.reshape(QBLOCKS, BLOCK)
    columns = jnp.arange(REFS * BLOCK, dtype=jnp.int32)

    def one_block(grad_sum, pieces):
        block_rows, listed, chosen = pieces
        gathered = passages[:, listed, :]
        candidate_passages = jnp.transpose(gathered, (1, 0, 2)).reshape(REFS * BLOCK, D)
        logits = SCORE_SCALE * jnp.dot(block_rows, candidate_passages.T, preferred_element_type=jnp.float32)
        highest = jnp.max(logits, axis=1, keepdims=True)
        log_total = highest + jnp.log(jnp.sum(jnp.exp(logits - highest), axis=1, keepdims=True))
        target = (columns[None, :] == chosen[:, None]).astype(jnp.float32)
        picked = jnp.sum(logits * target, axis=1)
        block_loss = log_total[:, 0] - picked
        logits_gradient = (jnp.exp(logits - log_total) - target).astype(jnp.bfloat16)
        block_grad = (SCORE_SCALE * jnp.dot(logits_gradient, candidate_passages, preferred_element_type=jnp.float32)).astype(jnp.bfloat16)
        contribution = (SCORE_SCALE * jnp.dot(logits_gradient.T, block_rows, preferred_element_type=jnp.float32)).astype(jnp.bfloat16)
        shaped = jnp.transpose(contribution.reshape(REFS, BLOCK, D), (1, 0, 2)).astype(jnp.float32)
        grad_sum = grad_sum.at[:, listed, :].add(shaped)
        return grad_sum, (block_loss, block_grad)

    start = jnp.zeros((BLOCK, NPB, D), jnp.float32)
    grad_sum, (losses, grads) = lax.scan(one_block, start, (query_block_list, block_ids, positive_rows))
    return losses.reshape(QUERIES), grads.reshape(QUERIES, D), grad_sum.astype(jnp.bfloat16)
```

```python
import functools

import jax
import jax.numpy as jnp
from jax import lax
from jax.experimental import pallas as pl
from jax.experimental.pallas import tpu as pltpu
from jax.sharding import Mesh
from jax.sharding import PartitionSpec as P

SCALE = 0.8
PLANES = 4
BF16 = jnp.bfloat16
F32 = jnp.float32
PLANE = ("group", "rank")
VMEM = pl.BlockSpec(memory_space=pltpu.VMEM)


def params():
    return pltpu.CompilerParams(vmem_limit_bytes=40 << 20)


def gather_kernel(ids, rows_ref, out_ref):
    slab = pl.program_id(0)
    height = rows_ref.shape[1]
    picks = out_ref.shape[1] // height
    for i in range(picks):
        out_ref[0, i * height : (i + 1) * height, :] = rows_ref[ids[slab * picks + i]]


def gather_rows(ids, rows, slabs):
    blocks, height, width = rows.shape
    picks = ids.shape[0] // slabs
    return pl.pallas_call(
        gather_kernel,
        grid_spec=pltpu.PrefetchScalarGridSpec(
            num_scalar_prefetch=1,
            grid=(slabs,),
            in_specs=[pl.BlockSpec((blocks, height, width), lambda s, ids: (0, 0, 0))],
            out_specs=pl.BlockSpec((1, picks * height, width), lambda s, ids: (s, 0, 0)),
        ),
        out_shape=jax.ShapeDtypeStruct((slabs, picks * height, width), rows.dtype),
        compiler_params=params(),
        name="gather_rows",
        cost_estimate=pl.CostEstimate(flops=0, bytes_accessed=6 << 20, transcendentals=0),
    )(ids, rows)


def segment_kernel(with_start, ids, slabs_ref, *refs):
    start_ref = refs[0] if with_start else None
    out_ref, total = refs[-2:]
    slab = pl.program_id(0)
    height = total.shape[1]
    picks = slabs_ref.shape[1] // height

    @pl.when(slab == 0)
    def _():
        if with_start:
            total[...] = start_ref[...].astype(F32)
        else:
            total[...] = jnp.zeros_like(total)

    for i in range(picks):
        n = ids[slab * picks + i]
        total[n] += slabs_ref[0, i * height : (i + 1) * height, :].astype(F32)

    @pl.when(slab == pl.num_programs(0) - 1)
    def _():
        out_ref[...] = total[...].astype(out_ref.dtype)


def segment_rows(ids, slabs, blocks, start=None):
    count, depth, width = slabs.shape
    picks = ids.shape[0] // count
    height = depth // picks
    whole = pl.BlockSpec((blocks, height, width), lambda s, ids: (0, 0, 0))
    extra = [] if start is None else [start]
    return pl.pallas_call(
        functools.partial(segment_kernel, start is not None),
        grid_spec=pltpu.PrefetchScalarGridSpec(
            num_scalar_prefetch=1,
            grid=(count,),
            in_specs=[pl.BlockSpec((1, depth, width), lambda s, ids: (s, 0, 0))] + [whole] * len(extra),
            out_specs=whole,
            scratch_shapes=[pltpu.VMEM((blocks, height, width), F32)],
        ),
        out_shape=jax.ShapeDtypeStruct((blocks, height, width), BF16),
        compiler_params=params(),
        name="segment_rows",
        cost_estimate=pl.CostEstimate(flops=1 << 21, bytes_accessed=6 << 20, transcendentals=0),
    )(ids, slabs, *extra)


def candidates(slabs_ref, q):
    slabs, depth, width = slabs_ref.shape
    half = depth // 2
    return slabs_ref[:, q * half : (q + 1) * half, :].reshape(slabs * half, width)


def hits(shape, target_row):
    return lax.broadcasted_iota(jnp.int32, shape, 0) == target_row


def logits_kernel(queries_ref, others_ref, slabs_ref, target_ref, logits_ref, stats_ref):
    for q, block_ref in enumerate((queries_ref, others_ref)):
        block = lax.dot_general(
            candidates(slabs_ref, q), block_ref[...], (((1,), (1,)), ((), ())), preferred_element_type=F32
        )
        block = SCALE * block
        logits_ref[q] = block
        top = jnp.max(block, axis=0, keepdims=True)
        stats_ref[4 * q : 4 * q + 1, :] = top
        stats_ref[4 * q + 1 : 4 * q + 2, :] = jnp.sum(jnp.exp(block - top), axis=0, keepdims=True)
        hit = hits(block.shape, target_ref[q : q + 1, :])
        stats_ref[4 * q + 2 : 4 * q + 3, :] = jnp.sum(jnp.where(hit, block, 0.0), axis=0, keepdims=True)
        stats_ref[4 * q + 3 : 4 * q + 4, :] = jnp.zeros_like(top)


def half_logits(queries, others, slabs, target):
    size = queries.shape[0]
    rows = slabs.shape[0] * slabs.shape[1] // 2
    return pl.pallas_call(
        logits_kernel,
        in_specs=[VMEM] * 4,
        out_specs=[VMEM] * 2,
        out_shape=[jax.ShapeDtypeStruct((2, rows, size), F32), jax.ShapeDtypeStruct((8, size), F32)],
        compiler_params=params(),
        name="half_logits",
        cost_estimate=pl.CostEstimate(flops=1 << 30, bytes_accessed=6 << 20, transcendentals=1 << 19),
    )(queries, others, slabs, target)


def joined(a, b):
    top = jnp.maximum(a[0], b[0])
    return top, a[1] * jnp.exp(a[0] - top) + b[1] * jnp.exp(b[0] - top), a[2] + b[2]


def stat_rows(ref, q):
    return [ref[4 * q + i : 4 * q + i + 1, :] for i in range(3)]


def log_totals(first_ref, second_ref, partner_first_ref, partner_second_ref):
    out = []
    for q in range(2):
        here = joined(stat_rows(first_ref, q), stat_rows(second_ref, q))
        there = joined(stat_rows(partner_first_ref, 1 - q), stat_rows(partner_second_ref, 1 - q))
        top, total, pick = joined(here, there)
        out.append((top + jnp.log(total), pick))
    return out


def dlogits(logits, log_total, target_row):
    hit = hits(logits.shape, target_row)
    return (jnp.exp(logits - log_total) - jnp.where(hit, 1.0, 0.0)).astype(BF16)


def store_contrib(out_ref, q, piece, block):
    slabs, depth, width = out_ref.shape
    half = depth // 2
    product = SCALE * jnp.dot(piece, block, preferred_element_type=F32)
    out_ref[:, q * half : (q + 1) * half, :] = product.astype(BF16).reshape(slabs, half, width)


def far_kernel(queries_ref, others_ref, logits_ref, target_ref, s0, s1, p0, p1, contrib_ref, dlogits_ref, totals_ref):
    totals = log_totals(s0, s1, p0, p1)
    totals_ref[...] = jnp.zeros_like(totals_ref)
    for q, block_ref in enumerate((queries_ref, others_ref)):
        piece = dlogits(logits_ref[q], totals[q][0], target_ref[q : q + 1, :])
        dlogits_ref[q] = piece
        store_contrib(contrib_ref, q, piece, block_ref[...])
        totals_ref[q : q + 1, :] = totals[q][0]
    totals_ref[2:3, :] = totals[0][0] - totals[0][1]


def far_grads(queries, others, logits, target, stats, slabs):
    size = queries.shape[0]
    rows = logits.shape[1]
    return pl.pallas_call(
        far_kernel,
        in_specs=[VMEM] * 8,
        out_specs=[VMEM] * 3,
        out_shape=[
            jax.ShapeDtypeStruct(slabs.shape, BF16),
            jax.ShapeDtypeStruct((2, rows, size), BF16),
            jax.ShapeDtypeStruct((8, size), F32),
        ],
        compiler_params=params(),
        name="far_grads",
        cost_estimate=pl.CostEstimate(flops=1 << 30, bytes_accessed=8 << 20, transcendentals=1 << 19),
    )(queries, others, logits, target, *stats)


def query_product(near, near_ref, far, far_ref, q):
    dims = (((0,), (0,)), ((), ()))
    total = lax.dot_general(near, candidates(near_ref, q), dims, preferred_element_type=F32)
    total += lax.dot_general(far, candidates(far_ref, q), dims, preferred_element_type=F32)
    return SCALE * total


def other_kernel(logits_ref, target_ref, totals_ref, far_ref, near_slabs_ref, far_slabs_ref, other_ref):
    near = dlogits(logits_ref[1], totals_ref[1:2, :], target_ref[1:2, :])
    other_ref[...] = query_product(near, near_slabs_ref, far_ref[1], far_slabs_ref, 1).astype(BF16)


def other_grads(logits, target, totals, far, near_slabs, far_slabs):
    size, width = logits.shape[2], near_slabs.shape[2]
    return pl.pallas_call(
        other_kernel,
        in_specs=[VMEM] * 6,
        out_specs=VMEM,
        out_shape=jax.ShapeDtypeStruct((size, width), BF16),
        compiler_params=params(),
        name="other_grads",
        cost_estimate=pl.CostEstimate(flops=1 << 30, bytes_accessed=8 << 20, transcendentals=1 << 18),
    )(logits, target, totals, far, near_slabs, far_slabs)


def near_kernel(queries_ref, others_ref, logits_ref, target_ref, totals_ref, far_ref, near_slabs_ref, far_slabs_ref, contrib_ref, own_ref):
    for q, block_ref in enumerate((queries_ref, others_ref)):
        piece = dlogits(logits_ref[q], totals_ref[q : q + 1, :], target_ref[q : q + 1, :])
        store_contrib(contrib_ref, q, piece, block_ref[...])
        if q == 0:
            own_ref[...] = query_product(piece, near_slabs_ref, far_ref[0], far_slabs_ref, 0)


def near_grads(queries, others, logits, target, totals, far, near_slabs, far_slabs):
    return pl.pallas_call(
        near_kernel,
        in_specs=[VMEM] * 8,
        out_specs=[VMEM] * 2,
        out_shape=[
            jax.ShapeDtypeStruct(near_slabs.shape, BF16),
            jax.ShapeDtypeStruct(queries.shape, F32),
        ],
        compiler_params=params(),
        name="near_grads",
        cost_estimate=pl.CostEstimate(flops=1 << 31, bytes_accessed=14 << 20, transcendentals=1 << 19),
    )(queries, others, logits, target, totals, far, near_slabs, far_slabs)


def on_device(queries, passages, block_ids, positives):
    height, blocks, width = passages.shape
    refs = block_ids.shape[1]
    groups, planes, ranks = lax.axis_size("group"), lax.axis_size("z"), lax.axis_size("rank")
    slabs = groups * ranks
    z = lax.axis_index("z")
    to_pair = [(i, i ^ 1) for i in range(planes)]
    across = [(i, (i + planes // 2) % planes) for i in range(planes)]

    own_rows = jnp.transpose(passages, (1, 0, 2))
    pair_rows = lax.ppermute(own_rows, "z", to_pair)
    others = lax.ppermute(queries, "z", across)
    others_positives = lax.ppermute(positives, "z", across)

    table = block_ids.reshape(groups, planes, ranks, refs)
    both = jnp.stack([jnp.take(table, z, axis=1), jnp.take(table, (z + planes // 2) % planes, axis=1)], axis=2)
    ids = both.reshape(-1)

    chosen = jnp.stack([positives, others_positives])
    owner = chosen // height
    place = (owner // (planes * ranks) * ranks + owner % ranks) * (refs * height) + chosen % height
    plane = owner // ranks % planes
    near_target = jnp.where(plane == z, place, -1)
    far_target = jnp.where(plane == z ^ 1, place, -1)

    def exchange(slab_array):
        return lax.all_to_all(slab_array, PLANE, split_axis=0, concat_axis=0, tiled=True)

    near_slabs = exchange(gather_rows(ids, own_rows, slabs))
    far_slabs = exchange(gather_rows(ids, pair_rows, slabs))
    near_logits, near_stats = half_logits(queries, others, near_slabs, near_target)
    far_logits, far_stats = half_logits(queries, others, far_slabs, far_target)
    stats = jnp.concatenate([near_stats, far_stats])
    partner = lax.ppermute(stats, "z", across)
    all_stats = (near_stats, far_stats, partner[:8], partner[8:])

    far_contrib, far_pieces, totals = far_grads(queries, others, far_logits, far_target, all_stats, far_slabs)
    far_back = exchange(far_contrib)
    other_part = other_grads(near_logits, near_target, totals, far_pieces, near_slabs, far_slabs)
    own_part = lax.ppermute(other_part, "z", across)
    near_contrib, own_grad = near_grads(
        queries, others, near_logits, near_target, totals, far_pieces, near_slabs, far_slabs
    )
    near_back = exchange(near_contrib)

    pair_sum = lax.ppermute(segment_rows(ids, far_back, blocks), "z", to_pair)
    query_grad = (own_grad + own_part.astype(F32)).astype(BF16)
    row_sum = segment_rows(ids, near_back, blocks, pair_sum)
    return totals[2], query_grad, jnp.transpose(row_sum, (1, 0, 2))


def solution(mesh):
    groups, members = mesh.devices.shape
    split = Mesh(mesh.devices.reshape(groups, PLANES, members // PLANES), ("group", "z", "rank"))
    rows = ("group", "z", "rank")
    return jax.shard_map(
        on_device,
        mesh=split,
        in_specs=(P(rows, None), P(rows, None, None), P(), P(rows)),
        out_specs=(P(rows), P(rows, None), P(rows, None, None)),
        check_vma=False,
    )
```

```python
import functools

import jax
import jax.numpy as jnp
from jax import lax
from jax.experimental import pallas as pl
from jax.experimental.pallas import tpu as pltpu
from jax.sharding import Mesh
from jax.sharding import PartitionSpec as P

SCALE = 0.8
PLANES = 4
CHUNKS = 2
EARLY = 4
BF16 = jnp.bfloat16
F32 = jnp.float32
BUSY = 1 << 37
PLANE = ("group", "rank")
ANY = pl.BlockSpec(memory_space=pl.ANY)
HBM = pl.BlockSpec(memory_space=pltpu.HBM)
VMEM = pl.BlockSpec(memory_space=pltpu.VMEM)
SMEM = pl.BlockSpec(memory_space=pltpu.SMEM)


def params():
    return pltpu.CompilerParams(vmem_limit_bytes=28 << 20)


def cost(flops, mib):
    return pl.CostEstimate(flops=flops, bytes_accessed=mib << 20, transcendentals=0)


def in_hbm(array):
    return pltpu.with_memory_space_constraint(array, pltpu.HBM)


def shape(dims, dtype):
    return jax.ShapeDtypeStruct(dims, dtype)


def after_kernel(*refs):
    del refs


def after(array, *others):
    return pl.pallas_call(
        after_kernel,
        in_specs=[ANY] * (1 + len(others)),
        out_specs=ANY,
        out_shape=shape(array.shape, array.dtype),
        input_output_aliases={0: 0},
        name="after",
    )(array, *others)


def gather_kernel(planes, ranks, ids, rows_ref, out_ref, made, left):
    slabs, depth, width = out_ref.shape
    height = rows_ref.shape[1]
    refs = ids.shape[0]
    z = lax.axis_index("z")

    def sent(slab):
        return pltpu.make_async_copy(made.at[slab], out_ref.at[slab], left.at[slab])

    def fill(slab, carry):
        for pick in range(2 * refs):
            there = (z + pick // refs * (planes // 2)) % planes
            owner = (slab // ranks * planes + there) * ranks + slab % ranks
            made[slab, pick * height : (pick + 1) * height, :] = rows_ref[ids[pick % refs, owner]]
        sent(slab).start()
        return carry

    def drain(slab, carry):
        sent(slab).wait()
        return carry

    lax.fori_loop(0, slabs, fill, 0)
    lax.fori_loop(0, slabs, drain, 0)


def gather_rows(ids, rows, slabs, planes, ranks, flops):
    blocks, height, width = rows.shape
    dims = (slabs, 2 * ids.shape[0] * height, width)
    return pl.pallas_call(
        functools.partial(gather_kernel, planes, ranks),
        in_specs=[SMEM, VMEM],
        out_specs=HBM,
        out_shape=pltpu.HBM(dims, BF16),
        scratch_shapes=[pltpu.VMEM(dims, BF16), pltpu.SemaphoreType.DMA((slabs,))],
        compiler_params=params(),
        name="gather_rows",
        cost_estimate=cost(flops, 4),
    )(ids, rows)


def segment_kernel(stripes, with_start, spread_ref, slabs_ref, *refs):
    start_ref = refs[0] if with_start else None
    out_ref, held, result, begun, arrived, left = refs[-6:]
    slabs, depth, width = slabs_ref.shape
    tile = width // stripes
    columns = [pl.ds(t * tile, tile) for t in range(stripes)]
    loads = [
        pltpu.make_async_copy(slabs_ref.at[:, :, columns[t]], held.at[t], arrived.at[t]) for t in range(stripes)
    ]
    for load in loads:
        load.start()
    if with_start:
        first = pltpu.make_async_copy(start_ref, begun, arrived.at[stripes])
        first.start()
        first.wait()
    stores = []
    for t in range(stripes):
        loads[t].wait()
        total = jnp.dot(spread_ref[...], held[t].reshape(slabs * depth, tile), preferred_element_type=F32)
        if with_start:
            total += begun[:, t * tile : (t + 1) * tile].astype(F32)
        result[t] = total.astype(BF16)
        stores.append(pltpu.make_async_copy(result.at[t], out_ref.at[:, columns[t]], left.at[t]))
        stores[t].start()
    for store in stores:
        store.wait()


def segment_rows(spread, slabs, *start):
    stripes = 4
    rows = spread.shape[0]
    count, depth, width = slabs.shape
    tile = width // stripes
    return pl.pallas_call(
        functools.partial(segment_kernel, stripes, len(start) > 0),
        in_specs=[VMEM, HBM] + [HBM] * len(start),
        out_specs=HBM,
        out_shape=pltpu.HBM((rows, width), BF16),
        scratch_shapes=[
            pltpu.VMEM((stripes, count, depth, tile), BF16),
            pltpu.VMEM((stripes, rows, tile), BF16),
            pltpu.VMEM((rows, width) if start else (16, 128), BF16),
            pltpu.SemaphoreType.DMA((stripes + 1,)),
            pltpu.SemaphoreType.DMA((stripes,)),
        ],
        compiler_params=params(),
        name="segment_rows",
        cost_estimate=cost(1 << 30, 4),
    )(spread, slabs, *start)


def candidates(slabs_ref, q, chunk):
    slabs, depth, width = slabs_ref.shape
    part, half = slabs // CHUNKS, depth // 2
    block = slabs_ref[chunk * part : (chunk + 1) * part, q * half : (q + 1) * half, :]
    return block.reshape(part * half, width)


def hits(rows, chunk, target_row):
    row = lax.broadcasted_iota(jnp.int32, (rows, target_row.shape[1]), 0)
    return row + chunk * rows == target_row


def joined(a, b):
    top = jnp.maximum(a[0], b[0])
    return top, a[1] * jnp.exp(a[0] - top) + b[1] * jnp.exp(b[0] - top), a[2] + b[2]


def stat_rows(ref, q):
    return [ref[4 * q + i : 4 * q + i + 1, :] for i in range(3)]


def chunk_rows(ref, chunk):
    rows = ref.shape[1] // CHUNKS
    return slice(chunk * rows, (chunk + 1) * rows)


def place_of(far, planes, ranks, refs, height, chosen):
    owner = chosen // height
    spot = (owner // (planes * ranks) * ranks + owner % ranks) * (refs * height) + chosen % height
    return jnp.where(owner // ranks % planes == lax.axis_index("z") ^ far, spot, -1)


def load_chunks(source, held, arrived):
    part = source.shape[0] // CHUNKS
    loads = []
    for c in range(CHUNKS):
        rows = pl.ds(c * part, part)
        loads.append(pltpu.make_async_copy(source.at[rows], held.at[rows], arrived.at[c]))
        loads[c].start()
    return loads


def logits_body(place, blocks, slabs_ref, chosen_refs, held, arrived, put, target_ref):
    loads = load_chunks(slabs_ref, held, arrived)
    target_ref[...] = jnp.full(target_ref.shape, -1, jnp.int32)
    for q, ref in enumerate(chosen_refs):
        target_ref[q : q + 1, :] = place(ref[...])
    stats = [None, None]
    for c in range(CHUNKS):
        loads[c].wait()
        for q, block_ref in enumerate(blocks):
            block = lax.dot_general(
                candidates(held, q, c), block_ref[...], (((1,), (1,)), ((), ())), preferred_element_type=F32
            )
            block = SCALE * block
            put(q, c, block)
            top = jnp.max(block, axis=0, keepdims=True)
            total = jnp.sum(jnp.exp(block - top), axis=0, keepdims=True)
            hit = hits(block.shape[0], c, target_ref[q : q + 1, :])
            pick = jnp.sum(jnp.where(hit, block, 0.0), axis=0, keepdims=True)
            here = (top, total, pick)
            stats[q] = here if c == 0 else joined(stats[q], here)
    return stats


def put_stats(stats_ref, stats):
    for q in range(2):
        for i in range(3):
            stats_ref[4 * q + i : 4 * q + i + 1, :] = stats[q][i]
        stats_ref[4 * q + 3 : 4 * q + 4, :] = jnp.zeros_like(stats[q][0])


def near_logits_kernel(
    place, queries_ref, low_ref, high_ref, slabs_ref, chosen_ref, chosen_others_ref,
    logits_ref, stats_ref, target_ref, others_ref, held, made, arrived, left,
):
    cut = low_ref.shape[0]
    others_ref[:cut, :] = low_ref[...]
    others_ref[cut:, :] = high_ref[...]
    stores = []

    def put(q, c, block):
        rows = chunk_rows(logits_ref, c)
        made[q, rows, :] = block
        piece = pl.ds(rows.start, rows.stop - rows.start)
        stores.append(pltpu.make_async_copy(made.at[q, piece], logits_ref.at[q, piece], left.at[q, c]))
        stores[-1].start()

    blocks = (queries_ref, others_ref)
    stats = logits_body(place, blocks, slabs_ref, (chosen_ref, chosen_others_ref), held, arrived, put, target_ref)
    put_stats(stats_ref, stats)
    for store in stores:
        store.wait()


def near_half(queries, low, high, slabs, chosen, chosen_others, place):
    size = queries.shape[0]
    rows = slabs.shape[0] * slabs.shape[1] // 2
    return pl.pallas_call(
        functools.partial(near_logits_kernel, place),
        in_specs=[VMEM, VMEM, VMEM, HBM, VMEM, VMEM],
        out_specs=[HBM, VMEM, VMEM, VMEM],
        out_shape=[
            pltpu.HBM((2, rows, size), F32),
            shape((8, size), F32),
            shape((8, size), jnp.int32),
            shape(queries.shape, BF16),
        ],
        scratch_shapes=[
            pltpu.VMEM(slabs.shape, BF16),
            pltpu.VMEM((2, rows, size), F32),
            pltpu.SemaphoreType.DMA((CHUNKS,)),
            pltpu.SemaphoreType.DMA((2, CHUNKS)),
        ],
        compiler_params=params(),
        name="near_half",
        cost_estimate=cost(BUSY, 4),
    )(queries, low, high, slabs, chosen, chosen_others)


def far_logits_kernel(
    place, queries_ref, others_ref, slabs_ref, chosen_ref, chosen_others_ref, near_stats_ref,
    logits_ref, stats_ref, target_ref, held, arrived,
):
    def put(q, c, block):
        logits_ref[q, chunk_rows(logits_ref, c), :] = block

    blocks = (queries_ref, others_ref)
    stats = logits_body(place, blocks, slabs_ref, (chosen_ref, chosen_others_ref), held, arrived, put, target_ref)
    put_stats(stats_ref, [joined(stat_rows(near_stats_ref, q), stats[q]) for q in range(2)])


def far_half(queries, others, slabs, chosen, chosen_others, near_stats, place):
    size = queries.shape[0]
    rows = slabs.shape[0] * slabs.shape[1] // 2
    return pl.pallas_call(
        functools.partial(far_logits_kernel, place),
        in_specs=[VMEM, VMEM, HBM, VMEM, VMEM, VMEM],
        out_specs=[VMEM] * 3,
        out_shape=[shape((2, rows, size), F32), shape((8, size), F32), shape((8, size), jnp.int32)],
        scratch_shapes=[pltpu.VMEM(slabs.shape, BF16), pltpu.SemaphoreType.DMA((CHUNKS,))],
        compiler_params=params(),
        name="far_half",
        cost_estimate=cost(1 << 30, 4),
    )(queries, others, slabs, chosen, chosen_others, near_stats)


def log_totals(here_ref, there_ref):
    out = []
    for q in range(2):
        top, total, pick = joined(stat_rows(here_ref, q), stat_rows(there_ref, 1 - q))
        out.append((top + jnp.log(total), pick))
    return out


def dlogits(logits, log_total, chunk, target_row):
    hit = hits(logits.shape[0], chunk, target_row)
    return (jnp.exp(logits - log_total) - jnp.where(hit, 1.0, 0.0)).astype(BF16)


def send_contrib(made, out_ref, left, chunk, q, piece, block, complete):
    slabs, depth, width = out_ref.shape
    part, half = slabs // CHUNKS, depth // 2
    product = SCALE * jnp.dot(piece, block, preferred_element_type=F32)
    made[chunk, :, q * half : (q + 1) * half, :] = product.astype(BF16).reshape(part, half, width)
    if not complete:
        return []
    store = pltpu.make_async_copy(made.at[chunk], out_ref.at[pl.ds(chunk * part, part)], left.at[chunk])
    store.start()
    return [store]


def contrib_scratch(slabs):
    return [
        pltpu.VMEM((CHUNKS, slabs.shape[0] // CHUNKS) + slabs.shape[1:], BF16),
        pltpu.SemaphoreType.DMA((CHUNKS,)),
    ]


def far_kernel(
    queries_ref, others_ref, logits_ref, target_ref, here_ref, there_ref,
    contrib_ref, dlogits_ref, totals_ref, loss_ref, made, left,
):
    totals = log_totals(here_ref, there_ref)
    stores = []
    for c in range(CHUNKS):
        rows = chunk_rows(logits_ref, c)
        for q, block_ref in enumerate((queries_ref, others_ref)):
            piece = dlogits(logits_ref[q, rows, :], totals[q][0], c, target_ref[q : q + 1, :])
            dlogits_ref[q, rows, :] = piece
            stores += send_contrib(made, contrib_ref, left, c, q, piece, block_ref[...], q == 1)
    totals_ref[...] = jnp.zeros_like(totals_ref)
    for q in range(2):
        totals_ref[q : q + 1, :] = totals[q][0]
    loss_ref[...] = totals[0][0] - totals[0][1]
    for store in stores:
        store.wait()


def far_grads(queries, others, logits, target, here, there, slabs):
    size = queries.shape[0]
    rows = logits.shape[1]
    return pl.pallas_call(
        far_kernel,
        in_specs=[VMEM] * 6,
        out_specs=[HBM, VMEM, VMEM, VMEM],
        out_shape=[
            pltpu.HBM(slabs.shape, BF16),
            shape((2, rows, size), BF16),
            shape((8, size), F32),
            shape((1, size), F32),
        ],
        scratch_shapes=contrib_scratch(slabs),
        compiler_params=params(),
        name="far_grads",
        cost_estimate=cost(1 << 30, 4),
    )(queries, others, logits, target, here, there)


def rest_kernel(
    queries_ref, others_ref, logits_ref, target_ref, totals_ref, far_ref, near_slabs_ref, far_slabs_ref,
    other_ref, contrib_ref, own_ref,
    near, far, logits, other, own, made, near_in, far_in, logits_in, other_out, own_out, left,
):
    dims = (((0,), (0,)), ((), ()))
    scores = []
    for q in (1, 0):
        scores.append(pltpu.make_async_copy(logits_ref.at[q], logits.at[q], logits_in.at[q]))
        scores[-1].start()
    near_loads = load_chunks(near_slabs_ref, near, near_in)
    far_loads = load_chunks(far_slabs_ref, far, far_in)
    stores = []
    for turn, (q, block_ref) in enumerate(((1, others_ref), (0, queries_ref))):
        scores[turn].wait()
        total = None
        for c in range(CHUNKS):
            rows = chunk_rows(logits, c)
            piece = dlogits(logits[q, rows, :], totals_ref[q : q + 1, :], c, target_ref[q : q + 1, :])
            if turn == 0:
                near_loads[c].wait()
                far_loads[c].wait()
            share = lax.dot_general(piece, candidates(near, q, c), dims, preferred_element_type=F32)
            share += lax.dot_general(far_ref[q, rows, :], candidates(far, q, c), dims, preferred_element_type=F32)
            total = share if c == 0 else total + share
            stores += send_contrib(made, contrib_ref, left, c, q, piece, block_ref[...], q == 0)
        if q == 1:
            other[...] = (SCALE * total).astype(BF16)
            stores.append(pltpu.make_async_copy(other, other_ref, other_out))
        else:
            own[...] = SCALE * total
            stores.append(pltpu.make_async_copy(own, own_ref, own_out))
        stores[-1].start()
    for store in stores:
        store.wait()


def rest_grads(queries, others, logits, target, totals, far_pieces, near_slabs, far_slabs):
    chunk_sems = pltpu.SemaphoreType.DMA((CHUNKS,))
    made, left = contrib_scratch(near_slabs)
    return pl.pallas_call(
        rest_kernel,
        in_specs=[VMEM, VMEM, HBM, VMEM, VMEM, VMEM, HBM, HBM],
        out_specs=[HBM] * 3,
        out_shape=[
            pltpu.HBM(queries.shape, BF16),
            pltpu.HBM(near_slabs.shape, BF16),
            pltpu.HBM(queries.shape, F32),
        ],
        scratch_shapes=[
            pltpu.VMEM(near_slabs.shape, BF16),
            pltpu.VMEM(far_slabs.shape, BF16),
            pltpu.VMEM(logits.shape, F32),
            pltpu.VMEM(queries.shape, BF16),
            pltpu.VMEM(queries.shape, F32),
            made,
            chunk_sems,
            chunk_sems,
            pltpu.SemaphoreType.DMA((2,)),
            pltpu.SemaphoreType.DMA,
            pltpu.SemaphoreType.DMA,
            left,
        ],
        compiler_params=params(),
        name="rest_grads",
        cost_estimate=cost(3 << 30, 8),
    )(queries, others, logits, target, totals, far_pieces, near_slabs, far_slabs)


def add_kernel(own_ref, part_ref, out_ref):
    out_ref[...] = (own_ref[...] + part_ref[...].astype(F32)).astype(BF16)


def add_parts(own, part):
    block = pl.BlockSpec((own.shape[0] // 4, own.shape[1]), lambda i: (i, 0))
    return pl.pallas_call(
        add_kernel,
        grid=(4,),
        in_specs=[block] * 2,
        out_specs=block,
        out_shape=shape(own.shape, BF16),
        compiler_params=params(),
        name="add_parts",
        cost_estimate=cost(BUSY, 4),
    )(own, part)


def on_device(queries, passages, block_ids, positives):
    height, blocks, width = passages.shape
    refs = block_ids.shape[1]
    groups, planes, ranks = lax.axis_size("group"), lax.axis_size("z"), lax.axis_size("rank")
    slabs = groups * ranks
    z = lax.axis_index("z")
    to_pair = [(i, i ^ 1) for i in range(planes)]
    across = [(i, (i + planes // 2) % planes) for i in range(planes)]

    def exchange(slab_array):
        return in_hbm(lax.all_to_all(slab_array, PLANE, split_axis=0, concat_axis=0, tiled=True))

    ids = block_ids.T
    early = queries.shape[0] // EARLY
    own_rows = jnp.transpose(passages, (1, 0, 2))
    near_slabs = exchange(gather_rows(ids, own_rows, slabs, planes, ranks, 0))
    pair_rows = lax.ppermute(own_rows, "z", to_pair)
    others_low = lax.ppermute(queries[:early], "z", across)
    others_high = lax.ppermute(after(queries[early:], pair_rows, others_low), "z", across)
    others_positives = lax.ppermute(positives, "z", across)
    far_slabs = exchange(gather_rows(ids, pair_rows, slabs, planes, ranks, BUSY))

    table = block_ids.reshape(groups, planes, ranks, refs)
    both = jnp.stack([jnp.take(table, z, axis=1), jnp.take(table, (z + planes // 2) % planes, axis=1)], axis=2)
    place = (jnp.arange(height, dtype=jnp.int32) * blocks + both.reshape(-1, 1)).reshape(1, -1)
    spread = (jnp.arange(height * blocks, dtype=jnp.int32)[:, None] == place).astype(BF16)

    chosen = positives.reshape(1, -1)
    chosen_others = others_positives.reshape(1, -1)
    near_logits, near_stats, near_target, others = near_half(
        queries,
        others_low,
        others_high,
        near_slabs,
        chosen,
        chosen_others,
        functools.partial(place_of, 0, planes, ranks, refs, height),
    )
    far_logits, stats, far_target = far_half(
        queries,
        others,
        far_slabs,
        chosen,
        chosen_others,
        near_stats,
        functools.partial(place_of, 1, planes, ranks, refs, height),
    )
    partner = lax.ppermute(stats, "z", across)
    far_contrib, far_pieces, totals, loss = far_grads(
        queries, others, far_logits, far_target, stats, partner, far_slabs
    )
    far_back = exchange(far_contrib)
    other_part, near_contrib, own_grad = rest_grads(
        queries, others, in_hbm(near_logits), near_target, totals, far_pieces, near_slabs, far_slabs
    )
    own_part = lax.ppermute(other_part, "z", across)
    far_sum = segment_rows(spread, far_back)
    pair_sum = lax.ppermute(far_sum, "z", to_pair)
    near_back = exchange(after(near_contrib, far_sum))
    query_grad = add_parts(own_grad, own_part)
    row_sum = segment_rows(spread, near_back, in_hbm(pair_sum), in_hbm(query_grad))
    return loss.reshape(-1), query_grad, row_sum.reshape(passages.shape)


def solution(mesh):
    groups, members = mesh.devices.shape
    split = Mesh(mesh.devices.reshape(groups, PLANES, members // PLANES), ("group", "z", "rank"))
    rows = ("group", "z", "rank")
    return jax.shard_map(
        on_device,
        mesh=split,
        in_specs=(P(rows, None), P(rows, None, None), P(), P(rows)),
        out_specs=(P(rows), P(rows, None), P(rows, None, None)),
        check_vma=False,
    )
```

```python
import functools

import jax
import jax.numpy as jnp
from jax import lax
from jax.experimental import pallas as pl
from jax.experimental.pallas import tpu as pltpu
from jax.sharding import Mesh
from jax.sharding import PartitionSpec as P

SCALE = 0.8
PLANES = 4
CHUNKS = 2
EARLY = 4
BF16 = jnp.bfloat16
F32 = jnp.float32
BUSY = 1 << 37
PLANE = ("group", "rank")
ANY = pl.BlockSpec(memory_space=pl.ANY)
HBM = pl.BlockSpec(memory_space=pltpu.HBM)
VMEM = pl.BlockSpec(memory_space=pltpu.VMEM)
SMEM = pl.BlockSpec(memory_space=pltpu.SMEM)


def params():
    return pltpu.CompilerParams(vmem_limit_bytes=28 << 20)


def cost(flops, mib):
    return pl.CostEstimate(flops=flops, bytes_accessed=mib << 20, transcendentals=0)


def in_hbm(array):
    return pltpu.with_memory_space_constraint(array, pltpu.HBM)


def shape(dims, dtype):
    return jax.ShapeDtypeStruct(dims, dtype)


def after_kernel(*refs):
    del refs


def after(array, *others):
    return pl.pallas_call(
        after_kernel,
        in_specs=[ANY] * (1 + len(others)),
        out_specs=ANY,
        out_shape=shape(array.shape, array.dtype),
        input_output_aliases={0: 0},
        name="after",
    )(array, *others)


def split_kernel(source_ref, low_ref, high_ref, held, done):
    cut = low_ref.shape[0]
    parts = [pl.ds(0, cut), pl.ds(cut, source_ref.shape[0] - cut)]
    for i, part in enumerate(parts):
        pltpu.make_async_copy(source_ref.at[part], held.at[part], done.at[i]).start()
    for i, (part, out_ref) in enumerate(zip(parts, (low_ref, high_ref))):
        pltpu.make_async_copy(source_ref.at[part], held.at[part], done.at[i]).wait()
        pltpu.make_async_copy(held.at[part], out_ref, done.at[i]).start()
    for i, (part, out_ref) in enumerate(zip(parts, (low_ref, high_ref))):
        pltpu.make_async_copy(held.at[part], out_ref, done.at[i]).wait()


def split_rows(array, cut):
    rows, width = array.shape
    return pl.pallas_call(
        split_kernel,
        in_specs=[HBM],
        out_specs=[HBM] * 2,
        out_shape=[pltpu.HBM((cut, width), BF16), pltpu.HBM((rows - cut, width), BF16)],
        scratch_shapes=[pltpu.VMEM(array.shape, BF16), pltpu.SemaphoreType.DMA((2,))],
        compiler_params=params(),
        name="split_rows",
        cost_estimate=cost(0, 2),
    )(array)


def gather_kernel(planes, ranks, ids, rows_ref, out_ref, made, left, *held):
    if held:
        load = pltpu.make_async_copy(rows_ref, *held)
        load.start()
        load.wait()
        rows_ref = held[0]
    slabs, depth, width = out_ref.shape
    height = rows_ref.shape[1]
    refs = ids.shape[0]
    z = lax.axis_index("z")

    def sent(slab):
        return pltpu.make_async_copy(made.at[slab], out_ref.at[slab], left.at[slab])

    def fill(slab, carry):
        for pick in range(2 * refs):
            there = (z + pick // refs * (planes // 2)) % planes
            owner = (slab // ranks * planes + there) * ranks + slab % ranks
            made[slab, pick * height : (pick + 1) * height, :] = rows_ref[ids[pick % refs, owner]]
        sent(slab).start()
        return carry

    def drain(slab, carry):
        sent(slab).wait()
        return carry

    lax.fori_loop(0, slabs, fill, 0)
    lax.fori_loop(0, slabs, drain, 0)


def gather_rows(ids, rows, slabs, planes, ranks, flops, arrived):
    blocks, height, width = rows.shape
    held = [pltpu.VMEM(rows.shape, BF16), pltpu.SemaphoreType.DMA] if arrived else []
    dims = (slabs, 2 * ids.shape[0] * height, width)
    return pl.pallas_call(
        functools.partial(gather_kernel, planes, ranks),
        in_specs=[SMEM, HBM if arrived else VMEM],
        out_specs=HBM,
        out_shape=pltpu.HBM(dims, BF16),
        scratch_shapes=[pltpu.VMEM(dims, BF16), pltpu.SemaphoreType.DMA((slabs,))] + held,
        compiler_params=params(),
        name="gather_rows",
        cost_estimate=cost(flops, 4),
    )(ids, rows)


def segment_kernel(stripes, with_start, spread_ref, slabs_ref, *refs):
    start_ref = refs[0] if with_start else None
    out_ref, held, result, begun, arrived, left = refs[-6:]
    slabs, depth, width = slabs_ref.shape
    tile = width // stripes
    columns = [pl.ds(t * tile, tile) for t in range(stripes)]
    loads = [
        pltpu.make_async_copy(slabs_ref.at[:, :, columns[t]], held.at[t], arrived.at[t]) for t in range(stripes)
    ]
    for load in loads:
        load.start()
    if with_start:
        first = pltpu.make_async_copy(start_ref, begun, arrived.at[stripes])
        first.start()
    stores = []
    for t in range(stripes):
        loads[t].wait()
        total = jnp.dot(spread_ref[...], held[t].reshape(slabs * depth, tile), preferred_element_type=F32)
        if with_start:
            if t == 0:
                first.wait()
            total += begun[:, t * tile : (t + 1) * tile].astype(F32)
        result[t] = total.astype(BF16)
        stores.append(pltpu.make_async_copy(result.at[t], out_ref.at[:, columns[t]], left.at[t]))
        stores[t].start()
    for store in stores:
        store.wait()


def segment_rows(spread, slabs, *start):
    stripes = 2
    rows = spread.shape[0]
    count, depth, width = slabs.shape
    tile = width // stripes
    return pl.pallas_call(
        functools.partial(segment_kernel, stripes, len(start) > 0),
        in_specs=[VMEM, HBM] + [HBM] * len(start),
        out_specs=HBM,
        out_shape=pltpu.HBM((rows, width), BF16),
        scratch_shapes=[
            pltpu.VMEM((stripes, count, depth, tile), BF16),
            pltpu.VMEM((stripes, rows, tile), BF16),
            pltpu.VMEM((rows, width) if start else (16, 128), BF16),
            pltpu.SemaphoreType.DMA((stripes + 1,)),
            pltpu.SemaphoreType.DMA((stripes,)),
        ],
        compiler_params=params(),
        name="segment_rows",
        cost_estimate=cost(1 << 30, 4),
    )(spread, slabs, *start)


def candidates(slabs_ref, q, chunk):
    slabs, depth, width = slabs_ref.shape
    part, half = slabs // CHUNKS, depth // 2
    block = slabs_ref[chunk * part : (chunk + 1) * part, q * half : (q + 1) * half, :]
    return block.reshape(part * half, width)


def hits(rows, chunk, target_row):
    row = lax.broadcasted_iota(jnp.int32, (rows, target_row.shape[1]), 0)
    return row + chunk * rows == target_row


def joined(a, b):
    top = jnp.maximum(a[0], b[0])
    return top, a[1] * jnp.exp(a[0] - top) + b[1] * jnp.exp(b[0] - top), a[2] + b[2]


def stat_rows(ref, q):
    return [ref[4 * q + i : 4 * q + i + 1, :] for i in range(3)]


def chunk_rows(ref, chunk):
    rows = ref.shape[1] // CHUNKS
    return slice(chunk * rows, (chunk + 1) * rows)


def place_of(far, planes, ranks, refs, height, chosen):
    owner = chosen // height
    spot = (owner // (planes * ranks) * ranks + owner % ranks) * (refs * height) + chosen % height
    return jnp.where(owner // ranks % planes == lax.axis_index("z") ^ far, spot, -1)


def load(source, held, arrived):
    copy = pltpu.make_async_copy(source, held, arrived)
    copy.start()
    return copy


def part_of(size, chunk):
    return pl.ds(chunk * (size // CHUNKS), size // CHUNKS)


def load_chunks(source, held, arrived):
    parts = [part_of(source.shape[0], c) for c in range(CHUNKS)]
    return [load(source.at[part], held.at[part], arrived.at[c]) for c, part in enumerate(parts)]


def block_logits(block_ref, slab_part, target_row, put):
    stats = None
    for c in range(CHUNKS):
        block = lax.dot_general(slab_part(c), block_ref[...], (((1,), (1,)), ((), ())), preferred_element_type=F32)
        block = SCALE * block
        put(c, block)
        top = jnp.max(block, axis=0, keepdims=True)
        total = jnp.sum(jnp.exp(block - top), axis=0, keepdims=True)
        hit = hits(block.shape[0], c, target_row)
        pick = jnp.sum(jnp.where(hit, block, 0.0), axis=0, keepdims=True)
        here = (top, total, pick)
        stats = here if c == 0 else joined(stats, here)
    return stats


def put_stats(stats_ref, q, stats):
    for i in range(3):
        stats_ref[4 * q + i : 4 * q + i + 1, :] = stats[i]
    stats_ref[4 * q + 3 : 4 * q + 4, :] = jnp.zeros_like(stats[0])


def put_targets(place, target_ref, chosen_ref, chosen_others_ref):
    target_ref[...] = jnp.full(target_ref.shape, -1, jnp.int32)
    target_ref[0:1, :] = place(chosen_ref[...])
    target_ref[1:2, :] = place(chosen_others_ref[...])


def near_logits_kernel(q, place, *refs):
    *block_refs, slabs_ref, chosen_ref, logits_ref, stats_ref, kept_ref, held, made, arrived, came, left = refs
    half = slabs_ref.shape[1] // 2
    picks = pl.ds(q * half, half)
    parts = [part_of(slabs_ref.shape[0], c) for c in range(CHUNKS)]
    loads = [load(slabs_ref.at[part, picks], held.at[part], arrived.at[c]) for c, part in enumerate(parts)]
    if q == 0:
        load(block_refs[0], kept_ref, came).wait()
    else:
        cut = block_refs[0].shape[0]
        kept_ref[:cut, :] = block_refs[0][...]
        kept_ref[cut:, :] = block_refs[1][...]
    stores = []

    def slab_part(c):
        loads[c].wait()
        slabs = held.shape[0] // CHUNKS
        return held[c * slabs : (c + 1) * slabs].reshape(slabs * half, held.shape[2])

    def put(c, block):
        part = part_of(logits_ref.shape[0], c)
        rows = block.shape[0]
        made[c * rows : (c + 1) * rows, :] = block
        stores.append(load(made.at[part], logits_ref.at[part], left.at[c]))

    stats = block_logits(kept_ref, slab_part, place(chosen_ref[...]), put)
    for i in range(3):
        stats_ref[i : i + 1, :] = stats[i]
    stats_ref[3:, :] = jnp.zeros((stats_ref.shape[0] - 3, stats_ref.shape[1]), F32)
    for store in stores:
        store.wait()


def near_half(q, parts, slabs, chosen, place, hint):
    size, width = sum(part.shape[0] for part in parts), slabs.shape[2]
    rows = slabs.shape[0] * slabs.shape[1] // 2
    return pl.pallas_call(
        functools.partial(near_logits_kernel, q, place),
        in_specs=[HBM if q == 0 else VMEM] * len(parts) + [HBM, VMEM],
        out_specs=[HBM, VMEM, VMEM],
        out_shape=[pltpu.HBM((rows, size), F32), shape((8, size), F32), shape((size, width), BF16)],
        scratch_shapes=[
            pltpu.VMEM((slabs.shape[0], slabs.shape[1] // 2, width), BF16),
            pltpu.VMEM((rows, size), F32),
            pltpu.SemaphoreType.DMA((CHUNKS,)),
            pltpu.SemaphoreType.DMA,
            pltpu.SemaphoreType.DMA((CHUNKS,)),
        ],
        compiler_params=params(),
        name="near_half",
        cost_estimate=cost(hint, 4),
    )(*parts, slabs, chosen)


def far_logits_kernel(
    near_place, far_place, queries_ref, others_ref, slabs_ref, chosen_ref, chosen_others_ref, own_stats_ref, other_stats_ref,
    logits_ref, stats_ref, near_target_ref, far_target_ref, held, arrived,
):
    loads = load_chunks(slabs_ref, held, arrived)
    put_targets(near_place, near_target_ref, chosen_ref, chosen_others_ref)
    put_targets(far_place, far_target_ref, chosen_ref, chosen_others_ref)
    for q, (block_ref, near_ref) in enumerate(((queries_ref, own_stats_ref), (others_ref, other_stats_ref))):

        def slab_part(c, q=q):
            if q == 0:
                loads[c].wait()
            return candidates(held, q, c)

        def put(c, block, q=q):
            logits_ref[q, chunk_rows(logits_ref, c), :] = block

        stats = block_logits(block_ref, slab_part, far_target_ref[q : q + 1, :], put)
        put_stats(stats_ref, q, joined(stat_rows(near_ref, 0), stats))


def far_half(queries, others, slabs, chosen, chosen_others, own_stats, other_stats, places):
    size = queries.shape[0]
    rows = slabs.shape[0] * slabs.shape[1] // 2
    return pl.pallas_call(
        functools.partial(far_logits_kernel, *places),
        in_specs=[VMEM, VMEM, HBM, VMEM, VMEM, VMEM, VMEM],
        out_specs=[VMEM] * 4,
        out_shape=[
            shape((2, rows, size), F32),
            shape((8, size), F32),
            shape((8, size), jnp.int32),
            shape((8, size), jnp.int32),
        ],
        scratch_shapes=[pltpu.VMEM(slabs.shape, BF16), pltpu.SemaphoreType.DMA((CHUNKS,))],
        compiler_params=params(),
        name="far_half",
        cost_estimate=cost(1 << 30, 4),
    )(queries, others, slabs, chosen, chosen_others, own_stats, other_stats)


def log_totals(here_ref, there_ref):
    out = []
    for q in range(2):
        top, total, pick = joined(stat_rows(here_ref, q), stat_rows(there_ref, 1 - q))
        out.append((top + jnp.log(total), pick))
    return out


def dlogits(logits, log_total, chunk, target_row):
    hit = hits(logits.shape[0], chunk, target_row)
    return (jnp.exp(logits - log_total) - jnp.where(hit, 1.0, 0.0)).astype(BF16)


def send_contrib(made, out_ref, left, chunk, q, piece, block, complete):
    slabs, depth, width = out_ref.shape
    part, half = slabs // CHUNKS, depth // 2
    product = SCALE * jnp.dot(piece, block, preferred_element_type=F32)
    made[chunk, :, q * half : (q + 1) * half, :] = product.astype(BF16).reshape(part, half, width)
    if not complete:
        return []
    store = pltpu.make_async_copy(made.at[chunk], out_ref.at[pl.ds(chunk * part, part)], left.at[chunk])
    store.start()
    return [store]


def contrib_scratch(slabs):
    return [
        pltpu.VMEM((CHUNKS, slabs.shape[0] // CHUNKS) + slabs.shape[1:], BF16),
        pltpu.SemaphoreType.DMA((CHUNKS,)),
    ]


def load_share(q, logits_ref, near_ref, far_ref, logits, near, far, came):
    rows, slabs, half = logits_ref.shape[0], near_ref.shape[0], near_ref.shape[1] // 2
    picks = pl.ds(q * half, half)
    copies = []
    for c in range(CHUNKS):
        part, some = part_of(rows, c), part_of(slabs, c)
        copies.append(
            [
                load(far_ref.at[some, picks], far.at[some], came.at[0, c]),
                load(logits_ref.at[part], logits.at[part], came.at[1, c]),
                load(near_ref.at[some, picks], near.at[some], came.at[2, c]),
            ]
        )
    return copies


def query_share(copies, far_piece, near_piece, near, far, use):
    dims = (((0,), (0,)), ((), ()))
    slabs, half, width = near.shape
    total = None
    for c in range(CHUNKS):
        some = slice(c * slabs // CHUNKS, (c + 1) * slabs // CHUNKS)
        rows = slabs // CHUNKS * half
        piece = far_piece(c)
        copies[c][0].wait()
        share = lax.dot_general(piece, far[some].reshape(rows, width), dims, preferred_element_type=F32)
        copies[c][1].wait()
        piece = near_piece(c)
        copies[c][2].wait()
        share += lax.dot_general(piece, near[some].reshape(rows, width), dims, preferred_element_type=F32)
        total = share if c == 0 else total + share
        if use is not None:
            use(c, piece)
    return total


def share_scratch(logits, slabs):
    part = (slabs.shape[0], slabs.shape[1] // 2, slabs.shape[2])
    return [
        pltpu.VMEM(logits.shape, F32),
        pltpu.VMEM(part, BF16),
        pltpu.VMEM(part, BF16),
        pltpu.SemaphoreType.DMA((3, CHUNKS)),
    ]


def row_chunk(rows, chunk):
    return slice(chunk * rows // CHUNKS, (chunk + 1) * rows // CHUNKS)


def other_kernel(
    here_ref, there_ref, near_target_ref, far_target_ref, far_logits_ref, near_logits_ref, near_ref, far_ref,
    other_ref, totals_ref, loss_ref, logits, near, far, came, made, left,
):
    copies = load_share(1, near_logits_ref, near_ref, far_ref, logits, near, far, came)
    totals = log_totals(here_ref, there_ref)
    rows = logits.shape[0]

    def far_piece(c):
        return dlogits(far_logits_ref[1, row_chunk(rows, c), :], totals[1][0], c, far_target_ref[1:2, :])

    def near_piece(c):
        return dlogits(logits[row_chunk(rows, c), :], totals[1][0], c, near_target_ref[1:2, :])

    total = query_share(copies, far_piece, near_piece, near, far, None)
    made[...] = (SCALE * total).astype(BF16)
    store = load(made, other_ref, left)
    totals_ref[...] = jnp.zeros_like(totals_ref)
    for q in range(2):
        totals_ref[q : q + 1, :] = totals[q][0]
    loss_ref[...] = totals[0][0] - totals[0][1]
    store.wait()


def other_grads(here, there, near_target, far_target, far_logits, near_logits, near_slabs, far_slabs):
    size, width = far_logits.shape[2], near_slabs.shape[2]
    return pl.pallas_call(
        other_kernel,
        in_specs=[VMEM] * 5 + [HBM] * 3,
        out_specs=[HBM, VMEM, VMEM],
        out_shape=[pltpu.HBM((size, width), BF16), shape((8, size), F32), shape((1, size), F32)],
        scratch_shapes=share_scratch(near_logits, near_slabs)
        + [pltpu.VMEM((size, width), BF16), pltpu.SemaphoreType.DMA],
        compiler_params=params(),
        name="other_grads",
        cost_estimate=cost(1 << 30, 8),
    )(here, there, near_target, far_target, far_logits, near_logits, near_slabs, far_slabs)


def far_kernel(
    queries_ref, others_ref, logits_ref, target_ref, totals_ref, wait_ref,
    contrib_ref, pieces_ref, made, left, pieces, pieces_out,
):
    del wait_ref
    stores = []
    for c in range(CHUNKS):
        rows = chunk_rows(logits_ref, c)
        for q, block_ref in enumerate((queries_ref, others_ref)):
            piece = dlogits(logits_ref[q, rows, :], totals_ref[q : q + 1, :], c, target_ref[q : q + 1, :])
            if q == 0:
                pieces[rows, :] = piece
                part = part_of(logits_ref.shape[1], c)
                stores.append(load(pieces.at[part], pieces_ref.at[part], pieces_out.at[c]))
            stores += send_contrib(made, contrib_ref, left, c, q, piece, block_ref[...], q == 1)
    for store in stores:
        store.wait()


def far_grads(queries, others, logits, target, totals, wait, slabs):
    size = queries.shape[0]
    rows = logits.shape[1]
    return pl.pallas_call(
        far_kernel,
        in_specs=[VMEM] * 5 + [ANY],
        out_specs=[HBM] * 2,
        out_shape=[pltpu.HBM(slabs.shape, BF16), pltpu.HBM((rows, size), BF16)],
        scratch_shapes=contrib_scratch(slabs)
        + [pltpu.VMEM((rows, size), BF16), pltpu.SemaphoreType.DMA((CHUNKS,))],
        compiler_params=params(),
        name="far_grads",
        cost_estimate=cost(1 << 30, 4),
    )(queries, others, logits, target, totals, wait)


def near_kernel(
    queries_ref, others_ref, target_ref, totals_ref, own_logits_ref, other_logits_ref, pieces_ref, near_ref, far_ref,
    contrib_ref, own_ref, logits, near, far, came, pieces, begun, score, scored, own, own_out, made, left,
):
    first = load(pieces_ref, pieces, begun)
    copies = load_share(0, own_logits_ref, near_ref, far_ref, logits, near, far, came)
    other_scores = load(other_logits_ref, score, scored)
    rows = logits.shape[0]
    first.wait()

    def far_piece(c):
        return pieces[row_chunk(rows, c), :]

    def near_piece(c):
        return dlogits(logits[row_chunk(rows, c), :], totals_ref[0:1, :], c, target_ref[0:1, :])

    def use(c, piece):
        send_contrib(made, contrib_ref, left, c, 0, piece, queries_ref[...], False)

    total = query_share(copies, far_piece, near_piece, near, far, use)
    own[...] = SCALE * total
    stores = [load(own, own_ref, own_out)]
    other_scores.wait()
    for c in range(CHUNKS):
        piece = dlogits(score[row_chunk(rows, c), :], totals_ref[1:2, :], c, target_ref[1:2, :])
        stores += send_contrib(made, contrib_ref, left, c, 1, piece, others_ref[...], True)
    for store in stores:
        store.wait()


def near_grads(queries, others, target, totals, own_logits, other_logits, pieces, near_slabs, far_slabs):
    return pl.pallas_call(
        near_kernel,
        in_specs=[VMEM] * 4 + [HBM] * 5,
        out_specs=[HBM] * 2,
        out_shape=[pltpu.HBM(near_slabs.shape, BF16), pltpu.HBM(queries.shape, F32)],
        scratch_shapes=share_scratch(own_logits, near_slabs)
        + [pltpu.VMEM(pieces.shape, BF16), pltpu.SemaphoreType.DMA]
        + [pltpu.VMEM(own_logits.shape, F32), pltpu.SemaphoreType.DMA]
        + [pltpu.VMEM(queries.shape, F32), pltpu.SemaphoreType.DMA]
        + contrib_scratch(near_slabs),
        compiler_params=params(),
        name="near_grads",
        cost_estimate=cost(BUSY, 8),
    )(queries, others, target, totals, own_logits, other_logits, pieces, near_slabs, far_slabs)


def add_kernel(own_ref, part_ref, out_ref):
    out_ref[...] = (own_ref[...] + part_ref[...].astype(F32)).astype(BF16)


def add_parts(own, part):
    block = pl.BlockSpec((own.shape[0] // 4, own.shape[1]), lambda i: (i, 0))
    return pl.pallas_call(
        add_kernel,
        grid=(4,),
        in_specs=[block] * 2,
        out_specs=block,
        out_shape=shape(own.shape, BF16),
        compiler_params=params(),
        name="add_parts",
        cost_estimate=cost(BUSY, 4),
    )(own, part)


def on_device(queries, passages, block_ids, positives):
    height, blocks, width = passages.shape
    refs = block_ids.shape[1]
    groups, planes, ranks = lax.axis_size("group"), lax.axis_size("z"), lax.axis_size("rank")
    slabs = groups * ranks
    z = lax.axis_index("z")
    to_pair = [(i, i ^ 1) for i in range(planes)]
    across = [(i, (i + planes // 2) % planes) for i in range(planes)]

    def exchange(slab_array):
        return in_hbm(lax.all_to_all(slab_array, PLANE, split_axis=0, concat_axis=0, tiled=True))

    ids = block_ids.T
    early = queries.shape[0] // EARLY
    own_rows = jnp.transpose(passages, (1, 0, 2))
    near_slabs = exchange(gather_rows(ids, own_rows, slabs, planes, ranks, 0, False))
    pair_rows = in_hbm(lax.ppermute(own_rows, "z", to_pair))
    low, high = split_rows(in_hbm(queries), early)
    others_low = lax.ppermute(low, "z", across)
    others_high = lax.ppermute(after(high, pair_rows, others_low), "z", across)
    others_positives = lax.ppermute(positives, "z", across)
    far_slabs = exchange(gather_rows(ids, pair_rows, slabs, planes, ranks, BUSY, True))

    table = block_ids.reshape(groups, planes, ranks, refs)
    both = jnp.stack([jnp.take(table, z, axis=1), jnp.take(table, (z + planes // 2) % planes, axis=1)], axis=2)
    place = (jnp.arange(height, dtype=jnp.int32) * blocks + both.reshape(-1, 1)).reshape(1, -1)
    spread = (jnp.arange(height * blocks, dtype=jnp.int32)[:, None] == place).astype(BF16)

    chosen = positives.reshape(1, -1)
    chosen_others = others_positives.reshape(1, -1)
    places = [functools.partial(place_of, far, planes, ranks, refs, height) for far in range(2)]
    own_logits, own_stats, own = near_half(0, [in_hbm(queries)], near_slabs, chosen, places[0], BUSY)
    other_logits, other_stats, others = near_half(
        1, [others_low, others_high], near_slabs, chosen_others, places[0], BUSY
    )
    far_logits, stats, near_target, far_target = far_half(
        own, others, far_slabs, chosen, chosen_others, own_stats, other_stats, places
    )
    partner = lax.ppermute(stats, "z", across)
    own_logits, other_logits = in_hbm(own_logits), in_hbm(other_logits)
    other_part, totals, loss = other_grads(
        stats, partner, near_target, far_target, far_logits, other_logits, near_slabs, far_slabs
    )
    far_contrib, pieces = far_grads(own, others, far_logits, far_target, totals, other_part, far_slabs)
    far_back = exchange(far_contrib)
    near_contrib, own_grad = near_grads(
        own, others, near_target, totals, own_logits, other_logits, in_hbm(pieces), near_slabs, far_slabs
    )
    own_part = lax.ppermute(other_part, "z", across)
    far_sum = segment_rows(spread, far_back)
    pair_sum = lax.ppermute(far_sum, "z", to_pair)
    near_back = exchange(near_contrib)
    query_grad = add_parts(own_grad, own_part)
    row_sum = segment_rows(spread, near_back, in_hbm(pair_sum), in_hbm(query_grad))
    return loss.reshape(-1), query_grad, row_sum.reshape(passages.shape)


def solution(mesh):
    groups, members = mesh.devices.shape
    split = Mesh(mesh.devices.reshape(groups, PLANES, members // PLANES), ("group", "z", "rank"))
    rows = ("group", "z", "rank")
    return jax.shard_map(
        on_device,
        mesh=split,
        in_specs=(P(rows, None), P(rows, None, None), P(), P(rows)),
        out_specs=(P(rows), P(rows, None), P(rows, None, None)),
        check_vma=False,
    )
```

```python
import functools

import jax
import jax.numpy as jnp
from jax import lax
from jax.experimental import pallas as pl
from jax.experimental.pallas import tpu as pltpu
from jax.sharding import Mesh
from jax.sharding import PartitionSpec as P

SCALE = 0.8
PLANES = 4
CHUNKS = 2
EARLY = 4
BF16 = jnp.bfloat16
F32 = jnp.float32
BUSY = 1 << 37
PLANE = ("group", "rank")
ANY = pl.BlockSpec(memory_space=pl.ANY)
HBM = pl.BlockSpec(memory_space=pltpu.HBM)
VMEM = pl.BlockSpec(memory_space=pltpu.VMEM)
SMEM = pl.BlockSpec(memory_space=pltpu.SMEM)


def params():
    return pltpu.CompilerParams(vmem_limit_bytes=28 << 20)


def cost(flops, mib):
    return pl.CostEstimate(flops=flops, bytes_accessed=mib << 20, transcendentals=0)


def in_hbm(array):
    return pltpu.with_memory_space_constraint(array, pltpu.HBM)


def shape(dims, dtype):
    return jax.ShapeDtypeStruct(dims, dtype)


def after_kernel(*refs):
    del refs


def after(array, *others):
    return pl.pallas_call(
        after_kernel,
        in_specs=[ANY] * (1 + len(others)),
        out_specs=ANY,
        out_shape=shape(array.shape, array.dtype),
        input_output_aliases={0: 0},
        name="after",
    )(array, *others)


def split_kernel(source_ref, low_ref, high_ref, held, done):
    cut = low_ref.shape[0]
    parts = [pl.ds(0, cut), pl.ds(cut, source_ref.shape[0] - cut)]
    for i, part in enumerate(parts):
        pltpu.make_async_copy(source_ref.at[part], held.at[part], done.at[i]).start()
    for i, (part, out_ref) in enumerate(zip(parts, (low_ref, high_ref))):
        pltpu.make_async_copy(source_ref.at[part], held.at[part], done.at[i]).wait()
        pltpu.make_async_copy(held.at[part], out_ref, done.at[i]).start()
    for i, (part, out_ref) in enumerate(zip(parts, (low_ref, high_ref))):
        pltpu.make_async_copy(held.at[part], out_ref, done.at[i]).wait()


def split_rows(array, cut):
    rows, width = array.shape
    return pl.pallas_call(
        split_kernel,
        in_specs=[HBM],
        out_specs=[HBM] * 2,
        out_shape=[pltpu.HBM((cut, width), BF16), pltpu.HBM((rows - cut, width), BF16)],
        scratch_shapes=[pltpu.VMEM(array.shape, BF16), pltpu.SemaphoreType.DMA((2,))],
        compiler_params=params(),
        name="split_rows",
        cost_estimate=cost(0, 2),
    )(array)


def gather_kernel(planes, ranks, ids, rows_ref, out_ref, made, left):
    slabs, depth, width = out_ref.shape
    height = rows_ref.shape[1]
    refs = ids.shape[0]
    z = lax.axis_index("z")

    def sent(slab):
        return pltpu.make_async_copy(made.at[slab], out_ref.at[slab], left.at[slab])

    def fill(slab, carry):
        for pick in range(2 * refs):
            there = (z + pick // refs * (planes // 2)) % planes
            owner = (slab // ranks * planes + there) * ranks + slab % ranks
            made[slab, pick * height : (pick + 1) * height, :] = rows_ref[ids[pick % refs, owner]]
        sent(slab).start()
        return carry

    def drain(slab, carry):
        sent(slab).wait()
        return carry

    lax.fori_loop(0, slabs, fill, 0)
    lax.fori_loop(0, slabs, drain, 0)


def gather_rows(ids, rows, slabs, planes, ranks, flops):
    blocks, height, width = rows.shape
    dims = (slabs, 2 * ids.shape[0] * height, width)
    return pl.pallas_call(
        functools.partial(gather_kernel, planes, ranks),
        in_specs=[SMEM, VMEM],
        out_specs=HBM,
        out_shape=pltpu.HBM(dims, BF16),
        scratch_shapes=[pltpu.VMEM(dims, BF16), pltpu.SemaphoreType.DMA((slabs,))],
        compiler_params=params(),
        name="gather_rows",
        cost_estimate=cost(flops, 4),
    )(ids, rows)


def segment_kernel(stripes, with_start, spread_ref, slabs_ref, *refs):
    out_ref, held, result, begun, arrived, came, left = refs[-7:]
    slabs, depth, width = slabs_ref.shape
    tile = width // stripes
    columns = [pl.ds(t * tile, tile) for t in range(stripes)]
    loads = [load(slabs_ref.at[:, :, columns[t]], held.at[t], arrived.at[t]) for t in range(stripes)]
    if with_start:
        starts = [load(refs[0].at[:, columns[t]], begun.at[t], came.at[t]) for t in range(stripes)]
    stores = []
    for t in range(stripes):
        loads[t].wait()
        total = jnp.dot(spread_ref[...], held[t].reshape(slabs * depth, tile), preferred_element_type=F32)
        if with_start:
            starts[t].wait()
            total += begun[t].astype(F32)
        result[t] = total.astype(BF16)
        stores.append(load(result.at[t], out_ref.at[:, columns[t]], left.at[t]))
    for store in stores:
        store.wait()


def segment_rows(spread, slabs, start=None, wait=None):
    stripes = 2
    rows = spread.shape[0]
    count, depth, width = slabs.shape
    tile = width // stripes
    extra = [array for array in (start, wait) if array is not None]
    sems = pltpu.SemaphoreType.DMA((stripes,))
    return pl.pallas_call(
        functools.partial(segment_kernel, stripes, start is not None),
        in_specs=[VMEM, ANY] + [ANY] * len(extra),
        out_specs=HBM,
        out_shape=pltpu.HBM((rows, width), BF16),
        scratch_shapes=[
            pltpu.VMEM((stripes, count, depth, tile), BF16),
            pltpu.VMEM((stripes, rows, tile), BF16),
            pltpu.VMEM((stripes, rows, tile), BF16),
        ]
        + [sems] * 3,
        compiler_params=params(),
        name="segment_rows",
        cost_estimate=cost(1 << 30, 4),
    )(spread, slabs, *extra)


def candidates(slabs_ref, q, chunk):
    slabs, depth, width = slabs_ref.shape
    part, half = slabs // CHUNKS, depth // 2
    block = slabs_ref[chunk * part : (chunk + 1) * part, q * half : (q + 1) * half, :]
    return block.reshape(part * half, width)


def hits(rows, chunk, target_row):
    row = lax.broadcasted_iota(jnp.int32, (rows, target_row.shape[1]), 0)
    return row + chunk * rows == target_row


def joined(a, b):
    top = jnp.maximum(a[0], b[0])
    return top, a[1] * jnp.exp(a[0] - top) + b[1] * jnp.exp(b[0] - top), a[2] + b[2]


def stat_rows(ref, q):
    return [ref[4 * q + i : 4 * q + i + 1, :] for i in range(3)]


def chunk_rows(ref, chunk):
    rows = ref.shape[1] // CHUNKS
    return slice(chunk * rows, (chunk + 1) * rows)


def place_of(far, planes, ranks, refs, height, chosen):
    owner = chosen // height
    spot = (owner // (planes * ranks) * ranks + owner % ranks) * (refs * height) + chosen % height
    return jnp.where(owner // ranks % planes == lax.axis_index("z") ^ far, spot, -1)


def load(source, held, arrived):
    copy = pltpu.make_async_copy(source, held, arrived)
    copy.start()
    return copy


def part_of(size, chunk):
    return pl.ds(chunk * (size // CHUNKS), size // CHUNKS)


def load_chunks(source, held, arrived):
    parts = [part_of(source.shape[0], c) for c in range(CHUNKS)]
    return [load(source.at[part], held.at[part], arrived.at[c]) for c, part in enumerate(parts)]


def block_logits(block_ref, slab_part, target_row, put):
    stats = None
    for c in range(CHUNKS):
        block = lax.dot_general(slab_part(c), block_ref[...], (((1,), (1,)), ((), ())), preferred_element_type=F32)
        block = SCALE * block
        put(c, block)
        top = jnp.max(block, axis=0, keepdims=True)
        total = jnp.sum(jnp.exp(block - top), axis=0, keepdims=True)
        hit = hits(block.shape[0], c, target_row)
        pick = jnp.sum(jnp.where(hit, block, 0.0), axis=0, keepdims=True)
        here = (top, total, pick)
        stats = here if c == 0 else joined(stats, here)
    return stats


def put_stats(stats_ref, q, stats):
    for i in range(3):
        stats_ref[4 * q + i : 4 * q + i + 1, :] = stats[i]
    stats_ref[4 * q + 3 : 4 * q + 4, :] = jnp.zeros_like(stats[0])


def held_rows(held, chunk):
    slabs = held.shape[0] // CHUNKS
    return held[chunk * slabs : (chunk + 1) * slabs].reshape(slabs * held.shape[1], held.shape[2])


def row_chunk(rows, chunk):
    return slice(chunk * rows // CHUNKS, (chunk + 1) * rows // CHUNKS)


def put_targets(place, target_ref, chosen_ref, chosen_others_ref):
    target_ref[...] = jnp.full(target_ref.shape, -1, jnp.int32)
    target_ref[0:1, :] = place(chosen_ref[...])
    target_ref[1:2, :] = place(chosen_others_ref[...])


def own_kernel(place, queries_ref, slabs_ref, chosen_ref, logits_ref, stats_ref, kept_ref, held, made, arrived, came, left):
    half = slabs_ref.shape[1] // 2
    loads = load_chunks(slabs_ref.at[:, pl.ds(0, half)], held, arrived)
    load(queries_ref, kept_ref, came).wait()
    stores = []

    def slab_part(c):
        loads[c].wait()
        return held_rows(held, c)

    def put(c, block):
        part = part_of(logits_ref.shape[0], c)
        made[row_chunk(made.shape[0], c), :] = block
        stores.append(load(made.at[part], logits_ref.at[part], left.at[c]))

    stats = block_logits(kept_ref, slab_part, place(chosen_ref[...]), put)
    put_stats(stats_ref, 0, stats)
    put_stats(stats_ref, 1, stats)
    for store in stores:
        store.wait()


def own_half(queries, slabs, chosen, place):
    size, width = queries.shape
    rows = slabs.shape[0] * slabs.shape[1] // 2
    return pl.pallas_call(
        functools.partial(own_kernel, place),
        in_specs=[HBM, HBM, VMEM],
        out_specs=[HBM, VMEM, VMEM],
        out_shape=[pltpu.HBM((rows, size), F32), shape((8, size), F32), shape((size, width), BF16)],
        scratch_shapes=[
            pltpu.VMEM((slabs.shape[0], slabs.shape[1] // 2, width), BF16),
            pltpu.VMEM((rows, size), F32),
            pltpu.SemaphoreType.DMA((CHUNKS,)),
            pltpu.SemaphoreType.DMA,
            pltpu.SemaphoreType.DMA((CHUNKS,)),
        ],
        compiler_params=params(),
        name="own_half",
        cost_estimate=cost(BUSY, 4),
    )(queries, slabs, chosen)


def rest_kernel(
    near_place, far_place, queries_ref, low_ref, high_ref, near_ref, far_ref, chosen_ref, chosen_others_ref, own_stats_ref,
    other_logits_ref, saved_ref, far_logits_ref, stats_ref, near_target_ref, far_target_ref, others_ref, near_rows, far_rows,
    held, near_in, far_in, held_in, left, came,
):
    half = near_ref.shape[1] // 2
    cut = low_ref.shape[0]
    size = others_ref.shape[0]
    whole = [
        load(low_ref, others_ref.at[pl.ds(0, cut)], came.at[0]),
        load(high_ref, others_ref.at[pl.ds(cut, size - cut)], came.at[1]),
    ]
    near_loads = load_chunks(near_ref.at[:, pl.ds(half, half)], near_rows, near_in)
    held_loads = load_chunks(far_ref.at[:, pl.ds(0, half)], held, held_in)
    far_loads = load_chunks(far_ref.at[:, pl.ds(half, half)], far_rows, far_in)
    put_targets(near_place, near_target_ref, chosen_ref, chosen_others_ref)
    put_targets(far_place, far_target_ref, chosen_ref, chosen_others_ref)
    stores = []

    def part(loads, rows):
        def get(c):
            loads[c].wait()
            return held_rows(rows, c)

        return get

    def put_near(c, block):
        rows = part_of(other_logits_ref.shape[0], c)
        other_logits_ref[row_chunk(other_logits_ref.shape[0], c), :] = block
        stores.append(load(other_logits_ref.at[rows], saved_ref.at[rows], left.at[c]))

    def put_far(q):
        def put(c, block):
            far_logits_ref[q, chunk_rows(far_logits_ref, c), :] = block

        return put

    for copy in whole:
        copy.wait()
    near = block_logits(others_ref, part(near_loads, near_rows), near_target_ref[1:2, :], put_near)
    own = block_logits(queries_ref, part(held_loads, held), far_target_ref[0:1, :], put_far(0))
    put_stats(stats_ref, 0, joined(stat_rows(own_stats_ref, 0), own))
    far = block_logits(others_ref, part(far_loads, far_rows), far_target_ref[1:2, :], put_far(1))
    put_stats(stats_ref, 1, joined(near, far))
    for store in stores:
        store.wait()


def rest_half(queries, low, high, near_slabs, far_slabs, chosen, chosen_others, own_stats, places):
    size, width = queries.shape
    rows = near_slabs.shape[0] * near_slabs.shape[1] // 2
    part = (near_slabs.shape[0], near_slabs.shape[1] // 2, width)
    chunk_sems = pltpu.SemaphoreType.DMA((CHUNKS,))
    return pl.pallas_call(
        functools.partial(rest_kernel, *places),
        in_specs=[VMEM] + [ANY] * 2 + [HBM] * 2 + [VMEM] * 3,
        out_specs=[VMEM, HBM] + [VMEM] * 7,
        out_shape=[
            shape((rows, size), F32),
            pltpu.HBM((rows, size), F32),
            shape((2, rows, size), F32),
            shape((8, size), F32),
            shape((8, size), jnp.int32),
            shape((8, size), jnp.int32),
            shape((size, width), BF16),
            shape(part, BF16),
            shape(part, BF16),
        ],
        scratch_shapes=[pltpu.VMEM(part, BF16)] + [chunk_sems] * 4 + [pltpu.SemaphoreType.DMA((2,))],
        compiler_params=params(),
        name="rest_half",
        cost_estimate=cost(3 << 29, 8),
    )(queries, low, high, near_slabs, far_slabs, chosen, chosen_others, own_stats)


def log_totals(here_ref, there_ref):
    out = []
    for q in range(2):
        top, total, pick = joined(stat_rows(here_ref, q), stat_rows(there_ref, 1 - q))
        out.append((top + jnp.log(total), pick))
    return out


def dlogits(logits, log_total, chunk, target_row):
    hit = hits(logits.shape[0], chunk, target_row)
    return (jnp.exp(logits - log_total) - jnp.where(hit, 1.0, 0.0)).astype(BF16)


def send_contrib(made, out_ref, left, chunk, q, piece, block, complete):
    slabs, depth, width = out_ref.shape
    part, half = slabs // CHUNKS, depth // 2
    product = SCALE * jnp.dot(piece, block, preferred_element_type=F32)
    made[chunk, :, q * half : (q + 1) * half, :] = product.astype(BF16).reshape(part, half, width)
    if not complete:
        return []
    store = pltpu.make_async_copy(made.at[chunk], out_ref.at[pl.ds(chunk * part, part)], left.at[chunk])
    store.start()
    return [store]


def contrib_scratch(slabs):
    return [
        pltpu.VMEM((CHUNKS, slabs.shape[0] // CHUNKS) + slabs.shape[1:], BF16),
        pltpu.SemaphoreType.DMA((CHUNKS,)),
    ]


def load_share(q, logits_ref, near_ref, far_ref, logits, near, far, came):
    rows, slabs, half = logits_ref.shape[0], near_ref.shape[0], near_ref.shape[1] // 2
    picks = pl.ds(q * half, half)
    copies = []
    for c in range(CHUNKS):
        part, some = part_of(rows, c), part_of(slabs, c)
        copies.append(
            [
                load(far_ref.at[some, picks], far.at[some], came.at[0, c]),
                load(logits_ref.at[part], logits.at[part], came.at[1, c]),
                load(near_ref.at[some, picks], near.at[some], came.at[2, c]),
            ]
        )
    return copies


def query_share(copies, far_piece, near_piece, near, far, use):
    dims = (((0,), (0,)), ((), ()))
    slabs, half, width = near.shape
    total = None
    for c in range(CHUNKS):
        some = slice(c * slabs // CHUNKS, (c + 1) * slabs // CHUNKS)
        rows = slabs // CHUNKS * half
        piece = far_piece(c)
        copies[c][0].wait()
        share = lax.dot_general(piece, far[some].reshape(rows, width), dims, preferred_element_type=F32)
        copies[c][1].wait()
        piece = near_piece(c)
        copies[c][2].wait()
        share += lax.dot_general(piece, near[some].reshape(rows, width), dims, preferred_element_type=F32)
        total = share if c == 0 else total + share
        if use is not None:
            use(c, piece)
    return total


def share_scratch(logits, slabs):
    part = (slabs.shape[0], slabs.shape[1] // 2, slabs.shape[2])
    return [
        pltpu.VMEM(logits.shape, F32),
        pltpu.VMEM(part, BF16),
        pltpu.VMEM(part, BF16),
        pltpu.SemaphoreType.DMA((3, CHUNKS)),
    ]


def early_kernel(stats_ref, near_target_ref, far_target_ref, near_logits_ref, far_logits_ref, near_ref, far_ref, sums_ref, hit_ref):
    dims = (((0,), (0,)), ((), ()))
    top = stats_ref[4:5, :]
    rows = near_logits_ref.shape[0]
    for c in range(CHUNKS):
        part = row_chunk(rows, c)
        for i, (score, target_ref, slab_ref) in enumerate(
            ((near_logits_ref[part, :], near_target_ref, near_ref), (far_logits_ref[1, part, :], far_target_ref, far_ref))
        ):
            block = held_rows(slab_ref, c)
            weight = jnp.exp(score - top).astype(BF16)
            hit = jnp.where(hits(score.shape[0], c, target_ref[1:2, :]), 1.0, 0.0).astype(BF16)
            product = lax.dot_general(weight, block, dims, preferred_element_type=F32)
            picked = lax.dot_general(hit, block, dims, preferred_element_type=F32)
            if c == 0 and i == 0:
                sums_ref[...] = product
                hit_ref[...] = picked
            else:
                sums_ref[...] += product
                hit_ref[...] += picked


def early_grads(stats, near_target, far_target, near_logits, far_logits, near_rows, far_rows):
    size, width = near_logits.shape[1], near_rows.shape[2]
    return pl.pallas_call(
        early_kernel,
        in_specs=[VMEM] * 7,
        out_specs=[VMEM] * 2,
        out_shape=[shape((size, width), F32)] * 2,
        compiler_params=params(),
        name="early_grads",
        cost_estimate=cost(BUSY, 4),
    )(stats, near_target, far_target, near_logits, far_logits, near_rows, far_rows)


def other_kernel(here_ref, there_ref, near_target_ref, far_target_ref, sums_ref, hit_ref, other_ref, totals_ref, loss_ref, made, left):
    totals = log_totals(here_ref, there_ref)
    total = totals[1][0]
    top, _, pick = stat_rows(here_ref, 1)
    held = jnp.maximum(near_target_ref[1:2, :], far_target_ref[1:2, :]) >= 0
    scale = jnp.exp(top - total)
    counted = scale * jnp.exp(jnp.where(held, pick - top, 0.0)).astype(BF16).astype(F32)
    wanted = (jnp.exp(jnp.where(held, pick - total, 0.0)) - 1.0).astype(BF16).astype(F32)
    rows = [scale, jnp.where(held, wanted - counted, 0.0)]
    columns = jnp.transpose(jnp.concatenate(rows + [jnp.zeros_like(scale)] * 6, axis=0))
    stores = []
    for c in range(CHUNKS):
        part = row_chunk(made.shape[0], c)
        share = columns[part, 0:1] * sums_ref[part, :] + columns[part, 1:2] * hit_ref[part, :]
        made[part, :] = (SCALE * share).astype(BF16)
        some = part_of(made.shape[0], c)
        stores.append(load(made.at[some], other_ref.at[some], left.at[c]))
    totals_ref[...] = jnp.zeros_like(totals_ref)
    for q in range(2):
        totals_ref[q : q + 1, :] = totals[q][0]
    loss_ref[...] = totals[0][0] - totals[0][1]
    for store in stores:
        store.wait()


def other_grads(here, there, near_target, far_target, sums, hit):
    size, width = sums.shape
    return pl.pallas_call(
        other_kernel,
        in_specs=[VMEM] * 6,
        out_specs=[HBM, VMEM, VMEM],
        out_shape=[pltpu.HBM((size, width), BF16), shape((8, size), F32), shape((1, size), F32)],
        scratch_shapes=[pltpu.VMEM((size, width), BF16), pltpu.SemaphoreType.DMA((CHUNKS,))],
        compiler_params=params(),
        name="other_grads",
        cost_estimate=cost(1 << 20, 4),
    )(here, there, near_target, far_target, sums, hit)


def far_kernel(
    queries_ref, others_ref, logits_ref, target_ref, totals_ref, wait_ref,
    contrib_ref, pieces_ref, made, left, pieces, pieces_out,
):
    del wait_ref
    stores = []
    for c in range(CHUNKS):
        rows = chunk_rows(logits_ref, c)
        for q, block_ref in enumerate((queries_ref, others_ref)):
            piece = dlogits(logits_ref[q, rows, :], totals_ref[q : q + 1, :], c, target_ref[q : q + 1, :])
            if q == 0:
                pieces[rows, :] = piece
                part = part_of(logits_ref.shape[1], c)
                stores.append(load(pieces.at[part], pieces_ref.at[part], pieces_out.at[c]))
            stores += send_contrib(made, contrib_ref, left, c, q, piece, block_ref[...], q == 1)
    for store in stores:
        store.wait()


def far_grads(queries, others, logits, target, totals, wait, slabs):
    size = queries.shape[0]
    rows = logits.shape[1]
    return pl.pallas_call(
        far_kernel,
        in_specs=[VMEM] * 5 + [ANY],
        out_specs=[HBM] * 2,
        out_shape=[pltpu.HBM(slabs.shape, BF16), pltpu.HBM((rows, size), BF16)],
        scratch_shapes=contrib_scratch(slabs)
        + [pltpu.VMEM((rows, size), BF16), pltpu.SemaphoreType.DMA((CHUNKS,))],
        compiler_params=params(),
        name="far_grads",
        cost_estimate=cost(1 << 30, 4),
    )(queries, others, logits, target, totals, wait)


def near_kernel(
    queries_ref, others_ref, target_ref, totals_ref, own_logits_ref, other_logits_ref, pieces_ref, near_ref, far_ref,
    contrib_ref, own_ref, logits, near, far, came, pieces, begun, score, scored, own, own_out, made, left,
):
    first = load(pieces_ref, pieces, begun)
    copies = load_share(0, own_logits_ref, near_ref, far_ref, logits, near, far, came)
    other_scores = load(other_logits_ref, score, scored)
    rows = logits.shape[0]
    first.wait()

    def far_piece(c):
        return pieces[row_chunk(rows, c), :]

    def near_piece(c):
        return dlogits(logits[row_chunk(rows, c), :], totals_ref[0:1, :], c, target_ref[0:1, :])

    def use(c, piece):
        send_contrib(made, contrib_ref, left, c, 0, piece, queries_ref[...], False)

    total = query_share(copies, far_piece, near_piece, near, far, use)
    own[...] = SCALE * total
    stores = [load(own, own_ref, own_out)]
    other_scores.wait()
    for c in range(CHUNKS):
        piece = dlogits(score[row_chunk(rows, c), :], totals_ref[1:2, :], c, target_ref[1:2, :])
        stores += send_contrib(made, contrib_ref, left, c, 1, piece, others_ref[...], True)
    for store in stores:
        store.wait()


def near_grads(queries, others, target, totals, own_logits, other_logits, pieces, near_slabs, far_slabs):
    return pl.pallas_call(
        near_kernel,
        in_specs=[VMEM] * 4 + [HBM] * 5,
        out_specs=[HBM] * 2,
        out_shape=[pltpu.HBM(near_slabs.shape, BF16), pltpu.HBM(queries.shape, F32)],
        scratch_shapes=share_scratch(own_logits, near_slabs)
        + [pltpu.VMEM(pieces.shape, BF16), pltpu.SemaphoreType.DMA]
        + [pltpu.VMEM(own_logits.shape, F32), pltpu.SemaphoreType.DMA]
        + [pltpu.VMEM(queries.shape, F32), pltpu.SemaphoreType.DMA]
        + contrib_scratch(near_slabs),
        compiler_params=params(),
        name="near_grads",
        cost_estimate=cost(BUSY, 8),
    )(queries, others, target, totals, own_logits, other_logits, pieces, near_slabs, far_slabs)


def add_kernel(own_ref, part_ref, *refs):
    out_ref, own, part, made, own_in, part_in, left = refs[-7:]
    pieces = [part_of(own.shape[0], c) for c in range(CHUNKS)]
    loads = [
        (load(own_ref.at[p], own.at[p], own_in.at[c]), load(part_ref.at[p], part.at[p], part_in.at[c]))
        for c, p in enumerate(pieces)
    ]
    stores = []
    for c, p in enumerate(pieces):
        for copy in loads[c]:
            copy.wait()
        rows = row_chunk(own.shape[0], c)
        made[rows, :] = (own[rows, :] + part[rows, :].astype(F32)).astype(BF16)
        stores.append(load(made.at[p], out_ref.at[p], left.at[c]))
    for store in stores:
        store.wait()


def add_parts(own, part, hint, *waits):
    chunk_sems = pltpu.SemaphoreType.DMA((CHUNKS,))
    return pl.pallas_call(
        add_kernel,
        in_specs=[HBM] * 2 + [ANY] * len(waits),
        out_specs=HBM,
        out_shape=pltpu.HBM(own.shape, BF16),
        scratch_shapes=[pltpu.VMEM(own.shape, F32), pltpu.VMEM(own.shape, BF16), pltpu.VMEM(own.shape, BF16)]
        + [chunk_sems] * 3,
        compiler_params=params(),
        name="add_parts",
        cost_estimate=cost(hint, 4),
    )(in_hbm(own), in_hbm(part), *waits)


def on_device(queries, passages, block_ids, positives):
    height, blocks, width = passages.shape
    refs = block_ids.shape[1]
    groups, planes, ranks = lax.axis_size("group"), lax.axis_size("z"), lax.axis_size("rank")
    slabs = groups * ranks
    z = lax.axis_index("z")
    to_pair = [(i, i ^ 1) for i in range(planes)]
    across = [(i, (i + planes // 2) % planes) for i in range(planes)]

    def exchange(slab_array):
        return lax.all_to_all(slab_array, PLANE, split_axis=0, concat_axis=0, tiled=True)

    ids = block_ids.T
    early = queries.shape[0] // EARLY
    own_rows = jnp.transpose(passages, (1, 0, 2))
    near_slabs = in_hbm(exchange(gather_rows(ids, own_rows, slabs, planes, ranks, 0)))
    pair_rows = lax.ppermute(own_rows, "z", to_pair)
    low, high = split_rows(in_hbm(queries), early)
    others_low = in_hbm(lax.ppermute(low, "z", across))
    others_high = lax.ppermute(after(high, others_low), "z", across)
    others_positives = lax.ppermute(positives, "z", across)
    far_slabs = in_hbm(exchange(gather_rows(ids, pair_rows, slabs, planes, ranks, BUSY)))

    table = block_ids.reshape(groups, planes, ranks, refs)
    both = jnp.stack([jnp.take(table, z, axis=1), jnp.take(table, (z + planes // 2) % planes, axis=1)], axis=2)
    place = (jnp.arange(height, dtype=jnp.int32) * blocks + both.reshape(-1, 1)).reshape(1, -1)
    spread = (jnp.arange(height * blocks, dtype=jnp.int32)[:, None] == place).astype(BF16)

    chosen = positives.reshape(1, -1)
    chosen_others = others_positives.reshape(1, -1)
    places = [functools.partial(place_of, far, planes, ranks, refs, height) for far in range(2)]
    own_logits, own_stats, own = own_half(in_hbm(queries), near_slabs, chosen, places[0])
    other_logits, saved_logits, far_logits, stats, near_target, far_target, others, near_rows, far_rows = rest_half(
        own, others_low, others_high, near_slabs, far_slabs, chosen, chosen_others, own_stats, places
    )
    partner = lax.ppermute(stats, "z", across)
    sums, hit = early_grads(stats, near_target, far_target, other_logits, far_logits, near_rows, far_rows)
    other_part, totals, loss = other_grads(stats, partner, near_target, far_target, sums, hit)
    own_logits, other_logits = in_hbm(own_logits), in_hbm(saved_logits)
    far_contrib, pieces = far_grads(own, others, far_logits, far_target, totals, in_hbm(other_part), far_slabs)
    far_back = in_hbm(exchange(far_contrib))
    near_contrib, own_grad = near_grads(
        own, others, near_target, totals, own_logits, other_logits, in_hbm(pieces), near_slabs, far_slabs
    )
    own_part = lax.ppermute(other_part, "z", across)
    far_sum = segment_rows(spread, far_back)
    pair_sum = lax.ppermute(far_sum, "z", to_pair)
    near_back = exchange(near_contrib)
    query_grad = add_parts(own_grad, own_part, BUSY, in_hbm(far_sum))
    row_sum = segment_rows(spread, near_back, pair_sum, in_hbm(query_grad))
    return loss.reshape(-1), query_grad, row_sum.reshape(passages.shape)


def solution(mesh):
    groups, members = mesh.devices.shape
    split = Mesh(mesh.devices.reshape(groups, PLANES, members // PLANES), ("group", "z", "rank"))
    rows = ("group", "z", "rank")
    return jax.shard_map(
        on_device,
        mesh=split,
        in_specs=(P(rows, None), P(rows, None, None), P(), P(rows)),
        out_specs=(P(rows), P(rows, None), P(rows, None, None)),
        check_vma=False,
    )
```

```python
import functools

import jax
import jax.numpy as jnp
from jax import lax
from jax.experimental import pallas as pl
from jax.experimental.pallas import tpu as pltpu
from jax.sharding import Mesh
from jax.sharding import PartitionSpec as P

SCALE = 0.8
PLANES = 4
CHUNKS = 1
EARLY = 4
BF16 = jnp.bfloat16
F32 = jnp.float32
BUSY = 1 << 37
PLANE = ("group", "rank")
ANY = pl.BlockSpec(memory_space=pl.ANY)
HBM = pl.BlockSpec(memory_space=pltpu.HBM)
VMEM = pl.BlockSpec(memory_space=pltpu.VMEM)
SMEM = pl.BlockSpec(memory_space=pltpu.SMEM)


def params():
    return pltpu.CompilerParams(vmem_limit_bytes=28 << 20)


def cost(flops, mib):
    return pl.CostEstimate(flops=flops, bytes_accessed=mib << 20, transcendentals=0)


def in_hbm(array):
    return pltpu.with_memory_space_constraint(array, pltpu.HBM)


def shape(dims, dtype):
    return jax.ShapeDtypeStruct(dims, dtype)


def after_kernel(*refs):
    del refs


def after(array, *others):
    return pl.pallas_call(
        after_kernel,
        in_specs=[ANY] * (1 + len(others)),
        out_specs=ANY,
        out_shape=shape(array.shape, array.dtype),
        input_output_aliases={0: 0},
        name="after",
    )(array, *others)


def split_kernel(source_ref, low_ref, high_ref, held, done):
    cut = low_ref.shape[0]
    parts = [pl.ds(0, cut), pl.ds(cut, source_ref.shape[0] - cut)]
    for i, part in enumerate(parts):
        pltpu.make_async_copy(source_ref.at[part], held.at[part], done.at[i]).start()
    for i, (part, out_ref) in enumerate(zip(parts, (low_ref, high_ref))):
        pltpu.make_async_copy(source_ref.at[part], held.at[part], done.at[i]).wait()
        pltpu.make_async_copy(held.at[part], out_ref, done.at[i]).start()
    for i, (part, out_ref) in enumerate(zip(parts, (low_ref, high_ref))):
        pltpu.make_async_copy(held.at[part], out_ref, done.at[i]).wait()


def split_rows(array, cut):
    rows, width = array.shape
    return pl.pallas_call(
        split_kernel,
        in_specs=[HBM],
        out_specs=[HBM] * 2,
        out_shape=[pltpu.HBM((cut, width), BF16), pltpu.HBM((rows - cut, width), BF16)],
        scratch_shapes=[pltpu.VMEM(array.shape, BF16), pltpu.SemaphoreType.DMA((2,))],
        compiler_params=params(),
        name="split_rows",
        cost_estimate=cost(0, 2),
    )(array)


def gather_kernel(planes, ranks, ids, rows_ref, out_ref, made, left):
    slabs, depth, width = out_ref.shape
    height = rows_ref.shape[1]
    refs = ids.shape[0]
    z = lax.axis_index("z")

    def sent(slab):
        return pltpu.make_async_copy(made.at[slab], out_ref.at[slab], left.at[slab])

    def fill(slab, carry):
        for pick in range(2 * refs):
            there = (z + pick // refs * (planes // 2)) % planes
            owner = (slab // ranks * planes + there) * ranks + slab % ranks
            made[slab, pick * height : (pick + 1) * height, :] = rows_ref[ids[pick % refs, owner]]
        sent(slab).start()
        return carry

    def drain(slab, carry):
        sent(slab).wait()
        return carry

    lax.fori_loop(0, slabs, fill, 0)
    lax.fori_loop(0, slabs, drain, 0)


def gather_rows(ids, rows, slabs, planes, ranks, flops):
    blocks, height, width = rows.shape
    dims = (slabs, 2 * ids.shape[0] * height, width)
    return pl.pallas_call(
        functools.partial(gather_kernel, planes, ranks),
        in_specs=[SMEM, VMEM],
        out_specs=HBM,
        out_shape=pltpu.HBM(dims, BF16),
        scratch_shapes=[pltpu.VMEM(dims, BF16), pltpu.SemaphoreType.DMA((slabs,))],
        compiler_params=params(),
        name="gather_rows",
        cost_estimate=cost(flops, 4),
    )(ids, rows)


def select_kernel(spread_ref, rows_ref, out_ref, made, left):
    slabs, depth, width = out_ref.shape
    part = slabs // 2
    stores = []
    for c in range(2):
        some = slice(c * part, (c + 1) * part)
        lanes = slice(c * part * depth, (c + 1) * part * depth)
        product = lax.dot_general(
            spread_ref[:, lanes], rows_ref[...], (((0,), (0,)), ((), ())), preferred_element_type=F32
        )
        made[some] = product.astype(BF16).reshape(part, depth, width)
        some = pl.ds(c * part, part)
        stores.append(load(made.at[some], out_ref.at[some], left.at[c]))
    for store in stores:
        store.wait()


def select_rows(spread, rows, slabs):
    dims = (slabs, spread.shape[1] // slabs, rows.shape[1])
    return pl.pallas_call(
        select_kernel,
        in_specs=[VMEM, VMEM],
        out_specs=HBM,
        out_shape=pltpu.HBM(dims, BF16),
        scratch_shapes=[pltpu.VMEM(dims, BF16), pltpu.SemaphoreType.DMA((2,))],
        compiler_params=params(),
        name="select_rows",
        cost_estimate=cost(BUSY, 4),
    )(spread, rows)


def segment_kernel(stripes, spread_ref, slabs_ref, *refs):
    out_ref, held, result, arrived, left = refs[-5:]
    slabs, depth, width = slabs_ref.shape
    tile = width // stripes
    columns = [pl.ds(t * tile, tile) for t in range(stripes)]
    loads = [load(slabs_ref.at[:, :, columns[t]], held.at[t], arrived.at[t]) for t in range(stripes)]
    stores = []
    for t in range(stripes):
        loads[t].wait()
        total = jnp.dot(spread_ref[...], held[t].reshape(slabs * depth, tile), preferred_element_type=F32)
        if out_ref.dtype == F32:
            out_ref[:, t * tile : (t + 1) * tile] = total
        else:
            result[t] = total.astype(BF16)
            stores.append(load(result.at[t], out_ref.at[:, columns[t]], left.at[t]))
    for store in stores:
        store.wait()


def segment_rows(spread, slabs, wait=None):
    stripes = 2
    rows = spread.shape[0]
    count, depth, width = slabs.shape
    tile = width // stripes
    extra = [] if wait is None else [wait]
    sems = pltpu.SemaphoreType.DMA((stripes,))
    return pl.pallas_call(
        functools.partial(segment_kernel, stripes),
        in_specs=[VMEM, ANY] + [ANY] * len(extra),
        out_specs=VMEM if extra else HBM,
        out_shape=shape((rows, width), F32) if extra else pltpu.HBM((rows, width), BF16),
        scratch_shapes=[
            pltpu.VMEM((stripes, count, depth, tile), BF16),
            pltpu.VMEM((stripes, rows, tile), BF16),
            sems,
            sems,
        ],
        compiler_params=params(),
        name="segment_rows",
        cost_estimate=cost(BUSY if extra else 1 << 30, 4),
    )(spread, slabs, *extra)


def candidates(slabs_ref, q, chunk):
    slabs, depth, width = slabs_ref.shape
    part, half = slabs // CHUNKS, depth // 2
    block = slabs_ref[chunk * part : (chunk + 1) * part, q * half : (q + 1) * half, :]
    return block.reshape(part * half, width)


def hits(rows, chunk, target_row):
    row = lax.broadcasted_iota(jnp.int32, (rows, target_row.shape[1]), 0)
    return row + chunk * rows == target_row


def joined(a, b):
    top = jnp.maximum(a[0], b[0])
    return top, a[1] * jnp.exp(a[0] - top) + b[1] * jnp.exp(b[0] - top), a[2] + b[2]


def stat_rows(ref, q):
    return [ref[4 * q + i : 4 * q + i + 1, :] for i in range(3)]


def chunk_rows(ref, chunk):
    rows = ref.shape[1] // CHUNKS
    return slice(chunk * rows, (chunk + 1) * rows)


def place_of(far, planes, ranks, refs, height, chosen):
    owner = chosen // height
    spot = (owner // (planes * ranks) * ranks + owner % ranks) * (refs * height) + chosen % height
    return jnp.where(owner // ranks % planes == lax.axis_index("z") ^ far, spot, -1)


def load(source, held, arrived):
    copy = pltpu.make_async_copy(source, held, arrived)
    copy.start()
    return copy


def part_of(size, chunk):
    return pl.ds(chunk * (size // CHUNKS), size // CHUNKS)


def load_chunks(source, held, arrived):
    parts = [part_of(source.shape[0], c) for c in range(CHUNKS)]
    return [load(source.at[part], held.at[part], arrived.at[c]) for c, part in enumerate(parts)]


def block_logits(block_ref, slab_part, target_row, put):
    stats = None
    for c in range(CHUNKS):
        block = lax.dot_general(slab_part(c), block_ref[...], (((1,), (1,)), ((), ())), preferred_element_type=F32)
        block = SCALE * block
        put(c, block)
        top = jnp.max(block, axis=0, keepdims=True)
        total = jnp.sum(jnp.exp(block - top), axis=0, keepdims=True)
        hit = hits(block.shape[0], c, target_row)
        pick = jnp.sum(jnp.where(hit, block, 0.0), axis=0, keepdims=True)
        here = (top, total, pick)
        stats = here if c == 0 else joined(stats, here)
    return stats


def put_stats(stats_ref, q, stats):
    for i in range(3):
        stats_ref[4 * q + i : 4 * q + i + 1, :] = stats[i]
    stats_ref[4 * q + 3 : 4 * q + 4, :] = jnp.zeros_like(stats[0])


def held_rows(held, chunk):
    slabs = held.shape[0] // CHUNKS
    return held[chunk * slabs : (chunk + 1) * slabs].reshape(slabs * held.shape[1], held.shape[2])


def row_chunk(rows, chunk):
    return slice(chunk * rows // CHUNKS, (chunk + 1) * rows // CHUNKS)


def put_targets(place, target_ref, chosen_ref, chosen_others_ref):
    target_ref[...] = jnp.full(target_ref.shape, -1, jnp.int32)
    target_ref[0:1, :] = place(chosen_ref[...])
    target_ref[1:2, :] = place(chosen_others_ref[...])


def own_kernel(place, queries_ref, slabs_ref, chosen_ref, logits_ref, stats_ref, kept_ref, held, made, arrived, came, left):
    half = slabs_ref.shape[1] // 2
    loads = load_chunks(slabs_ref.at[:, pl.ds(0, half)], held, arrived)
    load(queries_ref, kept_ref, came).wait()
    stores = []

    def slab_part(c):
        loads[c].wait()
        return held_rows(held, c)

    def put(c, block):
        part = part_of(logits_ref.shape[0], c)
        made[row_chunk(made.shape[0], c), :] = block
        stores.append(load(made.at[part], logits_ref.at[part], left.at[c]))

    stats = block_logits(kept_ref, slab_part, place(chosen_ref[...]), put)
    put_stats(stats_ref, 0, stats)
    put_stats(stats_ref, 1, stats)
    for store in stores:
        store.wait()


def own_half(queries, slabs, chosen, place):
    size, width = queries.shape
    rows = slabs.shape[0] * slabs.shape[1] // 2
    return pl.pallas_call(
        functools.partial(own_kernel, place),
        in_specs=[HBM, HBM, VMEM],
        out_specs=[HBM, VMEM, VMEM],
        out_shape=[pltpu.HBM((rows, size), F32), shape((8, size), F32), shape((size, width), BF16)],
        scratch_shapes=[
            pltpu.VMEM((slabs.shape[0], slabs.shape[1] // 2, width), BF16),
            pltpu.VMEM((rows, size), F32),
            pltpu.SemaphoreType.DMA((CHUNKS,)),
            pltpu.SemaphoreType.DMA,
            pltpu.SemaphoreType.DMA((CHUNKS,)),
        ],
        compiler_params=params(),
        name="own_half",
        cost_estimate=cost(BUSY, 4),
    )(queries, slabs, chosen)


def rest_kernel(
    near_place, far_place, queries_ref, low_ref, high_ref, near_ref, far_ref, chosen_ref, chosen_others_ref, own_stats_ref,
    other_logits_ref, saved_ref, far_logits_ref, stats_ref, near_target_ref, far_target_ref, others_ref, near_rows, far_rows,
    held, near_in, far_in, held_in, left, came,
):
    half = near_ref.shape[1] // 2
    cut = low_ref.shape[0]
    size = others_ref.shape[0]
    whole = [
        load(low_ref, others_ref.at[pl.ds(0, cut)], came.at[0]),
        load(high_ref, others_ref.at[pl.ds(cut, size - cut)], came.at[1]),
    ]
    near_loads = load_chunks(near_ref.at[:, pl.ds(half, half)], near_rows, near_in)
    held_loads = load_chunks(far_ref.at[:, pl.ds(0, half)], held, held_in)
    far_loads = load_chunks(far_ref.at[:, pl.ds(half, half)], far_rows, far_in)
    put_targets(near_place, near_target_ref, chosen_ref, chosen_others_ref)
    put_targets(far_place, far_target_ref, chosen_ref, chosen_others_ref)
    stores = []

    def part(loads, rows):
        def get(c):
            loads[c].wait()
            return held_rows(rows, c)

        return get

    def put_near(c, block):
        rows = part_of(other_logits_ref.shape[0], c)
        other_logits_ref[row_chunk(other_logits_ref.shape[0], c), :] = block
        stores.append(load(other_logits_ref.at[rows], saved_ref.at[rows], left.at[c]))

    def put_far(q):
        def put(c, block):
            far_logits_ref[q, chunk_rows(far_logits_ref, c), :] = block

        return put

    for copy in whole:
        copy.wait()
    near = block_logits(others_ref, part(near_loads, near_rows), near_target_ref[1:2, :], put_near)
    own = block_logits(queries_ref, part(held_loads, held), far_target_ref[0:1, :], put_far(0))
    put_stats(stats_ref, 0, joined(stat_rows(own_stats_ref, 0), own))
    far = block_logits(others_ref, part(far_loads, far_rows), far_target_ref[1:2, :], put_far(1))
    put_stats(stats_ref, 1, joined(near, far))
    for store in stores:
        store.wait()


def rest_half(queries, low, high, near_slabs, far_slabs, chosen, chosen_others, own_stats, places):
    size, width = queries.shape
    rows = near_slabs.shape[0] * near_slabs.shape[1] // 2
    part = (near_slabs.shape[0], near_slabs.shape[1] // 2, width)
    chunk_sems = pltpu.SemaphoreType.DMA((CHUNKS,))
    return pl.pallas_call(
        functools.partial(rest_kernel, *places),
        in_specs=[VMEM] + [ANY] * 2 + [HBM] * 2 + [VMEM] * 3,
        out_specs=[VMEM, HBM] + [VMEM] * 7,
        out_shape=[
            shape((rows, size), F32),
            pltpu.HBM((rows, size), F32),
            shape((2, rows, size), F32),
            shape((8, size), F32),
            shape((8, size), jnp.int32),
            shape((8, size), jnp.int32),
            shape((size, width), BF16),
            shape(part, BF16),
            shape(part, BF16),
        ],
        scratch_shapes=[pltpu.VMEM(part, BF16)] + [chunk_sems] * 4 + [pltpu.SemaphoreType.DMA((2,))],
        compiler_params=params(),
        name="rest_half",
        cost_estimate=cost(3 << 29, 8),
    )(queries, low, high, near_slabs, far_slabs, chosen, chosen_others, own_stats)


def log_totals(here_ref, there_ref):
    out = []
    for q in range(2):
        top, total, pick = joined(stat_rows(here_ref, q), stat_rows(there_ref, 1 - q))
        out.append((top + jnp.log(total), pick))
    return out


def dlogits(logits, log_total, chunk, target_row):
    hit = hits(logits.shape[0], chunk, target_row)
    return (jnp.exp(logits - log_total) - jnp.where(hit, 1.0, 0.0)).astype(BF16)


def send_contrib(made, out_ref, left, chunk, q, piece, block, complete):
    slabs, depth, width = out_ref.shape
    part, half = slabs // CHUNKS, depth // 2
    product = SCALE * jnp.dot(piece, block, preferred_element_type=F32)
    made[chunk, :, q * half : (q + 1) * half, :] = product.astype(BF16).reshape(part, half, width)
    if not complete:
        return []
    store = pltpu.make_async_copy(made.at[chunk], out_ref.at[pl.ds(chunk * part, part)], left.at[chunk])
    store.start()
    return [store]


def contrib_scratch(slabs):
    return [
        pltpu.VMEM((CHUNKS, slabs.shape[0] // CHUNKS) + slabs.shape[1:], BF16),
        pltpu.SemaphoreType.DMA((CHUNKS,)),
    ]


def load_share(q, logits_ref, near_ref, far_ref, logits, near, far, came):
    rows, slabs, half = logits_ref.shape[0], near_ref.shape[0], near_ref.shape[1] // 2
    picks = pl.ds(q * half, half)
    copies = []
    for c in range(CHUNKS):
        part, some = part_of(rows, c), part_of(slabs, c)
        copies.append(
            [
                load(far_ref.at[some, picks], far.at[some], came.at[0, c]),
                load(logits_ref.at[part], logits.at[part], came.at[1, c]),
                load(near_ref.at[some, picks], near.at[some], came.at[2, c]),
            ]
        )
    return copies


def query_share(copies, far_piece, near_piece, near, far, use):
    dims = (((0,), (0,)), ((), ()))
    slabs, half, width = near.shape
    total = None
    for c in range(CHUNKS):
        some = slice(c * slabs // CHUNKS, (c + 1) * slabs // CHUNKS)
        rows = slabs // CHUNKS * half
        piece = far_piece(c)
        copies[c][0].wait()
        share = lax.dot_general(piece, far[some].reshape(rows, width), dims, preferred_element_type=F32)
        copies[c][1].wait()
        piece = near_piece(c)
        copies[c][2].wait()
        share += lax.dot_general(piece, near[some].reshape(rows, width), dims, preferred_element_type=F32)
        total = share if c == 0 else total + share
        if use is not None:
            use(c, piece)
    return total


def share_scratch(logits, slabs):
    part = (slabs.shape[0], slabs.shape[1] // 2, slabs.shape[2])
    return [
        pltpu.VMEM(logits.shape, F32),
        pltpu.VMEM(part, BF16),
        pltpu.VMEM(part, BF16),
        pltpu.SemaphoreType.DMA((3, CHUNKS)),
    ]


def early_kernel(stats_ref, near_target_ref, far_target_ref, near_logits_ref, far_logits_ref, near_ref, far_ref, sums_ref, hit_ref):
    dims = (((0,), (0,)), ((), ()))
    top = stats_ref[4:5, :]
    rows = near_logits_ref.shape[0]
    for c in range(CHUNKS):
        part = row_chunk(rows, c)
        for i, (score, target_ref, slab_ref) in enumerate(
            ((near_logits_ref[part, :], near_target_ref, near_ref), (far_logits_ref[1, part, :], far_target_ref, far_ref))
        ):
            block = held_rows(slab_ref, c)
            weight = jnp.exp(score - top).astype(BF16)
            hit = jnp.where(hits(score.shape[0], c, target_ref[1:2, :]), 1.0, 0.0).astype(BF16)
            product = lax.dot_general(weight, block, dims, preferred_element_type=F32)
            picked = lax.dot_general(hit, block, dims, preferred_element_type=F32)
            if c == 0 and i == 0:
                sums_ref[...] = product
                hit_ref[...] = picked
            else:
                sums_ref[...] += product
                hit_ref[...] += picked


def early_grads(stats, near_target, far_target, near_logits, far_logits, near_rows, far_rows):
    size, width = near_logits.shape[1], near_rows.shape[2]
    return pl.pallas_call(
        early_kernel,
        in_specs=[VMEM] * 7,
        out_specs=[VMEM] * 2,
        out_shape=[shape((size, width), F32)] * 2,
        compiler_params=params(),
        name="early_grads",
        cost_estimate=cost(BUSY, 4),
    )(stats, near_target, far_target, near_logits, far_logits, near_rows, far_rows)


def other_kernel(here_ref, there_ref, near_target_ref, far_target_ref, sums_ref, hit_ref, other_ref, totals_ref, loss_ref, made, left):
    totals = log_totals(here_ref, there_ref)
    total = totals[1][0]
    top, _, pick = stat_rows(here_ref, 1)
    held = jnp.maximum(near_target_ref[1:2, :], far_target_ref[1:2, :]) >= 0
    scale = jnp.exp(top - total)
    counted = scale * jnp.exp(jnp.where(held, pick - top, 0.0)).astype(BF16).astype(F32)
    wanted = (jnp.exp(jnp.where(held, pick - total, 0.0)) - 1.0).astype(BF16).astype(F32)
    rows = [scale, jnp.where(held, wanted - counted, 0.0)]
    columns = jnp.transpose(jnp.concatenate(rows + [jnp.zeros_like(scale)] * 6, axis=0))
    stores = []
    for c in range(CHUNKS):
        part = row_chunk(made.shape[0], c)
        share = columns[part, 0:1] * sums_ref[part, :] + columns[part, 1:2] * hit_ref[part, :]
        made[part, :] = (SCALE * share).astype(BF16)
        some = part_of(made.shape[0], c)
        stores.append(load(made.at[some], other_ref.at[some], left.at[c]))
    totals_ref[...] = jnp.zeros_like(totals_ref)
    for q in range(2):
        totals_ref[q : q + 1, :] = totals[q][0]
    loss_ref[...] = totals[0][0] - totals[0][1]
    for store in stores:
        store.wait()


def other_grads(here, there, near_target, far_target, sums, hit):
    size, width = sums.shape
    return pl.pallas_call(
        other_kernel,
        in_specs=[VMEM] * 6,
        out_specs=[HBM, VMEM, VMEM],
        out_shape=[pltpu.HBM((size, width), BF16), shape((8, size), F32), shape((1, size), F32)],
        scratch_shapes=[pltpu.VMEM((size, width), BF16), pltpu.SemaphoreType.DMA((CHUNKS,))],
        compiler_params=params(),
        name="other_grads",
        cost_estimate=cost(1 << 20, 4),
    )(here, there, near_target, far_target, sums, hit)


def far_kernel(
    queries_ref, others_ref, logits_ref, target_ref, totals_ref, wait_ref,
    contrib_ref, pieces_ref, made, left, pieces, pieces_out,
):
    del wait_ref
    stores = []
    for c in range(CHUNKS):
        rows = chunk_rows(logits_ref, c)
        for q, block_ref in enumerate((queries_ref, others_ref)):
            piece = dlogits(logits_ref[q, rows, :], totals_ref[q : q + 1, :], c, target_ref[q : q + 1, :])
            if q == 0:
                pieces[rows, :] = piece
                part = part_of(logits_ref.shape[1], c)
                stores.append(load(pieces.at[part], pieces_ref.at[part], pieces_out.at[c]))
            stores += send_contrib(made, contrib_ref, left, c, q, piece, block_ref[...], q == 1)
    for store in stores:
        store.wait()


def far_grads(queries, others, logits, target, totals, wait, slabs):
    size = queries.shape[0]
    rows = logits.shape[1]
    return pl.pallas_call(
        far_kernel,
        in_specs=[VMEM] * 5 + [ANY],
        out_specs=[HBM] * 2,
        out_shape=[pltpu.HBM(slabs.shape, BF16), pltpu.HBM((rows, size), BF16)],
        scratch_shapes=contrib_scratch(slabs)
        + [pltpu.VMEM((rows, size), BF16), pltpu.SemaphoreType.DMA((CHUNKS,))],
        compiler_params=params(),
        name="far_grads",
        cost_estimate=cost(1 << 30, 4),
    )(queries, others, logits, target, totals, wait)


def near_kernel(
    queries_ref, others_ref, target_ref, totals_ref, own_logits_ref, other_logits_ref, pieces_ref, near_ref, far_ref,
    contrib_ref, own_ref, logits, near, far, came, pieces, begun, score, scored, own, own_out, made, left,
):
    first = load(pieces_ref, pieces, begun)
    copies = load_share(0, own_logits_ref, near_ref, far_ref, logits, near, far, came)
    other_scores = load(other_logits_ref, score, scored)
    rows = logits.shape[0]
    first.wait()

    def far_piece(c):
        return pieces[row_chunk(rows, c), :]

    def near_piece(c):
        return dlogits(logits[row_chunk(rows, c), :], totals_ref[0:1, :], c, target_ref[0:1, :])

    def use(c, piece):
        send_contrib(made, contrib_ref, left, c, 0, piece, queries_ref[...], False)

    total = query_share(copies, far_piece, near_piece, near, far, use)
    own[...] = SCALE * total
    stores = [load(own, own_ref, own_out)]
    other_scores.wait()
    for c in range(CHUNKS):
        piece = dlogits(score[row_chunk(rows, c), :], totals_ref[1:2, :], c, target_ref[1:2, :])
        stores += send_contrib(made, contrib_ref, left, c, 1, piece, others_ref[...], True)
    for store in stores:
        store.wait()


def near_grads(queries, others, target, totals, own_logits, other_logits, pieces, near_slabs, far_slabs):
    return pl.pallas_call(
        near_kernel,
        in_specs=[VMEM] * 4 + [HBM] * 5,
        out_specs=[HBM] * 2,
        out_shape=[pltpu.HBM(near_slabs.shape, BF16), pltpu.HBM(queries.shape, F32)],
        scratch_shapes=share_scratch(own_logits, near_slabs)
        + [pltpu.VMEM(pieces.shape, BF16), pltpu.SemaphoreType.DMA]
        + [pltpu.VMEM(own_logits.shape, F32), pltpu.SemaphoreType.DMA]
        + [pltpu.VMEM(queries.shape, F32), pltpu.SemaphoreType.DMA]
        + contrib_scratch(near_slabs),
        compiler_params=params(),
        name="near_grads",
        cost_estimate=cost(BUSY, 8),
    )(queries, others, target, totals, own_logits, other_logits, pieces, near_slabs, far_slabs)


def add_kernel(own_ref, part_ref, *refs):
    out_ref, own, part, made, own_in, part_in, left = refs[-7:]
    pieces = [pl.ds(i * (part.shape[0] // 4), part.shape[0] // 4) for i in range(4)]
    halves = [load(part_ref.at[p], part.at[p], part_in.at[i]) for i, p in enumerate(pieces)]
    if own.shape == part.shape:
        sums = [load(own_ref.at[p], own.at[p], own_in.at[i]) for i, p in enumerate(pieces)]
        own_ref = own
    stores = []
    for i, p in enumerate(pieces):
        halves[i].wait()
        if own_ref is own:
            sums[i].wait()
        rows = slice(p.start, p.start + p.size)
        made[rows, :] = (own_ref[rows, :] + part[rows, :].astype(F32)).astype(BF16)
        stores.append(load(made.at[p], out_ref.at[p], left.at[i]))
    for store in stores:
        store.wait()


def add_parts(own, part, hint, *waits):
    sems = pltpu.SemaphoreType.DMA((4,))
    return pl.pallas_call(
        add_kernel,
        in_specs=[HBM if waits else VMEM, ANY] + [ANY] * len(waits),
        out_specs=HBM,
        out_shape=pltpu.HBM(own.shape, BF16),
        scratch_shapes=[
            pltpu.VMEM(own.shape if waits else (8, 128), F32),
            pltpu.VMEM(own.shape, BF16),
            pltpu.VMEM(own.shape, BF16),
        ]
        + [sems] * 3,
        compiler_params=params(),
        name="add_parts",
        cost_estimate=cost(hint, 4),
    )(in_hbm(own) if waits else own, part, *waits)


def on_device(queries, passages, block_ids, positives):
    height, blocks, width = passages.shape
    refs = block_ids.shape[1]
    groups, planes, ranks = lax.axis_size("group"), lax.axis_size("z"), lax.axis_size("rank")
    slabs = groups * ranks
    z = lax.axis_index("z")
    to_pair = [(i, i ^ 1) for i in range(planes)]
    across = [(i, (i + planes // 2) % planes) for i in range(planes)]

    def exchange(slab_array):
        return lax.all_to_all(slab_array, PLANE, split_axis=0, concat_axis=0, tiled=True)

    ids = block_ids.T
    early = queries.shape[0] // EARLY
    own_rows = jnp.transpose(passages, (1, 0, 2))
    near_slabs = in_hbm(exchange(gather_rows(ids, own_rows, slabs, planes, ranks, 0)))
    pair_rows = lax.ppermute(passages.reshape(height * blocks, width), "z", to_pair)
    low, high = split_rows(in_hbm(queries), early)
    others_low = in_hbm(lax.ppermute(low, "z", across))
    others_high = lax.ppermute(after(high, others_low), "z", across)
    others_positives = lax.ppermute(positives, "z", across)

    table = block_ids.reshape(groups, planes, ranks, refs)
    both = jnp.stack([jnp.take(table, z, axis=1), jnp.take(table, (z + planes // 2) % planes, axis=1)], axis=2)
    place = (jnp.arange(height, dtype=jnp.int32) * blocks + both.reshape(-1, 1)).reshape(1, -1)
    spread = (jnp.arange(height * blocks, dtype=jnp.int32)[:, None] == place).astype(BF16)
    far_slabs = in_hbm(exchange(select_rows(spread, pair_rows, slabs)))

    chosen = positives.reshape(1, -1)
    chosen_others = others_positives.reshape(1, -1)
    places = [functools.partial(place_of, far, planes, ranks, refs, height) for far in range(2)]
    own_logits, own_stats, own = own_half(in_hbm(queries), near_slabs, chosen, places[0])
    other_logits, saved_logits, far_logits, stats, near_target, far_target, others, near_rows, far_rows = rest_half(
        own, others_low, others_high, near_slabs, far_slabs, chosen, chosen_others, own_stats, places
    )
    partner = lax.ppermute(stats, "z", across)
    sums, hit = early_grads(stats, near_target, far_target, other_logits, far_logits, near_rows, far_rows)
    other_part, totals, loss = other_grads(stats, partner, near_target, far_target, sums, hit)
    own_logits, other_logits = in_hbm(own_logits), in_hbm(saved_logits)
    far_contrib, pieces = far_grads(own, others, far_logits, far_target, totals, in_hbm(other_part), far_slabs)
    far_back = in_hbm(exchange(far_contrib))
    near_contrib, own_grad = near_grads(
        own, others, near_target, totals, own_logits, other_logits, in_hbm(pieces), near_slabs, far_slabs
    )
    own_part = lax.ppermute(other_part, "z", across)
    far_sum = segment_rows(spread, far_back)
    pair_sum = lax.ppermute(far_sum, "z", to_pair)
    near_back = exchange(near_contrib)
    query_grad = add_parts(own_grad, own_part, BUSY, in_hbm(far_sum))
    near_sum = segment_rows(spread, near_back, in_hbm(query_grad))
    row_sum = add_parts(near_sum, pair_sum, 1 << 20)
    return loss.reshape(-1), query_grad, row_sum.reshape(passages.shape)


def solution(mesh):
    groups, members = mesh.devices.shape
    split = Mesh(mesh.devices.reshape(groups, PLANES, members // PLANES), ("group", "z", "rank"))
    rows = ("group", "z", "rank")
    return jax.shard_map(
        on_device,
        mesh=split,
        in_specs=(P(rows, None), P(rows, None, None), P(), P(rows)),
        out_specs=(P(rows), P(rows, None), P(rows, None, None)),
        check_vma=False,
    )
```

```python
import functools

import jax
import jax.numpy as jnp
from jax import lax
from jax.experimental import pallas as pl
from jax.experimental.pallas import tpu as pltpu
from jax.sharding import Mesh
from jax.sharding import PartitionSpec as P

SCALE = 0.8
PLANES = 4
CHUNKS = 1
BF16 = jnp.bfloat16
F32 = jnp.float32
BUSY = 1 << 37
PLANE = ("group", "rank")
ANY = pl.BlockSpec(memory_space=pl.ANY)
HBM = pl.BlockSpec(memory_space=pltpu.HBM)
VMEM = pl.BlockSpec(memory_space=pltpu.VMEM)
SMEM = pl.BlockSpec(memory_space=pltpu.SMEM)


def params():
    return pltpu.CompilerParams(vmem_limit_bytes=28 << 20)


def cost(flops, mib):
    return pl.CostEstimate(flops=flops, bytes_accessed=mib << 20, transcendentals=0)


def in_hbm(array):
    return pltpu.with_memory_space_constraint(array, pltpu.HBM)


def shape(dims, dtype):
    return jax.ShapeDtypeStruct(dims, dtype)


def after_kernel(*refs):
    del refs


def after(array, *others):
    return pl.pallas_call(
        after_kernel,
        in_specs=[ANY] + [VMEM] * len(others),
        out_specs=ANY,
        out_shape=shape(array.shape, array.dtype),
        input_output_aliases={0: 0},
        name="after",
    )(array, *others)


def split_kernel(source_ref, low_ref, high_ref, held, done):
    cut = low_ref.shape[0]
    parts = [pl.ds(0, cut), pl.ds(cut, source_ref.shape[0] - cut)]
    for i, part in enumerate(parts):
        pltpu.make_async_copy(source_ref.at[part], held.at[part], done.at[i]).start()
    for i, (part, out_ref) in enumerate(zip(parts, (low_ref, high_ref))):
        pltpu.make_async_copy(source_ref.at[part], held.at[part], done.at[i]).wait()
        pltpu.make_async_copy(held.at[part], out_ref, done.at[i]).start()
    for i, (part, out_ref) in enumerate(zip(parts, (low_ref, high_ref))):
        pltpu.make_async_copy(held.at[part], out_ref, done.at[i]).wait()


def split_rows(array, cut):
    rows, width = array.shape
    return pl.pallas_call(
        split_kernel,
        in_specs=[HBM],
        out_specs=[HBM] * 2,
        out_shape=[pltpu.HBM((cut, width), BF16), pltpu.HBM((rows - cut, width), BF16)],
        scratch_shapes=[pltpu.VMEM(array.shape, BF16), pltpu.SemaphoreType.DMA((2,))],
        compiler_params=params(),
        name="split_rows",
        cost_estimate=cost(0, 2),
    )(array)


def gather_kernel(planes, ranks, ids, rows_ref, out_ref, made, left):
    slabs, depth, width = out_ref.shape
    height = rows_ref.shape[1]
    refs = ids.shape[0]
    z = lax.axis_index("z")

    def sent(slab):
        return pltpu.make_async_copy(made.at[slab], out_ref.at[slab], left.at[slab])

    def fill(slab, carry):
        for pick in range(2 * refs):
            there = (z + pick // refs * (planes // 2)) % planes
            owner = (slab // ranks * planes + there) * ranks + slab % ranks
            made[slab, pick * height : (pick + 1) * height, :] = rows_ref[ids[pick % refs, owner]]
        sent(slab).start()
        return carry

    def drain(slab, carry):
        sent(slab).wait()
        return carry

    lax.fori_loop(0, slabs, fill, 0)
    lax.fori_loop(0, slabs, drain, 0)


def gather_rows(ids, rows, slabs, planes, ranks, flops):
    blocks, height, width = rows.shape
    dims = (slabs, 2 * ids.shape[0] * height, width)
    return pl.pallas_call(
        functools.partial(gather_kernel, planes, ranks),
        in_specs=[SMEM, VMEM],
        out_specs=HBM,
        out_shape=pltpu.HBM(dims, BF16),
        scratch_shapes=[pltpu.VMEM(dims, BF16), pltpu.SemaphoreType.DMA((slabs,))],
        compiler_params=params(),
        name="gather_rows",
        cost_estimate=cost(flops, 4),
    )(ids, rows)


def select_kernel(spread_ref, rows_ref, out_ref, made, left):
    slabs, depth, width = out_ref.shape
    part = slabs // 2
    stores = []
    for c in range(2):
        some = slice(c * part, (c + 1) * part)
        lanes = slice(c * part * depth, (c + 1) * part * depth)
        product = lax.dot_general(
            spread_ref[:, lanes], rows_ref[...], (((0,), (0,)), ((), ())), preferred_element_type=F32
        )
        made[some] = product.astype(BF16).reshape(part, depth, width)
        some = pl.ds(c * part, part)
        stores.append(load(made.at[some], out_ref.at[some], left.at[c]))
    for store in stores:
        store.wait()


def select_rows(spread, rows, slabs):
    dims = (slabs, spread.shape[1] // slabs, rows.shape[1])
    return pl.pallas_call(
        select_kernel,
        in_specs=[VMEM, VMEM],
        out_specs=HBM,
        out_shape=pltpu.HBM(dims, BF16),
        scratch_shapes=[pltpu.VMEM(dims, BF16), pltpu.SemaphoreType.DMA((2,))],
        compiler_params=params(),
        name="select_rows",
        cost_estimate=cost(BUSY, 4),
    )(spread, rows)


def plane_place(ranks):
    return lax.axis_index("group") * ranks + lax.axis_index("rank")


def join_kernel(kept_ref, *refs):
    chips, depth, _ = kept_ref.shape
    given_refs = refs[:chips]
    *out_refs, held, arrived, left = refs[chips:]
    for g in range(chips):
        load(kept_ref.at[g], held.at[g, pl.ds(0, depth)], arrived.at[g, 0])
        load(given_refs[g], held.at[g, pl.ds(depth, depth)], arrived.at[g, 1])
    for g in range(chips):
        pltpu.make_async_copy(kept_ref.at[g], held.at[g, pl.ds(0, depth)], arrived.at[g, 0]).wait()
        pltpu.make_async_copy(given_refs[g], held.at[g, pl.ds(depth, depth)], arrived.at[g, 1]).wait()
        load(held.at[g], out_refs[g], left.at[g])
    for g in range(chips):
        pltpu.make_async_copy(held.at[g], out_refs[g], left.at[g]).wait()


def join_cores(kept, given):
    chips, depth, width = kept.shape
    return pl.pallas_call(
        join_kernel,
        in_specs=[HBM] + [ANY] * chips,
        out_specs=[HBM] * chips,
        out_shape=[pltpu.HBM((2 * depth, width), BF16)] * chips,
        scratch_shapes=[
            pltpu.VMEM((chips, 2 * depth, width), BF16),
            pltpu.SemaphoreType.DMA((chips, 2)),
            pltpu.SemaphoreType.DMA((chips,)),
        ],
        compiler_params=params(),
        name="join_cores",
        cost_estimate=cost(1 << 20, 4),
    )(kept, *given)


def segment_kernel(stripes, arrays, spread_ref, *refs):
    slab_refs = refs[:arrays]
    out_ref, held, result, arrived, left = refs[-5:]
    tile = out_ref.shape[1] // stripes
    depth = held.shape[1] // arrays
    columns = [pl.ds(t * tile, tile) for t in range(stripes)]
    loads = [
        Several(
            [
                load(ref.at[:, columns[t]], held.at[t, pl.ds(i * depth, depth)], arrived.at[t, i])
                for i, ref in enumerate(slab_refs)
            ]
        )
        for t in range(stripes)
    ]
    stores = []
    for t in range(stripes):
        loads[t].wait()
        total = jnp.dot(spread_ref[...], held[t], preferred_element_type=F32)
        if out_ref.dtype == F32:
            out_ref[:, t * tile : (t + 1) * tile] = total
        else:
            result[t] = total.astype(BF16)
            stores.append(load(result.at[t], out_ref.at[:, columns[t]], left.at[t]))
    for store in stores:
        store.wait()


class Several:
    def __init__(self, copies):
        self.copies = copies

    def wait(self):
        for copy in self.copies:
            copy.wait()


def segment_rows(spread, arrays, wait=None):
    stripes = 2
    rows, depth = spread.shape
    width = arrays[0].shape[-1]
    tile = width // stripes
    extra = [] if wait is None else [wait]
    return pl.pallas_call(
        functools.partial(segment_kernel, stripes, len(arrays)),
        in_specs=[VMEM] + [ANY] * (len(arrays) + len(extra)),
        out_specs=VMEM if extra else HBM,
        out_shape=shape((rows, width), F32) if extra else pltpu.HBM((rows, width), BF16),
        scratch_shapes=[
            pltpu.VMEM((stripes, depth, tile), BF16),
            pltpu.VMEM((stripes, rows, tile), BF16),
            pltpu.SemaphoreType.DMA((stripes, len(arrays))),
            pltpu.SemaphoreType.DMA((stripes,)),
        ],
        compiler_params=params(),
        name="segment_rows",
        cost_estimate=cost(BUSY if extra else 1 << 30, 4),
    )(spread, *arrays, *extra)


def candidates(slabs_ref, q, chunk):
    slabs, depth, width = slabs_ref.shape
    part, half = slabs // CHUNKS, depth // 2
    block = slabs_ref[chunk * part : (chunk + 1) * part, q * half : (q + 1) * half, :]
    return block.reshape(part * half, width)


def hits(rows, chunk, target_row):
    row = lax.broadcasted_iota(jnp.int32, (rows, target_row.shape[1]), 0)
    return row + chunk * rows == target_row


def joined(a, b):
    top = jnp.maximum(a[0], b[0])
    return top, a[1] * jnp.exp(a[0] - top) + b[1] * jnp.exp(b[0] - top), a[2] + b[2]


def stat_rows(ref, q):
    return [ref[4 * q + i : 4 * q + i + 1, :] for i in range(3)]


def chunk_rows(ref, chunk):
    rows = ref.shape[1] // CHUNKS
    return slice(chunk * rows, (chunk + 1) * rows)


def place_of(far, planes, ranks, refs, height, chosen):
    owner = chosen // height
    spot = (owner // (planes * ranks) * ranks + owner % ranks) * (refs * height) + chosen % height
    return jnp.where(owner // ranks % planes == lax.axis_index("z") ^ far, spot, -1)


def load(source, held, arrived):
    copy = pltpu.make_async_copy(source, held, arrived)
    copy.start()
    return copy


def part_of(size, chunk):
    return pl.ds(chunk * (size // CHUNKS), size // CHUNKS)


def load_chunks(source, held, arrived):
    parts = [part_of(source.shape[0], c) for c in range(CHUNKS)]
    return [load(source.at[part], held.at[part], arrived.at[c]) for c, part in enumerate(parts)]


def block_logits(block_ref, slab_part, target_row, put):
    stats = None
    for c in range(CHUNKS):
        block = lax.dot_general(slab_part(c), block_ref[...], (((1,), (1,)), ((), ())), preferred_element_type=F32)
        block = SCALE * block
        put(c, block)
        top = jnp.max(block, axis=0, keepdims=True)
        total = jnp.sum(jnp.exp(block - top), axis=0, keepdims=True)
        hit = hits(block.shape[0], c, target_row)
        pick = jnp.sum(jnp.where(hit, block, 0.0), axis=0, keepdims=True)
        here = (top, total, pick)
        stats = here if c == 0 else joined(stats, here)
    return stats


def put_stats(stats_ref, q, stats):
    for i in range(3):
        stats_ref[4 * q + i : 4 * q + i + 1, :] = stats[i]
    stats_ref[4 * q + 3 : 4 * q + 4, :] = jnp.zeros_like(stats[0])


def held_rows(held, chunk):
    slabs = held.shape[0] // CHUNKS
    return held[chunk * slabs : (chunk + 1) * slabs].reshape(slabs * held.shape[1], held.shape[2])


def row_chunk(rows, chunk):
    return slice(chunk * rows // CHUNKS, (chunk + 1) * rows // CHUNKS)


def put_targets(place, target_ref, chosen_ref, chosen_others_ref):
    target_ref[...] = jnp.full(target_ref.shape, -1, jnp.int32)
    target_ref[0:1, :] = place(chosen_ref[...])
    target_ref[1:2, :] = place(chosen_others_ref[...])


def own_kernel(place, queries_ref, slabs_ref, chosen_ref, logits_ref, stats_ref, kept_ref, held, made, arrived, came, left):
    half = slabs_ref.shape[1] // 2
    loads = load_chunks(slabs_ref.at[:, pl.ds(0, half)], held, arrived)
    load(queries_ref, kept_ref, came).wait()
    stores = []

    def slab_part(c):
        loads[c].wait()
        return held_rows(held, c)

    def put(c, block):
        part = part_of(logits_ref.shape[0], c)
        made[row_chunk(made.shape[0], c), :] = block
        stores.append(load(made.at[part], logits_ref.at[part], left.at[c]))

    stats = block_logits(kept_ref, slab_part, place(chosen_ref[...]), put)
    put_stats(stats_ref, 0, stats)
    put_stats(stats_ref, 1, stats)
    for store in stores:
        store.wait()


def own_half(queries, slabs, chosen, place):
    size, width = queries.shape
    rows = slabs.shape[0] * slabs.shape[1] // 2
    return pl.pallas_call(
        functools.partial(own_kernel, place),
        in_specs=[HBM, HBM, VMEM],
        out_specs=[HBM, VMEM, VMEM],
        out_shape=[pltpu.HBM((rows, size), F32), shape((8, size), F32), shape((size, width), BF16)],
        scratch_shapes=[
            pltpu.VMEM((slabs.shape[0], slabs.shape[1] // 2, width), BF16),
            pltpu.VMEM((rows, size), F32),
            pltpu.SemaphoreType.DMA((CHUNKS,)),
            pltpu.SemaphoreType.DMA,
            pltpu.SemaphoreType.DMA((CHUNKS,)),
        ],
        compiler_params=params(),
        name="own_half",
        cost_estimate=cost(BUSY, 4),
    )(queries, slabs, chosen)


def rest_kernel(
    near_place, far_place, queries_ref, low_ref, high_ref, near_ref, far_ref, chosen_ref, chosen_others_ref, own_stats_ref,
    other_logits_ref, saved_ref, far_logits_ref, stats_ref, near_target_ref, far_target_ref, others_ref, near_rows, far_rows,
    held, near_in, far_in, held_in, left, came,
):
    half = near_ref.shape[1] // 2
    cut = low_ref.shape[0]
    size = others_ref.shape[0]
    held_loads = load_chunks(far_ref.at[:, pl.ds(0, half)], held, held_in)
    whole = [
        load(low_ref, others_ref.at[pl.ds(0, cut)], came.at[0]),
        load(high_ref, others_ref.at[pl.ds(cut, size - cut)], came.at[1]),
    ]
    near_loads = load_chunks(near_ref.at[:, pl.ds(half, half)], near_rows, near_in)
    far_loads = load_chunks(far_ref.at[:, pl.ds(half, half)], far_rows, far_in)
    put_targets(near_place, near_target_ref, chosen_ref, chosen_others_ref)
    put_targets(far_place, far_target_ref, chosen_ref, chosen_others_ref)
    stores = []

    def part(loads, rows):
        def get(c):
            loads[c].wait()
            return held_rows(rows, c)

        return get

    def put_near(c, block):
        rows = part_of(other_logits_ref.shape[0], c)
        other_logits_ref[row_chunk(other_logits_ref.shape[0], c), :] = block
        stores.append(load(other_logits_ref.at[rows], saved_ref.at[rows], left.at[c]))

    def put_far(q):
        def put(c, block):
            far_logits_ref[q, chunk_rows(far_logits_ref, c), :] = block

        return put

    own = block_logits(queries_ref, part(held_loads, held), far_target_ref[0:1, :], put_far(0))
    put_stats(stats_ref, 0, joined(stat_rows(own_stats_ref, 0), own))
    for copy in whole:
        copy.wait()
    near = block_logits(others_ref, part(near_loads, near_rows), near_target_ref[1:2, :], put_near)
    far = block_logits(others_ref, part(far_loads, far_rows), far_target_ref[1:2, :], put_far(1))
    put_stats(stats_ref, 1, joined(near, far))
    for store in stores:
        store.wait()


def rest_half(queries, low, high, near_slabs, far_slabs, chosen, chosen_others, own_stats, places):
    size, width = queries.shape
    rows = near_slabs.shape[0] * near_slabs.shape[1] // 2
    part = (near_slabs.shape[0], near_slabs.shape[1] // 2, width)
    chunk_sems = pltpu.SemaphoreType.DMA((CHUNKS,))
    return pl.pallas_call(
        functools.partial(rest_kernel, *places),
        in_specs=[VMEM] + [ANY] * 2 + [HBM] * 2 + [VMEM] * 3,
        out_specs=[VMEM, HBM] + [VMEM] * 7,
        out_shape=[
            shape((rows, size), F32),
            pltpu.HBM((rows, size), F32),
            shape((2, rows, size), F32),
            shape((8, size), F32),
            shape((8, size), jnp.int32),
            shape((8, size), jnp.int32),
            shape((size, width), BF16),
            shape(part, BF16),
            shape(part, BF16),
        ],
        scratch_shapes=[pltpu.VMEM(part, BF16)] + [chunk_sems] * 4 + [pltpu.SemaphoreType.DMA((2,))],
        compiler_params=params(),
        name="rest_half",
        cost_estimate=cost(3 << 29, 8),
    )(queries, low, high, near_slabs, far_slabs, chosen, chosen_others, own_stats)


def log_totals(here_ref, there_ref):
    out = []
    for q in range(2):
        top, total, pick = joined(stat_rows(here_ref, q), stat_rows(there_ref, 1 - q))
        out.append((top + jnp.log(total), pick))
    return out


def dlogits(logits, log_total, chunk, target_row):
    hit = hits(logits.shape[0], chunk, target_row)
    return (jnp.exp(logits - log_total) - jnp.where(hit, 1.0, 0.0)).astype(BF16)


def send_contrib(made, out_ref, left, chunk, q, piece, block, complete):
    slabs, depth, width = out_ref.shape
    part, half = slabs // CHUNKS, depth // 2
    product = SCALE * jnp.dot(piece, block, preferred_element_type=F32)
    made[chunk, :, q * half : (q + 1) * half, :] = product.astype(BF16).reshape(part, half, width)
    if not complete:
        return []
    store = pltpu.make_async_copy(made.at[chunk], out_ref.at[pl.ds(chunk * part, part)], left.at[chunk])
    store.start()
    return [store]


def contrib_scratch(slabs):
    return [
        pltpu.VMEM((CHUNKS, slabs.shape[0] // CHUNKS) + slabs.shape[1:], BF16),
        pltpu.SemaphoreType.DMA((CHUNKS,)),
    ]


def load_share(q, logits_ref, near_ref, far_ref, logits, near, far, came):
    rows, slabs, half = logits_ref.shape[0], near_ref.shape[0], near_ref.shape[1] // 2
    picks = pl.ds(q * half, half)
    copies = []
    for c in range(CHUNKS):
        part, some = part_of(rows, c), part_of(slabs, c)
        copies.append(
            [
                load(far_ref.at[some, picks], far.at[some], came.at[0, c]),
                load(logits_ref.at[part], logits.at[part], came.at[1, c]),
                load(near_ref.at[some, picks], near.at[some], came.at[2, c]),
            ]
        )
    return copies


def query_share(copies, far_piece, near_piece, near, far, use):
    dims = (((0,), (0,)), ((), ()))
    slabs, half, width = near.shape
    total = None
    for c in range(CHUNKS):
        some = slice(c * slabs // CHUNKS, (c + 1) * slabs // CHUNKS)
        rows = slabs // CHUNKS * half
        piece = far_piece(c)
        copies[c][0].wait()
        share = lax.dot_general(piece, far[some].reshape(rows, width), dims, preferred_element_type=F32)
        copies[c][1].wait()
        piece = near_piece(c)
        copies[c][2].wait()
        share += lax.dot_general(piece, near[some].reshape(rows, width), dims, preferred_element_type=F32)
        total = share if c == 0 else total + share
        if use is not None:
            use(c, piece)
    return total


def share_scratch(logits, slabs):
    part = (slabs.shape[0], slabs.shape[1] // 2, slabs.shape[2])
    return [
        pltpu.VMEM(logits.shape, F32),
        pltpu.VMEM(part, BF16),
        pltpu.VMEM(part, BF16),
        pltpu.SemaphoreType.DMA((3, CHUNKS)),
    ]


def early_kernel(stats_ref, near_target_ref, far_target_ref, near_logits_ref, far_logits_ref, near_ref, far_ref, sums_ref, hit_ref):
    dims = (((0,), (0,)), ((), ()))
    top = stats_ref[4:5, :]
    rows = near_logits_ref.shape[0]
    for c in range(CHUNKS):
        part = row_chunk(rows, c)
        for i, (score, target_ref, slab_ref) in enumerate(
            ((near_logits_ref[part, :], near_target_ref, near_ref), (far_logits_ref[1, part, :], far_target_ref, far_ref))
        ):
            block = held_rows(slab_ref, c)
            weight = jnp.exp(score - top).astype(BF16)
            hit = jnp.where(hits(score.shape[0], c, target_ref[1:2, :]), 1.0, 0.0).astype(BF16)
            product = lax.dot_general(weight, block, dims, preferred_element_type=F32)
            picked = lax.dot_general(hit, block, dims, preferred_element_type=F32)
            if c == 0 and i == 0:
                sums_ref[...] = product
                hit_ref[...] = picked
            else:
                sums_ref[...] += product
                hit_ref[...] += picked


def early_grads(stats, near_target, far_target, near_logits, far_logits, near_rows, far_rows):
    size, width = near_logits.shape[1], near_rows.shape[2]
    return pl.pallas_call(
        early_kernel,
        in_specs=[VMEM] * 7,
        out_specs=[VMEM] * 2,
        out_shape=[shape((size, width), F32)] * 2,
        compiler_params=params(),
        name="early_grads",
        cost_estimate=cost(BUSY, 4),
    )(stats, near_target, far_target, near_logits, far_logits, near_rows, far_rows)


def other_kernel(here_ref, there_ref, near_target_ref, far_target_ref, sums_ref, hit_ref, other_ref, totals_ref, loss_ref, made, left):
    totals = log_totals(here_ref, there_ref)
    total = totals[1][0]
    top, _, pick = stat_rows(here_ref, 1)
    held = jnp.maximum(near_target_ref[1:2, :], far_target_ref[1:2, :]) >= 0
    scale = jnp.exp(top - total)
    counted = scale * jnp.exp(jnp.where(held, pick - top, 0.0)).astype(BF16).astype(F32)
    wanted = (jnp.exp(jnp.where(held, pick - total, 0.0)) - 1.0).astype(BF16).astype(F32)
    rows = [scale, jnp.where(held, wanted - counted, 0.0)]
    columns = jnp.transpose(jnp.concatenate(rows + [jnp.zeros_like(scale)] * 6, axis=0))
    stores = []
    size = made.shape[0] // 4
    for c in range(4):
        part = slice(c * size, (c + 1) * size)
        share = columns[part, 0:1] * sums_ref[part, :] + columns[part, 1:2] * hit_ref[part, :]
        made[part, :] = (SCALE * share).astype(BF16)
        some = pl.ds(c * size, size)
        stores.append(load(made.at[some], other_ref.at[some], left.at[c]))
    totals_ref[...] = jnp.zeros_like(totals_ref)
    for q in range(2):
        totals_ref[q : q + 1, :] = totals[q][0]
    loss_ref[...] = totals[0][0] - totals[0][1]
    for store in stores:
        store.wait()


def other_grads(here, there, near_target, far_target, sums, hit):
    size, width = sums.shape
    return pl.pallas_call(
        other_kernel,
        in_specs=[VMEM] * 6,
        out_specs=[HBM, VMEM, VMEM],
        out_shape=[pltpu.HBM((size, width), BF16), shape((8, size), F32), shape((1, size), F32)],
        scratch_shapes=[pltpu.VMEM((size, width), BF16), pltpu.SemaphoreType.DMA((4,))],
        compiler_params=params(),
        name="other_grads",
        cost_estimate=cost(1 << 20, 4),
    )(here, there, near_target, far_target, sums, hit)


def far_kernel(
    queries_ref, others_ref, logits_ref, target_ref, totals_ref, wait_ref,
    contrib_ref, pieces_ref, made, left, pieces, pieces_out,
):
    del wait_ref
    slabs, depth, width = contrib_ref.shape
    half = depth // 2
    stores = []
    for q, block_ref in enumerate((queries_ref, others_ref)):
        piece = dlogits(logits_ref[q], totals_ref[q : q + 1, :], 0, target_ref[q : q + 1, :])
        if q == 0:
            pieces[...] = piece
            stores.append(load(pieces, pieces_ref, pieces_out))
        product = SCALE * jnp.dot(piece, block_ref[...], preferred_element_type=F32)
        made[q] = product.astype(BF16).reshape(slabs, half, width)
        stores.append(load(made.at[q], contrib_ref.at[:, pl.ds(q * half, half)], left.at[q]))
    for store in stores:
        store.wait()


def far_grads(queries, others, logits, target, totals, wait, slabs):
    size = queries.shape[0]
    rows = logits.shape[1]
    count, depth, width = slabs.shape
    return pl.pallas_call(
        far_kernel,
        in_specs=[VMEM] * 5 + [ANY],
        out_specs=[HBM] * 2,
        out_shape=[pltpu.HBM(slabs.shape, BF16), pltpu.HBM((rows, size), BF16)],
        scratch_shapes=[
            pltpu.VMEM((2, count, depth // 2, width), BF16),
            pltpu.SemaphoreType.DMA((2,)),
            pltpu.VMEM((rows, size), BF16),
            pltpu.SemaphoreType.DMA,
        ],
        compiler_params=params(),
        name="far_grads",
        cost_estimate=cost(1 << 30, 4),
    )(queries, others, logits, target, totals, wait)


def near_kernel(
    ranks, queries_ref, others_ref, target_ref, totals_ref, own_logits_ref, other_logits_ref, pieces_ref, near_ref, far_ref,
    kept_ref, *refs,
):
    *given_refs, own_ref, logits, near, far, came, pieces, begun, score, scored, own, own_out, made, left = refs
    first = load(pieces_ref, pieces, begun)
    copies = load_share(0, own_logits_ref, near_ref, far_ref, logits, near, far, came)
    other_scores = load(other_logits_ref, score, scored)
    slabs, depth, width = made.shape
    half = depth // 2

    def store_part(q, piece, block_ref):
        product = SCALE * jnp.dot(piece, block_ref[...], preferred_element_type=F32)
        made[:, q * half : (q + 1) * half, :] = product.astype(BF16).reshape(slabs, half, width)

    other_scores.wait()
    store_part(1, dlogits(score[...], totals_ref[1:2, :], 0, target_ref[1:2, :]), others_ref)
    first.wait()

    def far_piece(c):
        return pieces[row_chunk(logits.shape[0], c), :]

    def near_piece(c):
        return dlogits(logits[row_chunk(logits.shape[0], c), :], totals_ref[0:1, :], c, target_ref[0:1, :])

    def use(c, piece):
        store_part(0, piece, queries_ref)

    total = query_share(copies, far_piece, near_piece, near, far, use)
    place = plane_place(ranks)
    stores = []
    for s in range(slabs):
        out_ref = given_refs[s // 2] if s % 2 else kept_ref.at[s // 2]
        stores.append(load(made.at[place ^ s], out_ref, left.at[s]))
    own[...] = SCALE * total
    stores.append(load(own, own_ref, own_out))
    for store in stores:
        store.wait()


def near_grads(queries, others, target, totals, own_logits, other_logits, pieces, near_slabs, far_slabs, ranks):
    slabs, depth, width = near_slabs.shape
    kept = pltpu.HBM((slabs // 2, depth, width), BF16)
    given = [pltpu.HBM((depth, width), BF16)] * (slabs // 2)
    return pl.pallas_call(
        functools.partial(near_kernel, ranks),
        in_specs=[VMEM] * 4 + [HBM] * 5,
        out_specs=[HBM] * (2 + slabs // 2),
        out_shape=[kept, *given, pltpu.HBM(queries.shape, F32)],
        scratch_shapes=share_scratch(own_logits, near_slabs)
        + [pltpu.VMEM(pieces.shape, BF16), pltpu.SemaphoreType.DMA]
        + [pltpu.VMEM(own_logits.shape, F32), pltpu.SemaphoreType.DMA]
        + [pltpu.VMEM(queries.shape, F32), pltpu.SemaphoreType.DMA]
        + [pltpu.VMEM(near_slabs.shape, BF16), pltpu.SemaphoreType.DMA((slabs,))],
        compiler_params=params(),
        name="near_grads",
        cost_estimate=cost(BUSY, 8),
    )(queries, others, target, totals, own_logits, other_logits, pieces, near_slabs, far_slabs)


def add_kernel(own_ref, part_ref, *refs):
    out_ref, own, part, made, own_in, part_in, left = refs[-7:]
    pieces = [pl.ds(i * (part.shape[0] // 4), part.shape[0] // 4) for i in range(4)]
    halves = [load(part_ref.at[p], part.at[p], part_in.at[i]) for i, p in enumerate(pieces)]
    if own.shape == part.shape:
        sums = [load(own_ref.at[p], own.at[p], own_in.at[i]) for i, p in enumerate(pieces)]
        own_ref = own
    stores = []
    for i, p in enumerate(pieces):
        halves[i].wait()
        if own_ref is own:
            sums[i].wait()
        rows = slice(p.start, p.start + p.size)
        made[rows, :] = (own_ref[rows, :] + part[rows, :].astype(F32)).astype(BF16)
        stores.append(load(made.at[p], out_ref.at[p], left.at[i]))
    for store in stores:
        store.wait()


def add_parts(own, part, hint, *waits):
    sems = pltpu.SemaphoreType.DMA((4,))
    return pl.pallas_call(
        add_kernel,
        in_specs=[HBM if waits else VMEM, ANY] + [ANY] * len(waits),
        out_specs=HBM,
        out_shape=pltpu.HBM(own.shape, BF16),
        scratch_shapes=[
            pltpu.VMEM(own.shape if waits else (8, 128), F32),
            pltpu.VMEM(own.shape, BF16),
            pltpu.VMEM(own.shape, BF16),
        ]
        + [sems] * 3,
        compiler_params=params(),
        name="add_parts",
        cost_estimate=cost(hint, 4),
    )(in_hbm(own) if waits else own, part, *waits)


def on_device(queries, passages, block_ids, positives):
    height, blocks, width = passages.shape
    refs = block_ids.shape[1]
    groups, planes, ranks = lax.axis_size("group"), lax.axis_size("z"), lax.axis_size("rank")
    slabs = groups * ranks
    z = lax.axis_index("z")
    to_pair = [(i, i ^ 1) for i in range(planes)]
    across = [(i, (i + planes // 2) % planes) for i in range(planes)]

    def exchange(slab_array):
        return lax.all_to_all(slab_array, PLANE, split_axis=0, concat_axis=0, tiled=True)

    ids = block_ids.T
    early = queries.shape[0] * 3 // 8
    own_rows = jnp.transpose(passages, (1, 0, 2))
    near_slabs = in_hbm(exchange(gather_rows(ids, own_rows, slabs, planes, ranks, 0)))
    pair_rows = lax.ppermute(passages.reshape(height * blocks, width), "z", to_pair)
    low, high = split_rows(in_hbm(queries), early)
    others_low = lax.ppermute(low, "z", across)
    others_positives = lax.ppermute(positives, "z", across).reshape(1, -1)
    others_high = lax.ppermute(after(high, others_positives), "z", across)

    table = block_ids.reshape(groups, planes, ranks, refs)
    both = jnp.stack([jnp.take(table, z, axis=1), jnp.take(table, (z + planes // 2) % planes, axis=1)], axis=2)
    place = (jnp.arange(height, dtype=jnp.int32) * blocks + both.reshape(-1, 1)).reshape(1, -1)
    spread = (jnp.arange(height * blocks, dtype=jnp.int32)[:, None] == place).astype(BF16)
    by_shift = jnp.take(both.reshape(slabs, -1), plane_place(ranks) ^ jnp.arange(slabs), axis=0)
    near_place = (jnp.arange(height, dtype=jnp.int32) * blocks + by_shift.reshape(-1, 1)).reshape(1, -1)
    near_spread = (jnp.arange(height * blocks, dtype=jnp.int32)[:, None] == near_place).astype(BF16)
    far_slabs = in_hbm(exchange(select_rows(spread, pair_rows, slabs)))

    chosen = positives.reshape(1, -1)
    chosen_others = others_positives
    places = [functools.partial(place_of, far, planes, ranks, refs, height) for far in range(2)]
    own_logits, own_stats, own = own_half(in_hbm(queries), near_slabs, chosen, places[0])
    other_logits, saved_logits, far_logits, stats, near_target, far_target, others, near_rows, far_rows = rest_half(
        own, others_low, others_high, near_slabs, far_slabs, chosen, chosen_others, own_stats, places
    )
    partner = lax.ppermute(stats, "z", across)
    sums, hit = early_grads(stats, near_target, far_target, other_logits, far_logits, near_rows, far_rows)
    other_part, totals, loss = other_grads(stats, partner, near_target, far_target, sums, hit)
    own_logits, other_logits = in_hbm(own_logits), in_hbm(saved_logits)
    far_contrib, pieces = far_grads(own, others, far_logits, far_target, totals, in_hbm(other_part), far_slabs)
    far_back = in_hbm(exchange(far_contrib).reshape(-1, width))
    kept, *given, own_grad = near_grads(
        own, others, near_target, totals, own_logits, other_logits, in_hbm(pieces), near_slabs, far_slabs, ranks
    )
    joined = join_cores(kept, [lax.ppermute(array, PLANE, [(i, i ^ 1) for i in range(slabs)]) for array in given])
    own_part = lax.ppermute(other_part, "z", across)
    far_sum = segment_rows(spread, [far_back])
    pair_sum = lax.ppermute(far_sum, "z", to_pair)
    near_back = [
        lax.ppermute(array, PLANE, [(i, i ^ (2 * g)) for i in range(slabs)]) if g else array
        for g, array in enumerate(joined)
    ]
    query_grad = add_parts(own_grad, own_part, BUSY, in_hbm(far_sum))
    near_sum = segment_rows(near_spread, near_back, in_hbm(query_grad))
    row_sum = add_parts(near_sum, pair_sum, 1 << 20)
    return loss.reshape(-1), query_grad, row_sum.reshape(passages.shape)


def solution(mesh):
    groups, members = mesh.devices.shape
    split = Mesh(mesh.devices.reshape(groups, PLANES, members // PLANES), ("group", "z", "rank"))
    rows = ("group", "z", "rank")
    return jax.shard_map(
        on_device,
        mesh=split,
        in_specs=(P(rows, None), P(rows, None, None), P(), P(rows)),
        out_specs=(P(rows), P(rows, None), P(rows, None, None)),
        check_vma=False,
    )
```

```python
import functools

import jax
import jax.numpy as jnp
from jax import lax
from jax.experimental import pallas as pl
from jax.experimental.pallas import tpu as pltpu
from jax.sharding import Mesh
from jax.sharding import PartitionSpec as P

SCALE = 0.8
PLANES = 4
CHUNKS = 1
BF16 = jnp.bfloat16
F32 = jnp.float32
BUSY = 1 << 37
PLANE = ("group", "rank")
ANY = pl.BlockSpec(memory_space=pl.ANY)
HBM = pl.BlockSpec(memory_space=pltpu.HBM)
VMEM = pl.BlockSpec(memory_space=pltpu.VMEM)
SMEM = pl.BlockSpec(memory_space=pltpu.SMEM)


def params():
    return pltpu.CompilerParams(vmem_limit_bytes=28 << 20)


def cost(flops, mib):
    return pl.CostEstimate(flops=flops, bytes_accessed=mib << 20, transcendentals=0)


def in_hbm(array):
    return pltpu.with_memory_space_constraint(array, pltpu.HBM)


def shape(dims, dtype):
    return jax.ShapeDtypeStruct(dims, dtype)


def after_kernel(*refs):
    del refs


def after(array, *others, where=VMEM):
    return pl.pallas_call(
        after_kernel,
        in_specs=[ANY] + [where] * len(others),
        out_specs=ANY,
        out_shape=shape(array.shape, array.dtype),
        input_output_aliases={0: 0},
        name="after",
    )(array, *others)


def copy_kernel(source_ref, out_ref, held, done):
    pieces = [pl.ds(i * (held.shape[0] // 4), held.shape[0] // 4) for i in range(4)]
    loads = [load(source_ref.at[p], held.at[p], done.at[0, i]) for i, p in enumerate(pieces)]
    stores = []
    for i, p in enumerate(pieces):
        loads[i].wait()
        stores.append(load(held.at[p], out_ref.at[p], done.at[1, i]))
    for store in stores:
        store.wait()


def copy_rows(array):
    return pl.pallas_call(
        copy_kernel,
        in_specs=[HBM],
        out_specs=HBM,
        out_shape=pltpu.HBM(array.shape, BF16),
        scratch_shapes=[pltpu.VMEM(array.shape, BF16), pltpu.SemaphoreType.DMA((2, 4))],
        compiler_params=params(),
        name="copy_rows",
        cost_estimate=cost(0, 2),
    )(array)


def gather_kernel(planes, ranks, ids, rows_ref, out_ref, made, left):
    slabs, depth, width = out_ref.shape
    height = rows_ref.shape[1]
    refs = ids.shape[0]
    z = lax.axis_index("z")

    def sent(slab):
        return pltpu.make_async_copy(made.at[slab], out_ref.at[slab], left.at[slab])

    def fill(slab, carry):
        for pick in range(2 * refs):
            there = z if pick < refs else planes - 1 - z
            owner = (slab // ranks * planes + there) * ranks + slab % ranks
            made[slab, pick * height : (pick + 1) * height, :] = rows_ref[ids[pick % refs, owner]]
        sent(slab).start()
        return carry

    def drain(slab, carry):
        sent(slab).wait()
        return carry

    lax.fori_loop(0, slabs, fill, 0)
    lax.fori_loop(0, slabs, drain, 0)


def gather_rows(ids, rows, slabs, planes, ranks, flops):
    blocks, height, width = rows.shape
    dims = (slabs, 2 * ids.shape[0] * height, width)
    return pl.pallas_call(
        functools.partial(gather_kernel, planes, ranks),
        in_specs=[SMEM, VMEM],
        out_specs=HBM,
        out_shape=pltpu.HBM(dims, BF16),
        scratch_shapes=[pltpu.VMEM(dims, BF16), pltpu.SemaphoreType.DMA((slabs,))],
        compiler_params=params(),
        name="gather_rows",
        cost_estimate=cost(flops, 4),
    )(ids, rows)


def select_kernel(spread_ref, rows_ref, out_ref, made, left):
    slabs, depth, width = out_ref.shape
    part = slabs // 2
    stores = []
    for c in range(2):
        some = slice(c * part, (c + 1) * part)
        lanes = slice(c * part * depth, (c + 1) * part * depth)
        product = lax.dot_general(
            spread_ref[:, lanes], rows_ref[...], (((0,), (0,)), ((), ())), preferred_element_type=F32
        )
        made[some] = product.astype(BF16).reshape(part, depth, width)
        some = pl.ds(c * part, part)
        stores.append(load(made.at[some], out_ref.at[some], left.at[c]))
    for store in stores:
        store.wait()


def select_rows(spread, rows, slabs):
    dims = (slabs, spread.shape[1] // slabs, rows.shape[1])
    return pl.pallas_call(
        select_kernel,
        in_specs=[VMEM, VMEM],
        out_specs=HBM,
        out_shape=pltpu.HBM(dims, BF16),
        scratch_shapes=[pltpu.VMEM(dims, BF16), pltpu.SemaphoreType.DMA((2,))],
        compiler_params=params(),
        name="select_rows",
        cost_estimate=cost(BUSY, 4),
    )(spread, rows)


def plane_place(ranks):
    return lax.axis_index("group") * ranks + lax.axis_index("rank")


def join_kernel(kept_ref, *refs):
    chips, depth, _ = kept_ref.shape
    given_refs = refs[:chips]
    *out_refs, held, arrived, left = refs[chips:]
    for g in range(chips):
        load(kept_ref.at[g], held.at[g, pl.ds(0, depth)], arrived.at[g, 0])
        load(given_refs[g], held.at[g, pl.ds(depth, depth)], arrived.at[g, 1])
    for g in range(chips):
        pltpu.make_async_copy(kept_ref.at[g], held.at[g, pl.ds(0, depth)], arrived.at[g, 0]).wait()
        pltpu.make_async_copy(given_refs[g], held.at[g, pl.ds(depth, depth)], arrived.at[g, 1]).wait()
        load(held.at[g], out_refs[g], left.at[g])
    for g in range(chips):
        pltpu.make_async_copy(held.at[g], out_refs[g], left.at[g]).wait()


def join_cores(kept, given):
    chips, depth, width = kept.shape
    return pl.pallas_call(
        join_kernel,
        in_specs=[HBM] + [ANY] * chips,
        out_specs=[HBM] * chips,
        out_shape=[pltpu.HBM((2 * depth, width), BF16)] * chips,
        scratch_shapes=[
            pltpu.VMEM((chips, 2 * depth, width), BF16),
            pltpu.SemaphoreType.DMA((chips, 2)),
            pltpu.SemaphoreType.DMA((chips,)),
        ],
        compiler_params=params(),
        name="join_cores",
        cost_estimate=cost(1 << 20, 4),
    )(kept, *given)


def segment_kernel(stripes, arrays, spread_ref, *refs):
    slab_refs = refs[:arrays]
    out_ref, held, result, arrived, left = refs[-5:]
    tile = out_ref.shape[1] // stripes
    depth = held.shape[1] // arrays
    columns = [pl.ds(t * tile, tile) for t in range(stripes)]
    loads = [
        Several(
            [
                load(ref.at[:, columns[t]], held.at[t, pl.ds(i * depth, depth)], arrived.at[t, i])
                for i, ref in enumerate(slab_refs)
            ]
        )
        for t in range(stripes)
    ]
    stores = []
    for t in range(stripes):
        loads[t].wait()
        total = jnp.dot(spread_ref[...], held[t], preferred_element_type=F32)
        if out_ref.dtype == F32:
            out_ref[:, t * tile : (t + 1) * tile] = total
        else:
            result[t] = total.astype(BF16)
            stores.append(load(result.at[t], out_ref.at[:, columns[t]], left.at[t]))
    for store in stores:
        store.wait()


class Several:
    def __init__(self, copies):
        self.copies = copies

    def wait(self):
        for copy in self.copies:
            copy.wait()


def segment_rows(spread, arrays, wait=None):
    stripes = 2
    rows, depth = spread.shape
    width = arrays[0].shape[-1]
    tile = width // stripes
    extra = [] if wait is None else [wait]
    return pl.pallas_call(
        functools.partial(segment_kernel, stripes, len(arrays)),
        in_specs=[VMEM] + [ANY] * (len(arrays) + len(extra)),
        out_specs=VMEM if extra else HBM,
        out_shape=shape((rows, width), F32) if extra else pltpu.HBM((rows, width), BF16),
        scratch_shapes=[
            pltpu.VMEM((stripes, depth, tile), BF16),
            pltpu.VMEM((stripes, rows, tile), BF16),
            pltpu.SemaphoreType.DMA((stripes, len(arrays))),
            pltpu.SemaphoreType.DMA((stripes,)),
        ],
        compiler_params=params(),
        name="segment_rows",
        cost_estimate=cost(BUSY if extra else 1 << 30, 4),
    )(spread, *arrays, *extra)


def candidates(slabs_ref, q, chunk):
    slabs, depth, width = slabs_ref.shape
    part, half = slabs // CHUNKS, depth // 2
    block = slabs_ref[chunk * part : (chunk + 1) * part, q * half : (q + 1) * half, :]
    return block.reshape(part * half, width)


def hits(rows, chunk, target_row):
    row = lax.broadcasted_iota(jnp.int32, (rows, target_row.shape[1]), 0)
    return row + chunk * rows == target_row


def joined(a, b):
    top = jnp.maximum(a[0], b[0])
    return top, a[1] * jnp.exp(a[0] - top) + b[1] * jnp.exp(b[0] - top), a[2] + b[2]


def stat_rows(ref, q):
    return [ref[4 * q + i : 4 * q + i + 1, :] for i in range(3)]


def chunk_rows(ref, chunk):
    rows = ref.shape[1] // CHUNKS
    return slice(chunk * rows, (chunk + 1) * rows)


def place_of(far, planes, ranks, refs, height, chosen):
    owner = chosen // height
    spot = (owner // (planes * ranks) * ranks + owner % ranks) * (refs * height) + chosen % height
    return jnp.where(owner // ranks % planes == lax.axis_index("z") ^ far, spot, -1)


def load(source, held, arrived):
    copy = pltpu.make_async_copy(source, held, arrived)
    copy.start()
    return copy


def part_of(size, chunk):
    return pl.ds(chunk * (size // CHUNKS), size // CHUNKS)


def load_chunks(source, held, arrived):
    parts = [part_of(source.shape[0], c) for c in range(CHUNKS)]
    return [load(source.at[part], held.at[part], arrived.at[c]) for c, part in enumerate(parts)]


def block_logits(block_ref, slab_part, target_row, put):
    stats = None
    for c in range(CHUNKS):
        block = lax.dot_general(slab_part(c), block_ref[...], (((1,), (1,)), ((), ())), preferred_element_type=F32)
        block = SCALE * block
        put(c, block)
        top = jnp.max(block, axis=0, keepdims=True)
        total = jnp.sum(jnp.exp(block - top), axis=0, keepdims=True)
        hit = hits(block.shape[0], c, target_row)
        pick = jnp.sum(jnp.where(hit, block, 0.0), axis=0, keepdims=True)
        here = (top, total, pick)
        stats = here if c == 0 else joined(stats, here)
    return stats


def put_stats(stats_ref, q, stats):
    for i in range(3):
        stats_ref[4 * q + i : 4 * q + i + 1, :] = stats[i]
    stats_ref[4 * q + 3 : 4 * q + 4, :] = jnp.zeros_like(stats[0])


def held_rows(held, chunk):
    slabs = held.shape[0] // CHUNKS
    return held[chunk * slabs : (chunk + 1) * slabs].reshape(slabs * held.shape[1], held.shape[2])


def row_chunk(rows, chunk):
    return slice(chunk * rows // CHUNKS, (chunk + 1) * rows // CHUNKS)


def put_targets(place, target_ref, chosen_ref, chosen_others_ref):
    target_ref[...] = jnp.full(target_ref.shape, -1, jnp.int32)
    target_ref[0:1, :] = place(chosen_ref[...])
    target_ref[1:2, :] = place(chosen_others_ref[...])


def own_kernel(place, queries_ref, slabs_ref, chosen_ref, logits_ref, stats_ref, kept_ref, held, made, arrived, came, left):
    half = slabs_ref.shape[1] // 2
    loads = load_chunks(slabs_ref.at[:, pl.ds(0, half)], held, arrived)
    load(queries_ref, kept_ref, came).wait()
    stores = []

    def slab_part(c):
        loads[c].wait()
        return held_rows(held, c)

    def put(c, block):
        part = part_of(logits_ref.shape[0], c)
        made[row_chunk(made.shape[0], c), :] = block
        stores.append(load(made.at[part], logits_ref.at[part], left.at[c]))

    stats = block_logits(kept_ref, slab_part, place(chosen_ref[...]), put)
    put_stats(stats_ref, 0, stats)
    put_stats(stats_ref, 1, stats)
    for store in stores:
        store.wait()


def own_half(queries, slabs, chosen, place):
    size, width = queries.shape
    rows = slabs.shape[0] * slabs.shape[1] // 2
    return pl.pallas_call(
        functools.partial(own_kernel, place),
        in_specs=[HBM, HBM, VMEM],
        out_specs=[HBM, VMEM, VMEM],
        out_shape=[pltpu.HBM((rows, size), F32), shape((8, size), F32), shape((size, width), BF16)],
        scratch_shapes=[
            pltpu.VMEM((slabs.shape[0], slabs.shape[1] // 2, width), BF16),
            pltpu.VMEM((rows, size), F32),
            pltpu.SemaphoreType.DMA((CHUNKS,)),
            pltpu.SemaphoreType.DMA,
            pltpu.SemaphoreType.DMA((CHUNKS,)),
        ],
        compiler_params=params(),
        name="own_half",
        cost_estimate=cost(BUSY, 4),
    )(queries, slabs, chosen)


def rest_kernel(
    near_place, far_place, queries_ref, inner_ref, outer_ref, near_ref, far_ref, chosen_ref, chosen_others_ref, own_stats_ref,
    other_logits_ref, saved_ref, far_logits_ref, stats_ref, near_target_ref, far_target_ref, others_ref, near_rows, far_rows,
    held, near_in, far_in, held_in, left, came,
):
    half = near_ref.shape[1] // 2
    held_loads = load_chunks(far_ref.at[:, pl.ds(0, half)], held, held_in)
    z = lax.axis_index("z")
    inner = (z > 0) & (z < lax.axis_size("z") - 1)

    @pl.when(inner)
    def _():
        load(inner_ref, others_ref, came)

    @pl.when(jnp.logical_not(inner))
    def _():
        load(outer_ref, others_ref, came)

    whole = [pltpu.make_async_copy(outer_ref, others_ref, came)]
    near_loads = load_chunks(near_ref.at[:, pl.ds(half, half)], near_rows, near_in)
    far_loads = load_chunks(far_ref.at[:, pl.ds(half, half)], far_rows, far_in)
    put_targets(near_place, near_target_ref, chosen_ref, chosen_others_ref)
    put_targets(far_place, far_target_ref, chosen_ref, chosen_others_ref)
    stores = []

    def part(loads, rows):
        def get(c):
            loads[c].wait()
            return held_rows(rows, c)

        return get

    def put_near(c, block):
        rows = part_of(other_logits_ref.shape[0], c)
        other_logits_ref[row_chunk(other_logits_ref.shape[0], c), :] = block
        stores.append(load(other_logits_ref.at[rows], saved_ref.at[rows], left.at[c]))

    def put_far(q):
        def put(c, block):
            far_logits_ref[q, chunk_rows(far_logits_ref, c), :] = block

        return put

    own = block_logits(queries_ref, part(held_loads, held), far_target_ref[0:1, :], put_far(0))
    put_stats(stats_ref, 0, joined(stat_rows(own_stats_ref, 0), own))
    for copy in whole:
        copy.wait()
    near = block_logits(others_ref, part(near_loads, near_rows), near_target_ref[1:2, :], put_near)
    far = block_logits(others_ref, part(far_loads, far_rows), far_target_ref[1:2, :], put_far(1))
    put_stats(stats_ref, 1, joined(near, far))
    for store in stores:
        store.wait()


def rest_half(queries, inner, outer, near_slabs, far_slabs, chosen, chosen_others, own_stats, places):
    size, width = queries.shape
    rows = near_slabs.shape[0] * near_slabs.shape[1] // 2
    part = (near_slabs.shape[0], near_slabs.shape[1] // 2, width)
    chunk_sems = pltpu.SemaphoreType.DMA((CHUNKS,))
    return pl.pallas_call(
        functools.partial(rest_kernel, *places),
        in_specs=[VMEM] + [ANY] * 2 + [HBM] * 2 + [VMEM] * 3,
        out_specs=[VMEM, HBM] + [VMEM] * 7,
        out_shape=[
            shape((rows, size), F32),
            pltpu.HBM((rows, size), F32),
            shape((2, rows, size), F32),
            shape((8, size), F32),
            shape((8, size), jnp.int32),
            shape((8, size), jnp.int32),
            shape((size, width), BF16),
            shape(part, BF16),
            shape(part, BF16),
        ],
        scratch_shapes=[pltpu.VMEM(part, BF16)] + [chunk_sems] * 4 + [pltpu.SemaphoreType.DMA],
        compiler_params=params(),
        name="rest_half",
        cost_estimate=cost(3 << 29, 8),
    )(queries, inner, outer, near_slabs, far_slabs, chosen, chosen_others, own_stats)


def log_totals(here_ref, there_ref):
    out = []
    for q in range(2):
        top, total, pick = joined(stat_rows(here_ref, q), stat_rows(there_ref, 1 - q))
        out.append((top + jnp.log(total), pick))
    return out


def dlogits(logits, log_total, chunk, target_row):
    hit = hits(logits.shape[0], chunk, target_row)
    return (jnp.exp(logits - log_total) - jnp.where(hit, 1.0, 0.0)).astype(BF16)


def send_contrib(made, out_ref, left, chunk, q, piece, block, complete):
    slabs, depth, width = out_ref.shape
    part, half = slabs // CHUNKS, depth // 2
    product = SCALE * jnp.dot(piece, block, preferred_element_type=F32)
    made[chunk, :, q * half : (q + 1) * half, :] = product.astype(BF16).reshape(part, half, width)
    if not complete:
        return []
    store = pltpu.make_async_copy(made.at[chunk], out_ref.at[pl.ds(chunk * part, part)], left.at[chunk])
    store.start()
    return [store]


def contrib_scratch(slabs):
    return [
        pltpu.VMEM((CHUNKS, slabs.shape[0] // CHUNKS) + slabs.shape[1:], BF16),
        pltpu.SemaphoreType.DMA((CHUNKS,)),
    ]


def load_share(q, logits_ref, near_ref, far_ref, logits, near, far, came):
    rows, slabs, half = logits_ref.shape[0], near_ref.shape[0], near_ref.shape[1] // 2
    picks = pl.ds(q * half, half)
    copies = []
    for c in range(CHUNKS):
        part, some = part_of(rows, c), part_of(slabs, c)
        copies.append(
            [
                load(far_ref.at[some, picks], far.at[some], came.at[0, c]),
                load(logits_ref.at[part], logits.at[part], came.at[1, c]),
                load(near_ref.at[some, picks], near.at[some], came.at[2, c]),
            ]
        )
    return copies


def query_share(copies, far_piece, near_piece, near, far, use):
    dims = (((0,), (0,)), ((), ()))
    slabs, half, width = near.shape
    total = None
    for c in range(CHUNKS):
        some = slice(c * slabs // CHUNKS, (c + 1) * slabs // CHUNKS)
        rows = slabs // CHUNKS * half
        piece = far_piece(c)
        copies[c][0].wait()
        share = lax.dot_general(piece, far[some].reshape(rows, width), dims, preferred_element_type=F32)
        copies[c][1].wait()
        piece = near_piece(c)
        copies[c][2].wait()
        share += lax.dot_general(piece, near[some].reshape(rows, width), dims, preferred_element_type=F32)
        total = share if c == 0 else total + share
        if use is not None:
            use(c, piece)
    return total


def share_scratch(logits, slabs):
    part = (slabs.shape[0], slabs.shape[1] // 2, slabs.shape[2])
    return [
        pltpu.VMEM(logits.shape, F32),
        pltpu.VMEM(part, BF16),
        pltpu.VMEM(part, BF16),
        pltpu.SemaphoreType.DMA((3, CHUNKS)),
    ]


def early_kernel(stats_ref, near_target_ref, far_target_ref, near_logits_ref, far_logits_ref, near_ref, far_ref, sums_ref, hit_ref):
    dims = (((0,), (0,)), ((), ()))
    top = stats_ref[4:5, :]
    rows = near_logits_ref.shape[0]
    for c in range(CHUNKS):
        part = row_chunk(rows, c)
        for i, (score, target_ref, slab_ref) in enumerate(
            ((near_logits_ref[part, :], near_target_ref, near_ref), (far_logits_ref[1, part, :], far_target_ref, far_ref))
        ):
            block = held_rows(slab_ref, c)
            weight = jnp.exp(score - top).astype(BF16)
            hit = jnp.where(hits(score.shape[0], c, target_ref[1:2, :]), 1.0, 0.0).astype(BF16)
            product = lax.dot_general(weight, block, dims, preferred_element_type=F32)
            picked = lax.dot_general(hit, block, dims, preferred_element_type=F32)
            if c == 0 and i == 0:
                sums_ref[...] = product
                hit_ref[...] = picked
            else:
                sums_ref[...] += product
                hit_ref[...] += picked


def early_grads(stats, near_target, far_target, near_logits, far_logits, near_rows, far_rows):
    size, width = near_logits.shape[1], near_rows.shape[2]
    return pl.pallas_call(
        early_kernel,
        in_specs=[VMEM] * 7,
        out_specs=[VMEM] * 2,
        out_shape=[shape((size, width), F32)] * 2,
        compiler_params=params(),
        name="early_grads",
        cost_estimate=cost(BUSY, 4),
    )(stats, near_target, far_target, near_logits, far_logits, near_rows, far_rows)


def other_kernel(here_ref, there_ref, near_target_ref, far_target_ref, sums_ref, hit_ref, other_ref, totals_ref, loss_ref, made, left):
    totals = log_totals(here_ref, there_ref)
    total = totals[1][0]
    top, _, pick = stat_rows(here_ref, 1)
    held = jnp.maximum(near_target_ref[1:2, :], far_target_ref[1:2, :]) >= 0
    scale = jnp.exp(top - total)
    counted = scale * jnp.exp(jnp.where(held, pick - top, 0.0)).astype(BF16).astype(F32)
    wanted = (jnp.exp(jnp.where(held, pick - total, 0.0)) - 1.0).astype(BF16).astype(F32)
    rows = [scale, jnp.where(held, wanted - counted, 0.0)]
    columns = jnp.transpose(jnp.concatenate(rows + [jnp.zeros_like(scale)] * 6, axis=0))
    stores = []
    size = made.shape[0] // 4
    for c in range(4):
        part = slice(c * size, (c + 1) * size)
        share = columns[part, 0:1] * sums_ref[part, :] + columns[part, 1:2] * hit_ref[part, :]
        made[part, :] = (SCALE * share).astype(BF16)
        some = pl.ds(c * size, size)
        stores.append(load(made.at[some], other_ref.at[some], left.at[c]))
    totals_ref[...] = jnp.zeros_like(totals_ref)
    for q in range(2):
        totals_ref[q : q + 1, :] = totals[q][0]
    loss_ref[...] = totals[0][0] - totals[0][1]
    for store in stores:
        store.wait()


def other_grads(here, there, near_target, far_target, sums, hit):
    size, width = sums.shape
    return pl.pallas_call(
        other_kernel,
        in_specs=[VMEM] * 6,
        out_specs=[HBM, VMEM, VMEM],
        out_shape=[pltpu.HBM((size, width), BF16), shape((8, size), F32), shape((1, size), F32)],
        scratch_shapes=[pltpu.VMEM((size, width), BF16), pltpu.SemaphoreType.DMA((4,))],
        compiler_params=params(),
        name="other_grads",
        cost_estimate=cost(1 << 20, 4),
    )(here, there, near_target, far_target, sums, hit)


def far_kernel(
    queries_ref, others_ref, logits_ref, target_ref, totals_ref, wait_ref,
    contrib_ref, pieces_ref, made, left, pieces, pieces_out,
):
    del wait_ref
    slabs, depth, width = contrib_ref.shape
    half = depth // 2
    stores = []
    for q, block_ref in enumerate((queries_ref, others_ref)):
        piece = dlogits(logits_ref[q], totals_ref[q : q + 1, :], 0, target_ref[q : q + 1, :])
        if q == 0:
            pieces[...] = piece
            stores.append(load(pieces, pieces_ref, pieces_out))
        product = SCALE * jnp.dot(piece, block_ref[...], preferred_element_type=F32)
        made[q] = product.astype(BF16).reshape(slabs, half, width)
        stores.append(load(made.at[q], contrib_ref.at[:, pl.ds(q * half, half)], left.at[q]))
    for store in stores:
        store.wait()


def far_grads(queries, others, logits, target, totals, wait, slabs):
    size = queries.shape[0]
    rows = logits.shape[1]
    count, depth, width = slabs.shape
    return pl.pallas_call(
        far_kernel,
        in_specs=[VMEM] * 5 + [ANY],
        out_specs=[HBM] * 2,
        out_shape=[pltpu.HBM(slabs.shape, BF16), pltpu.HBM((rows, size), BF16)],
        scratch_shapes=[
            pltpu.VMEM((2, count, depth // 2, width), BF16),
            pltpu.SemaphoreType.DMA((2,)),
            pltpu.VMEM((rows, size), BF16),
            pltpu.SemaphoreType.DMA,
        ],
        compiler_params=params(),
        name="far_grads",
        cost_estimate=cost(1 << 30, 4),
    )(queries, others, logits, target, totals, wait)


def near_kernel(
    ranks, queries_ref, others_ref, target_ref, totals_ref, own_logits_ref, other_logits_ref, pieces_ref, near_ref, far_ref,
    kept_ref, *refs,
):
    *given_refs, own_ref, logits, near, far, came, pieces, begun, score, scored, own, own_out, made, left = refs
    first = load(pieces_ref, pieces, begun)
    copies = load_share(0, own_logits_ref, near_ref, far_ref, logits, near, far, came)
    other_scores = load(other_logits_ref, score, scored)
    slabs, depth, width = made.shape
    half = depth // 2

    def store_part(q, piece, block_ref):
        product = SCALE * jnp.dot(piece, block_ref[...], preferred_element_type=F32)
        made[:, q * half : (q + 1) * half, :] = product.astype(BF16).reshape(slabs, half, width)

    other_scores.wait()
    store_part(1, dlogits(score[...], totals_ref[1:2, :], 0, target_ref[1:2, :]), others_ref)
    first.wait()

    def far_piece(c):
        return pieces[row_chunk(logits.shape[0], c), :]

    def near_piece(c):
        return dlogits(logits[row_chunk(logits.shape[0], c), :], totals_ref[0:1, :], c, target_ref[0:1, :])

    def use(c, piece):
        store_part(0, piece, queries_ref)

    total = query_share(copies, far_piece, near_piece, near, far, use)
    place = plane_place(ranks)
    stores = []
    for s in range(slabs):
        out_ref = given_refs[s // 2] if s % 2 else kept_ref.at[s // 2]
        stores.append(load(made.at[place ^ s], out_ref, left.at[s]))
    own[...] = SCALE * total
    stores.append(load(own, own_ref, own_out))
    for store in stores:
        store.wait()


def near_grads(queries, others, target, totals, own_logits, other_logits, pieces, near_slabs, far_slabs, ranks):
    slabs, depth, width = near_slabs.shape
    kept = pltpu.HBM((slabs // 2, depth, width), BF16)
    given = [pltpu.HBM((depth, width), BF16)] * (slabs // 2)
    return pl.pallas_call(
        functools.partial(near_kernel, ranks),
        in_specs=[VMEM] * 4 + [HBM] * 5,
        out_specs=[HBM] * (2 + slabs // 2),
        out_shape=[kept, *given, pltpu.HBM(queries.shape, F32)],
        scratch_shapes=share_scratch(own_logits, near_slabs)
        + [pltpu.VMEM(pieces.shape, BF16), pltpu.SemaphoreType.DMA]
        + [pltpu.VMEM(own_logits.shape, F32), pltpu.SemaphoreType.DMA]
        + [pltpu.VMEM(queries.shape, F32), pltpu.SemaphoreType.DMA]
        + [pltpu.VMEM(near_slabs.shape, BF16), pltpu.SemaphoreType.DMA((slabs,))],
        compiler_params=params(),
        name="near_grads",
        cost_estimate=cost(BUSY, 8),
    )(queries, others, target, totals, own_logits, other_logits, pieces, near_slabs, far_slabs)


def add_kernel(own_ref, part_ref, *refs):
    out_ref, own, part, made, own_in, part_in, left = refs[-7:]
    pieces = [pl.ds(i * (part.shape[0] // 4), part.shape[0] // 4) for i in range(4)]
    halves = [load(part_ref.at[p], part.at[p], part_in.at[i]) for i, p in enumerate(pieces)]
    if own.shape == part.shape:
        sums = [load(own_ref.at[p], own.at[p], own_in.at[i]) for i, p in enumerate(pieces)]
        own_ref = own
    stores = []
    for i, p in enumerate(pieces):
        halves[i].wait()
        if own_ref is own:
            sums[i].wait()
        rows = slice(p.start, p.start + p.size)
        made[rows, :] = (own_ref[rows, :] + part[rows, :].astype(F32)).astype(BF16)
        stores.append(load(made.at[p], out_ref.at[p], left.at[i]))
    for store in stores:
        store.wait()


def add_parts(own, part, hint, *waits):
    sems = pltpu.SemaphoreType.DMA((4,))
    return pl.pallas_call(
        add_kernel,
        in_specs=[HBM if waits else VMEM, ANY] + [ANY] * len(waits),
        out_specs=HBM,
        out_shape=pltpu.HBM(own.shape, BF16),
        scratch_shapes=[
            pltpu.VMEM(own.shape if waits else (8, 128), F32),
            pltpu.VMEM(own.shape, BF16),
            pltpu.VMEM(own.shape, BF16),
        ]
        + [sems] * 3,
        compiler_params=params(),
        name="add_parts",
        cost_estimate=cost(hint, 4),
    )(in_hbm(own) if waits else own, part, *waits)


def on_device(queries, passages, block_ids, positives):
    height, blocks, width = passages.shape
    refs = block_ids.shape[1]
    groups, planes, ranks = lax.axis_size("group"), lax.axis_size("z"), lax.axis_size("rank")
    slabs = groups * ranks
    z = lax.axis_index("z")
    to_pair = [(i, i ^ 1) for i in range(planes)]
    across = [(i, planes - 1 - i) for i in range(planes)]

    def exchange(slab_array):
        return lax.all_to_all(slab_array, PLANE, split_axis=0, concat_axis=0, tiled=True)

    ids = block_ids.T
    own_rows = jnp.transpose(passages, (1, 0, 2))
    near_slabs = in_hbm(exchange(gather_rows(ids, own_rows, slabs, planes, ranks, 0)))
    pair_rows = lax.ppermute(passages.reshape(height * blocks, width), "z", to_pair)
    inner = [pair for pair in across if 0 < pair[0] < planes - 1]
    outer = [pair for pair in across if pair not in inner]
    others_inner = lax.ppermute(queries, "z", inner)
    others_positives = lax.ppermute(positives, "z", across).reshape(1, -1)

    table = block_ids.reshape(groups, planes, ranks, refs)
    both = jnp.stack([jnp.take(table, z, axis=1), jnp.take(table, planes - 1 - z, axis=1)], axis=2)
    place = (jnp.arange(height, dtype=jnp.int32) * blocks + both.reshape(-1, 1)).reshape(1, -1)
    spread = (jnp.arange(height * blocks, dtype=jnp.int32)[:, None] == place).astype(BF16)
    by_shift = jnp.take(both.reshape(slabs, -1), plane_place(ranks) ^ jnp.arange(slabs), axis=0)
    near_place = (jnp.arange(height, dtype=jnp.int32) * blocks + by_shift.reshape(-1, 1)).reshape(1, -1)
    near_spread = (jnp.arange(height * blocks, dtype=jnp.int32)[:, None] == near_place).astype(BF16)
    far_sent = select_rows(spread, pair_rows, slabs)
    others_outer = lax.ppermute(after(copy_rows(in_hbm(queries)), in_hbm(far_sent), where=HBM), "z", outer)
    far_slabs = in_hbm(exchange(far_sent))

    chosen = positives.reshape(1, -1)
    chosen_others = others_positives
    places = [functools.partial(place_of, far, planes, ranks, refs, height) for far in range(2)]
    own_logits, own_stats, own = own_half(in_hbm(queries), near_slabs, chosen, places[0])
    other_logits, saved_logits, far_logits, stats, near_target, far_target, others, near_rows, far_rows = rest_half(
        own, others_inner, others_outer, near_slabs, far_slabs, chosen, chosen_others, own_stats, places
    )
    partner = lax.ppermute(stats, "z", across)
    sums, hit = early_grads(stats, near_target, far_target, other_logits, far_logits, near_rows, far_rows)
    other_part, totals, loss = other_grads(stats, partner, near_target, far_target, sums, hit)
    own_logits, other_logits = in_hbm(own_logits), in_hbm(saved_logits)
    far_contrib, pieces = far_grads(own, others, far_logits, far_target, totals, in_hbm(other_part), far_slabs)
    far_back = in_hbm(exchange(far_contrib).reshape(-1, width))
    kept, *given, own_grad = near_grads(
        own, others, near_target, totals, own_logits, other_logits, in_hbm(pieces), near_slabs, far_slabs, ranks
    )
    joined = join_cores(kept, [lax.ppermute(array, PLANE, [(i, i ^ 1) for i in range(slabs)]) for array in given])
    own_part = lax.ppermute(other_part, "z", across)
    far_sum = segment_rows(spread, [far_back])
    pair_sum = lax.ppermute(far_sum, "z", to_pair)
    near_back = [
        lax.ppermute(array, PLANE, [(i, i ^ (2 * g)) for i in range(slabs)]) if g else array
        for g, array in enumerate(joined)
    ]
    query_grad = add_parts(own_grad, own_part, BUSY, in_hbm(far_sum))
    near_sum = segment_rows(near_spread, near_back, in_hbm(query_grad))
    row_sum = add_parts(near_sum, pair_sum, 1 << 20)
    return loss.reshape(-1), query_grad, row_sum.reshape(passages.shape)


def solution(mesh):
    groups, members = mesh.devices.shape
    split = Mesh(mesh.devices.reshape(groups, PLANES, members // PLANES), ("group", "z", "rank"))
    rows = ("group", "z", "rank")
    return jax.shard_map(
        on_device,
        mesh=split,
        in_specs=(P(rows, None), P(rows, None, None), P(), P(rows)),
        out_specs=(P(rows), P(rows, None), P(rows, None, None)),
        check_vma=False,
    )
```

```python
import functools

import jax
import jax.numpy as jnp
from jax import lax
from jax.experimental import pallas as pl
from jax.experimental.pallas import tpu as pltpu
from jax.sharding import Mesh
from jax.sharding import PartitionSpec as P

SCALE = 0.8
PLANES = 4
CHUNKS = 1
BF16 = jnp.bfloat16
F32 = jnp.float32
BUSY = 1 << 37
PLANE = ("group", "rank")
ANY = pl.BlockSpec(memory_space=pl.ANY)
HBM = pl.BlockSpec(memory_space=pltpu.HBM)
VMEM = pl.BlockSpec(memory_space=pltpu.VMEM)
SMEM = pl.BlockSpec(memory_space=pltpu.SMEM)


def params():
    return pltpu.CompilerParams(vmem_limit_bytes=28 << 20)


def cost(flops, mib):
    return pl.CostEstimate(flops=flops, bytes_accessed=mib << 20, transcendentals=0)


def in_hbm(array):
    return pltpu.with_memory_space_constraint(array, pltpu.HBM)


def shape(dims, dtype):
    return jax.ShapeDtypeStruct(dims, dtype)


def after_kernel(*refs):
    del refs


def after(array, *others, where=VMEM):
    return pl.pallas_call(
        after_kernel,
        in_specs=[ANY] + [where] * len(others),
        out_specs=ANY,
        out_shape=shape(array.shape, array.dtype),
        input_output_aliases={0: 0},
        name="after",
    )(array, *others)


def copy_kernel(source_ref, out_ref, held, done):
    pieces = [pl.ds(i * (held.shape[0] // 4), held.shape[0] // 4) for i in range(4)]
    loads = [load(source_ref.at[p], held.at[p], done.at[0, i]) for i, p in enumerate(pieces)]
    stores = []
    for i, p in enumerate(pieces):
        loads[i].wait()
        stores.append(load(held.at[p], out_ref.at[p], done.at[1, i]))
    for store in stores:
        store.wait()


def copy_rows(array):
    return pl.pallas_call(
        copy_kernel,
        in_specs=[HBM],
        out_specs=HBM,
        out_shape=pltpu.HBM(array.shape, BF16),
        scratch_shapes=[pltpu.VMEM(array.shape, BF16), pltpu.SemaphoreType.DMA((2, 4))],
        compiler_params=params(),
        name="copy_rows",
        cost_estimate=cost(0, 2),
    )(array)


def gather_kernel(planes, ranks, ids, rows_ref, out_ref, made, left):
    slabs, depth, width = out_ref.shape
    height = rows_ref.shape[1]
    refs = ids.shape[0]
    z = lax.axis_index("z")

    def sent(slab):
        return pltpu.make_async_copy(made.at[slab], out_ref.at[slab], left.at[slab])

    def fill(slab, carry):
        for pick in range(2 * refs):
            there = z if pick < refs else planes - 1 - z
            owner = (slab // ranks * planes + there) * ranks + slab % ranks
            made[slab, pick * height : (pick + 1) * height, :] = rows_ref[ids[pick % refs, owner]]
        sent(slab).start()
        return carry

    def drain(slab, carry):
        sent(slab).wait()
        return carry

    lax.fori_loop(0, slabs, fill, 0)
    lax.fori_loop(0, slabs, drain, 0)


def gather_rows(ids, rows, slabs, planes, ranks, flops):
    blocks, height, width = rows.shape
    dims = (slabs, 2 * ids.shape[0] * height, width)
    return pl.pallas_call(
        functools.partial(gather_kernel, planes, ranks),
        in_specs=[SMEM, VMEM],
        out_specs=HBM,
        out_shape=pltpu.HBM(dims, BF16),
        scratch_shapes=[pltpu.VMEM(dims, BF16), pltpu.SemaphoreType.DMA((slabs,))],
        compiler_params=params(),
        name="gather_rows",
        cost_estimate=cost(flops, 4),
    )(ids, rows)


def select_kernel(spread_ref, rows_ref, out_ref, made, left):
    slabs, depth, width = out_ref.shape
    part = slabs // 2
    stores = []
    for c in range(2):
        some = slice(c * part, (c + 1) * part)
        lanes = slice(c * part * depth, (c + 1) * part * depth)
        product = lax.dot_general(
            spread_ref[:, lanes], rows_ref[...], (((0,), (0,)), ((), ())), preferred_element_type=F32
        )
        made[some] = product.astype(BF16).reshape(part, depth, width)
        some = pl.ds(c * part, part)
        stores.append(load(made.at[some], out_ref.at[some], left.at[c]))
    for store in stores:
        store.wait()


def select_rows(spread, rows, slabs):
    dims = (slabs, spread.shape[1] // slabs, rows.shape[1])
    return pl.pallas_call(
        select_kernel,
        in_specs=[VMEM, VMEM],
        out_specs=HBM,
        out_shape=pltpu.HBM(dims, BF16),
        scratch_shapes=[pltpu.VMEM(dims, BF16), pltpu.SemaphoreType.DMA((2,))],
        compiler_params=params(),
        name="select_rows",
        cost_estimate=cost(BUSY, 4),
    )(spread, rows)


def plane_place(ranks):
    return lax.axis_index("group") * ranks + lax.axis_index("rank")


def join_kernel(kept_ref, *refs):
    chips, depth, _ = kept_ref.shape
    given_refs = refs[:chips]
    *out_refs, held, arrived, left = refs[chips:]
    for g in range(chips):
        load(kept_ref.at[g], held.at[g, pl.ds(0, depth)], arrived.at[g, 0])
        load(given_refs[g], held.at[g, pl.ds(depth, depth)], arrived.at[g, 1])
    for g in range(chips):
        pltpu.make_async_copy(kept_ref.at[g], held.at[g, pl.ds(0, depth)], arrived.at[g, 0]).wait()
        pltpu.make_async_copy(given_refs[g], held.at[g, pl.ds(depth, depth)], arrived.at[g, 1]).wait()
        load(held.at[g], out_refs[g], left.at[g])
    for g in range(chips):
        pltpu.make_async_copy(held.at[g], out_refs[g], left.at[g]).wait()


def join_cores(kept, given):
    chips, depth, width = kept.shape
    return pl.pallas_call(
        join_kernel,
        in_specs=[HBM] + [ANY] * chips,
        out_specs=[HBM] * chips,
        out_shape=[pltpu.HBM((2 * depth, width), BF16)] * chips,
        scratch_shapes=[
            pltpu.VMEM((chips, 2 * depth, width), BF16),
            pltpu.SemaphoreType.DMA((chips, 2)),
            pltpu.SemaphoreType.DMA((chips,)),
        ],
        compiler_params=params(),
        name="join_cores",
        cost_estimate=cost(1 << 20, 4),
    )(kept, *given)


def segment_kernel(stripes, arrays, spread_ref, *refs):
    slab_refs = refs[:arrays]
    out_ref, held, result, arrived, left = refs[-5:]
    tile = out_ref.shape[1] // stripes
    depth = held.shape[1] // arrays
    columns = [pl.ds(t * tile, tile) for t in range(stripes)]
    loads = [
        Several(
            [
                load(ref.at[:, columns[t]], held.at[t, pl.ds(i * depth, depth)], arrived.at[t, i])
                for i, ref in enumerate(slab_refs)
            ]
        )
        for t in range(stripes)
    ]
    stores = []
    for t in range(stripes):
        loads[t].wait()
        total = jnp.dot(spread_ref[...], held[t], preferred_element_type=F32)
        if out_ref.dtype == F32:
            out_ref[:, t * tile : (t + 1) * tile] = total
        else:
            result[t] = total.astype(BF16)
            stores.append(load(result.at[t], out_ref.at[:, columns[t]], left.at[t]))
    for store in stores:
        store.wait()


class Several:
    def __init__(self, copies):
        self.copies = copies

    def wait(self):
        for copy in self.copies:
            copy.wait()


def segment_rows(spread, arrays, wait=None):
    stripes = 2
    rows, depth = spread.shape
    width = arrays[0].shape[-1]
    tile = width // stripes
    extra = [] if wait is None else [wait]
    return pl.pallas_call(
        functools.partial(segment_kernel, stripes, len(arrays)),
        in_specs=[VMEM] + [ANY] * (len(arrays) + len(extra)),
        out_specs=VMEM if extra else HBM,
        out_shape=shape((rows, width), F32) if extra else pltpu.HBM((rows, width), BF16),
        scratch_shapes=[
            pltpu.VMEM((stripes, depth, tile), BF16),
            pltpu.VMEM((stripes, rows, tile), BF16),
            pltpu.SemaphoreType.DMA((stripes, len(arrays))),
            pltpu.SemaphoreType.DMA((stripes,)),
        ],
        compiler_params=params(),
        name="segment_rows",
        cost_estimate=cost(BUSY if extra else 1 << 30, 4),
    )(spread, *arrays, *extra)


def candidates(slabs_ref, q, chunk):
    slabs, depth, width = slabs_ref.shape
    part, half = slabs // CHUNKS, depth // 2
    block = slabs_ref[chunk * part : (chunk + 1) * part, q * half : (q + 1) * half, :]
    return block.reshape(part * half, width)


def hits(rows, chunk, target_row):
    row = lax.broadcasted_iota(jnp.int32, (rows, target_row.shape[1]), 0)
    return row + chunk * rows == target_row


def joined(a, b):
    top = jnp.maximum(a[0], b[0])
    return top, a[1] * jnp.exp(a[0] - top) + b[1] * jnp.exp(b[0] - top), a[2] + b[2]


def stat_rows(ref, q):
    return [ref[4 * q + i : 4 * q + i + 1, :] for i in range(3)]


def chunk_rows(ref, chunk):
    rows = ref.shape[1] // CHUNKS
    return slice(chunk * rows, (chunk + 1) * rows)


def place_of(far, planes, ranks, refs, height, chosen):
    owner = chosen // height
    spot = (owner // (planes * ranks) * ranks + owner % ranks) * (refs * height) + chosen % height
    return jnp.where(owner // ranks % planes == lax.axis_index("z") ^ far, spot, -1)


def load(source, held, arrived):
    copy = pltpu.make_async_copy(source, held, arrived)
    copy.start()
    return copy


def part_of(size, chunk):
    return pl.ds(chunk * (size // CHUNKS), size // CHUNKS)


def load_chunks(source, held, arrived):
    parts = [part_of(source.shape[0], c) for c in range(CHUNKS)]
    return [load(source.at[part], held.at[part], arrived.at[c]) for c, part in enumerate(parts)]


def block_logits(block_ref, slab_part, target_row, put):
    stats = None
    for c in range(CHUNKS):
        block = lax.dot_general(slab_part(c), block_ref[...], (((1,), (1,)), ((), ())), preferred_element_type=F32)
        block = SCALE * block
        put(c, block)
        top = jnp.max(block, axis=0, keepdims=True)
        total = jnp.sum(jnp.exp(block - top), axis=0, keepdims=True)
        hit = hits(block.shape[0], c, target_row)
        pick = jnp.sum(jnp.where(hit, block, 0.0), axis=0, keepdims=True)
        here = (top, total, pick)
        stats = here if c == 0 else joined(stats, here)
    return stats


def put_stats(stats_ref, q, stats):
    for i in range(3):
        stats_ref[4 * q + i : 4 * q + i + 1, :] = stats[i]
    stats_ref[4 * q + 3 : 4 * q + 4, :] = jnp.zeros_like(stats[0])


def held_rows(held, chunk):
    slabs = held.shape[0] // CHUNKS
    return held[chunk * slabs : (chunk + 1) * slabs].reshape(slabs * held.shape[1], held.shape[2])


def row_chunk(rows, chunk):
    return slice(chunk * rows // CHUNKS, (chunk + 1) * rows // CHUNKS)


def put_targets(place, target_ref, chosen_ref, chosen_others_ref):
    target_ref[...] = jnp.full(target_ref.shape, -1, jnp.int32)
    target_ref[0:1, :] = place(chosen_ref[...])
    target_ref[1:2, :] = place(chosen_others_ref[...])


def own_kernel(place, queries_ref, slabs_ref, chosen_ref, logits_ref, stats_ref, kept_ref, held, made, arrived, came, left):
    half = slabs_ref.shape[1] // 2
    loads = load_chunks(slabs_ref.at[:, pl.ds(0, half)], held, arrived)
    load(queries_ref, kept_ref, came).wait()
    stores = []

    def slab_part(c):
        loads[c].wait()
        return held_rows(held, c)

    def put(c, block):
        part = part_of(logits_ref.shape[0], c)
        made[row_chunk(made.shape[0], c), :] = block
        stores.append(load(made.at[part], logits_ref.at[part], left.at[c]))

    stats = block_logits(kept_ref, slab_part, place(chosen_ref[...]), put)
    put_stats(stats_ref, 0, stats)
    put_stats(stats_ref, 1, stats)
    for store in stores:
        store.wait()


def own_half(queries, slabs, chosen, place):
    size, width = queries.shape
    rows = slabs.shape[0] * slabs.shape[1] // 2
    return pl.pallas_call(
        functools.partial(own_kernel, place),
        in_specs=[HBM, HBM, VMEM],
        out_specs=[HBM, VMEM, VMEM],
        out_shape=[pltpu.HBM((rows, size), F32), shape((8, size), F32), shape((size, width), BF16)],
        scratch_shapes=[
            pltpu.VMEM((slabs.shape[0], slabs.shape[1] // 2, width), BF16),
            pltpu.VMEM((rows, size), F32),
            pltpu.SemaphoreType.DMA((CHUNKS,)),
            pltpu.SemaphoreType.DMA,
            pltpu.SemaphoreType.DMA((CHUNKS,)),
        ],
        compiler_params=params(),
        name="own_half",
        cost_estimate=cost(BUSY, 4),
    )(queries, slabs, chosen)


def rest_kernel(
    near_place, far_place, queries_ref, inner_ref, outer_ref, near_ref, far_ref, chosen_ref, chosen_others_ref, own_stats_ref,
    other_logits_ref, saved_ref, far_logits_ref, stats_ref, near_target_ref, far_target_ref, others_ref, near_rows, far_rows,
    held, near_in, far_in, held_in, left, came,
):
    half = near_ref.shape[1] // 2
    held_loads = load_chunks(far_ref.at[:, pl.ds(0, half)], held, held_in)
    z = lax.axis_index("z")
    inner = (z > 0) & (z < lax.axis_size("z") - 1)

    @pl.when(inner)
    def _():
        load(inner_ref, others_ref, came)

    @pl.when(jnp.logical_not(inner))
    def _():
        load(outer_ref, others_ref, came)

    whole = [pltpu.make_async_copy(outer_ref, others_ref, came)]
    near_loads = load_chunks(near_ref.at[:, pl.ds(half, half)], near_rows, near_in)
    far_loads = load_chunks(far_ref.at[:, pl.ds(half, half)], far_rows, far_in)
    put_targets(near_place, near_target_ref, chosen_ref, chosen_others_ref)
    put_targets(far_place, far_target_ref, chosen_ref, chosen_others_ref)
    stores = []

    def part(loads, rows):
        def get(c):
            loads[c].wait()
            return held_rows(rows, c)

        return get

    def put_near(c, block):
        rows = part_of(other_logits_ref.shape[0], c)
        other_logits_ref[row_chunk(other_logits_ref.shape[0], c), :] = block
        stores.append(load(other_logits_ref.at[rows], saved_ref.at[rows], left.at[c]))

    def put_far(q):
        def put(c, block):
            far_logits_ref[q, chunk_rows(far_logits_ref, c), :] = block

        return put

    own = block_logits(queries_ref, part(held_loads, held), far_target_ref[0:1, :], put_far(0))
    put_stats(stats_ref, 0, joined(stat_rows(own_stats_ref, 0), own))
    for copy in whole:
        copy.wait()
    near = block_logits(others_ref, part(near_loads, near_rows), near_target_ref[1:2, :], put_near)
    far = block_logits(others_ref, part(far_loads, far_rows), far_target_ref[1:2, :], put_far(1))
    put_stats(stats_ref, 1, joined(near, far))
    for store in stores:
        store.wait()


def rest_half(queries, inner, outer, near_slabs, far_slabs, chosen, chosen_others, own_stats, places):
    size, width = queries.shape
    rows = near_slabs.shape[0] * near_slabs.shape[1] // 2
    part = (near_slabs.shape[0], near_slabs.shape[1] // 2, width)
    chunk_sems = pltpu.SemaphoreType.DMA((CHUNKS,))
    return pl.pallas_call(
        functools.partial(rest_kernel, *places),
        in_specs=[VMEM] + [ANY] * 2 + [HBM] * 2 + [VMEM] * 3,
        out_specs=[VMEM, HBM] + [VMEM] * 7,
        out_shape=[
            shape((rows, size), F32),
            pltpu.HBM((rows, size), F32),
            shape((2, rows, size), F32),
            shape((8, size), F32),
            shape((8, size), jnp.int32),
            shape((8, size), jnp.int32),
            shape((size, width), BF16),
            shape(part, BF16),
            shape(part, BF16),
        ],
        scratch_shapes=[pltpu.VMEM(part, BF16)] + [chunk_sems] * 4 + [pltpu.SemaphoreType.DMA],
        compiler_params=params(),
        name="rest_half",
        cost_estimate=cost(3 << 29, 8),
    )(queries, inner, outer, near_slabs, far_slabs, chosen, chosen_others, own_stats)


def log_totals(here_ref, there_ref):
    out = []
    for q in range(2):
        top, total, pick = joined(stat_rows(here_ref, q), stat_rows(there_ref, 1 - q))
        out.append((top + jnp.log(total), pick))
    return out


def dlogits(logits, log_total, chunk, target_row):
    hit = hits(logits.shape[0], chunk, target_row)
    return (jnp.exp(logits - log_total) - jnp.where(hit, 1.0, 0.0)).astype(BF16)


def send_contrib(made, out_ref, left, chunk, q, piece, block, complete):
    slabs, depth, width = out_ref.shape
    part, half = slabs // CHUNKS, depth // 2
    product = SCALE * jnp.dot(piece, block, preferred_element_type=F32)
    made[chunk, :, q * half : (q + 1) * half, :] = product.astype(BF16).reshape(part, half, width)
    if not complete:
        return []
    store = pltpu.make_async_copy(made.at[chunk], out_ref.at[pl.ds(chunk * part, part)], left.at[chunk])
    store.start()
    return [store]


def contrib_scratch(slabs):
    return [
        pltpu.VMEM((CHUNKS, slabs.shape[0] // CHUNKS) + slabs.shape[1:], BF16),
        pltpu.SemaphoreType.DMA((CHUNKS,)),
    ]


def load_share(q, logits_ref, near_ref, far_ref, logits, near, far, came):
    rows, slabs, half = logits_ref.shape[0], near_ref.shape[0], near_ref.shape[1] // 2
    picks = pl.ds(q * half, half)
    copies = []
    for c in range(CHUNKS):
        part, some = part_of(rows, c), part_of(slabs, c)
        copies.append(
            [
                load(far_ref.at[some, picks], far.at[some], came.at[0, c]),
                load(logits_ref.at[part], logits.at[part], came.at[1, c]),
                load(near_ref.at[some, picks], near.at[some], came.at[2, c]),
            ]
        )
    return copies


def query_share(copies, far_piece, near_piece, near, far, use):
    dims = (((0,), (0,)), ((), ()))
    slabs, half, width = near.shape
    total = None
    for c in range(CHUNKS):
        some = slice(c * slabs // CHUNKS, (c + 1) * slabs // CHUNKS)
        rows = slabs // CHUNKS * half
        piece = far_piece(c)
        copies[c][0].wait()
        share = lax.dot_general(piece, far[some].reshape(rows, width), dims, preferred_element_type=F32)
        copies[c][1].wait()
        piece = near_piece(c)
        copies[c][2].wait()
        share += lax.dot_general(piece, near[some].reshape(rows, width), dims, preferred_element_type=F32)
        total = share if c == 0 else total + share
        if use is not None:
            use(c, piece)
    return total


def share_scratch(logits, slabs):
    part = (slabs.shape[0], slabs.shape[1] // 2, slabs.shape[2])
    return [
        pltpu.VMEM(logits.shape, F32),
        pltpu.VMEM(part, BF16),
        pltpu.VMEM(part, BF16),
        pltpu.SemaphoreType.DMA((3, CHUNKS)),
    ]


def early_kernel(stats_ref, near_target_ref, far_target_ref, near_logits_ref, far_logits_ref, near_ref, far_ref, sums_ref, hit_ref):
    dims = (((0,), (0,)), ((), ()))
    top = stats_ref[4:5, :]
    rows = near_logits_ref.shape[0]
    for c in range(CHUNKS):
        part = row_chunk(rows, c)
        for i, (score, target_ref, slab_ref) in enumerate(
            ((near_logits_ref[part, :], near_target_ref, near_ref), (far_logits_ref[1, part, :], far_target_ref, far_ref))
        ):
            block = held_rows(slab_ref, c)
            weight = jnp.exp(score - top).astype(BF16)
            hit = jnp.where(hits(score.shape[0], c, target_ref[1:2, :]), 1.0, 0.0).astype(BF16)
            product = lax.dot_general(weight, block, dims, preferred_element_type=F32)
            picked = lax.dot_general(hit, block, dims, preferred_element_type=F32)
            if c == 0 and i == 0:
                sums_ref[...] = product
                hit_ref[...] = picked
            else:
                sums_ref[...] += product
                hit_ref[...] += picked


def early_grads(stats, near_target, far_target, near_logits, far_logits, near_rows, far_rows):
    size, width = near_logits.shape[1], near_rows.shape[2]
    return pl.pallas_call(
        early_kernel,
        in_specs=[VMEM] * 7,
        out_specs=[VMEM] * 2,
        out_shape=[shape((size, width), F32)] * 2,
        compiler_params=params(),
        name="early_grads",
        cost_estimate=cost(BUSY, 4),
    )(stats, near_target, far_target, near_logits, far_logits, near_rows, far_rows)


def other_kernel(here_ref, totals_ref, near_target_ref, far_target_ref, sums_ref, hit_ref, wait_ref, other_ref, made, left):
    del wait_ref
    total = totals_ref[1:2, :]
    top, _, pick = stat_rows(here_ref, 1)
    held = jnp.maximum(near_target_ref[1:2, :], far_target_ref[1:2, :]) >= 0
    scale = jnp.exp(top - total)
    counted = scale * jnp.exp(jnp.where(held, pick - top, 0.0)).astype(BF16).astype(F32)
    wanted = (jnp.exp(jnp.where(held, pick - total, 0.0)) - 1.0).astype(BF16).astype(F32)
    rows = [scale, jnp.where(held, wanted - counted, 0.0)]
    columns = jnp.transpose(jnp.concatenate(rows + [jnp.zeros_like(scale)] * 6, axis=0))
    stores = []
    size = made.shape[0] // 4
    for c in range(4):
        part = slice(c * size, (c + 1) * size)
        share = columns[part, 0:1] * sums_ref[part, :] + columns[part, 1:2] * hit_ref[part, :]
        made[part, :] = (SCALE * share).astype(BF16)
        some = pl.ds(c * size, size)
        stores.append(load(made.at[some], other_ref.at[some], left.at[c]))
    for store in stores:
        store.wait()


def other_grads(here, totals, near_target, far_target, sums, hit, wait):
    size, width = sums.shape
    return pl.pallas_call(
        other_kernel,
        in_specs=[VMEM] * 6 + [HBM],
        out_specs=HBM,
        out_shape=pltpu.HBM((size, width), BF16),
        scratch_shapes=[pltpu.VMEM((size, width), BF16), pltpu.SemaphoreType.DMA((4,))],
        compiler_params=params(),
        name="other_grads",
        cost_estimate=cost(1 << 20, 4),
    )(here, totals, near_target, far_target, sums, hit, wait)


def far_kernel(
    queries_ref, others_ref, logits_ref, target_ref, here_ref, there_ref, wait_ref,
    contrib_ref, pieces_ref, totals_ref, loss_ref, made, left, pieces, pieces_out,
):
    del wait_ref
    totals = log_totals(here_ref, there_ref)
    totals_ref[...] = jnp.zeros_like(totals_ref)
    for q in range(2):
        totals_ref[q : q + 1, :] = totals[q][0]
    loss_ref[...] = totals[0][0] - totals[0][1]
    slabs, depth, width = contrib_ref.shape
    half = depth // 2
    stores = []
    for q, block_ref in enumerate((queries_ref, others_ref)):
        piece = dlogits(logits_ref[q], totals[q][0], 0, target_ref[q : q + 1, :])
        if q == 0:
            pieces[...] = piece
            stores.append(load(pieces, pieces_ref, pieces_out))
        product = SCALE * jnp.dot(piece, block_ref[...], preferred_element_type=F32)
        made[q] = product.astype(BF16).reshape(slabs, half, width)
        stores.append(load(made.at[q], contrib_ref.at[:, pl.ds(q * half, half)], left.at[q]))
    for store in stores:
        store.wait()


def far_grads(queries, others, logits, target, here, there, wait, slabs):
    size = queries.shape[0]
    rows = logits.shape[1]
    count, depth, width = slabs.shape
    return pl.pallas_call(
        far_kernel,
        in_specs=[VMEM] * 7,
        out_specs=[HBM] * 2 + [VMEM] * 2,
        out_shape=[
            pltpu.HBM(slabs.shape, BF16),
            pltpu.HBM((rows, size), BF16),
            shape((8, size), F32),
            shape((1, size), F32),
        ],
        scratch_shapes=[
            pltpu.VMEM((2, count, depth // 2, width), BF16),
            pltpu.SemaphoreType.DMA((2,)),
            pltpu.VMEM((rows, size), BF16),
            pltpu.SemaphoreType.DMA,
        ],
        compiler_params=params(),
        name="far_grads",
        cost_estimate=cost(1 << 30, 4),
    )(queries, others, logits, target, here, there, wait)


def near_kernel(
    ranks, queries_ref, others_ref, target_ref, totals_ref, own_logits_ref, other_logits_ref, pieces_ref, near_ref, far_ref,
    kept_ref, *refs,
):
    *given_refs, own_ref, logits, near, far, came, pieces, begun, score, scored, own, own_out, made, left = refs
    first = load(pieces_ref, pieces, begun)
    copies = load_share(0, own_logits_ref, near_ref, far_ref, logits, near, far, came)
    other_scores = load(other_logits_ref, score, scored)
    slabs, depth, width = made.shape
    half = depth // 2

    def store_part(q, piece, block_ref):
        product = SCALE * jnp.dot(piece, block_ref[...], preferred_element_type=F32)
        made[:, q * half : (q + 1) * half, :] = product.astype(BF16).reshape(slabs, half, width)

    other_scores.wait()
    store_part(1, dlogits(score[...], totals_ref[1:2, :], 0, target_ref[1:2, :]), others_ref)
    first.wait()

    def far_piece(c):
        return pieces[row_chunk(logits.shape[0], c), :]

    def near_piece(c):
        return dlogits(logits[row_chunk(logits.shape[0], c), :], totals_ref[0:1, :], c, target_ref[0:1, :])

    def use(c, piece):
        store_part(0, piece, queries_ref)

    total = query_share(copies, far_piece, near_piece, near, far, use)
    place = plane_place(ranks)
    stores = []
    for s in range(slabs):
        out_ref = given_refs[s // 2] if s % 2 else kept_ref.at[s // 2]
        stores.append(load(made.at[place ^ s], out_ref, left.at[s]))
    own[...] = SCALE * total
    stores.append(load(own, own_ref, own_out))
    for store in stores:
        store.wait()


def near_grads(queries, others, target, totals, own_logits, other_logits, pieces, near_slabs, far_slabs, ranks):
    slabs, depth, width = near_slabs.shape
    kept = pltpu.HBM((slabs // 2, depth, width), BF16)
    given = [pltpu.HBM((depth, width), BF16)] * (slabs // 2)
    return pl.pallas_call(
        functools.partial(near_kernel, ranks),
        in_specs=[VMEM] * 4 + [HBM] * 5,
        out_specs=[HBM] * (2 + slabs // 2),
        out_shape=[kept, *given, pltpu.HBM(queries.shape, F32)],
        scratch_shapes=share_scratch(own_logits, near_slabs)
        + [pltpu.VMEM(pieces.shape, BF16), pltpu.SemaphoreType.DMA]
        + [pltpu.VMEM(own_logits.shape, F32), pltpu.SemaphoreType.DMA]
        + [pltpu.VMEM(queries.shape, F32), pltpu.SemaphoreType.DMA]
        + [pltpu.VMEM(near_slabs.shape, BF16), pltpu.SemaphoreType.DMA((slabs,))],
        compiler_params=params(),
        name="near_grads",
        cost_estimate=cost(2 << 30, 8),
    )(queries, others, target, totals, own_logits, other_logits, pieces, near_slabs, far_slabs)


def add_kernel(own_ref, part_ref, *refs):
    out_ref, own, part, made, own_in, part_in, left = refs[-7:]
    pieces = [pl.ds(i * (part.shape[0] // 4), part.shape[0] // 4) for i in range(4)]
    halves = [load(part_ref.at[p], part.at[p], part_in.at[i]) for i, p in enumerate(pieces)]
    if own.shape == part.shape:
        sums = [load(own_ref.at[p], own.at[p], own_in.at[i]) for i, p in enumerate(pieces)]
        own_ref = own
    stores = []
    for i, p in enumerate(pieces):
        halves[i].wait()
        if own_ref is own:
            sums[i].wait()
        rows = slice(p.start, p.start + p.size)
        made[rows, :] = (own_ref[rows, :] + part[rows, :].astype(F32)).astype(BF16)
        stores.append(load(made.at[p], out_ref.at[p], left.at[i]))
    for store in stores:
        store.wait()


def add_parts(own, part, hint, *waits):
    sems = pltpu.SemaphoreType.DMA((4,))
    return pl.pallas_call(
        add_kernel,
        in_specs=[HBM if waits else VMEM, ANY] + [ANY] * len(waits),
        out_specs=HBM,
        out_shape=pltpu.HBM(own.shape, BF16),
        scratch_shapes=[
            pltpu.VMEM(own.shape if waits else (8, 128), F32),
            pltpu.VMEM(own.shape, BF16),
            pltpu.VMEM(own.shape, BF16),
        ]
        + [sems] * 3,
        compiler_params=params(),
        name="add_parts",
        cost_estimate=cost(hint, 4),
    )(in_hbm(own) if waits else own, part, *waits)


def on_device(queries, passages, block_ids, positives):
    height, blocks, width = passages.shape
    refs = block_ids.shape[1]
    groups, planes, ranks = lax.axis_size("group"), lax.axis_size("z"), lax.axis_size("rank")
    slabs = groups * ranks
    z = lax.axis_index("z")
    to_pair = [(i, i ^ 1) for i in range(planes)]
    across = [(i, planes - 1 - i) for i in range(planes)]

    def exchange(slab_array):
        return lax.all_to_all(slab_array, PLANE, split_axis=0, concat_axis=0, tiled=True)

    ids = block_ids.T
    own_rows = jnp.transpose(passages, (1, 0, 2))
    near_slabs = in_hbm(exchange(gather_rows(ids, own_rows, slabs, planes, ranks, 0)))
    pair_rows = lax.ppermute(passages.reshape(height * blocks, width), "z", to_pair)
    inner = [pair for pair in across if 0 < pair[0] < planes - 1]
    outer = [pair for pair in across if pair not in inner]
    others_inner = lax.ppermute(queries, "z", inner)
    others_positives = lax.ppermute(positives, "z", across).reshape(1, -1)

    table = block_ids.reshape(groups, planes, ranks, refs)
    both = jnp.stack([jnp.take(table, z, axis=1), jnp.take(table, planes - 1 - z, axis=1)], axis=2)
    place = (jnp.arange(height, dtype=jnp.int32) * blocks + both.reshape(-1, 1)).reshape(1, -1)
    spread = (jnp.arange(height * blocks, dtype=jnp.int32)[:, None] == place).astype(BF16)
    by_shift = jnp.take(both.reshape(slabs, -1), plane_place(ranks) ^ jnp.arange(slabs), axis=0)
    near_place = (jnp.arange(height, dtype=jnp.int32) * blocks + by_shift.reshape(-1, 1)).reshape(1, -1)
    near_spread = (jnp.arange(height * blocks, dtype=jnp.int32)[:, None] == near_place).astype(BF16)
    far_sent = select_rows(spread, pair_rows, slabs)
    others_outer = lax.ppermute(after(copy_rows(in_hbm(queries)), in_hbm(far_sent), where=HBM), "z", outer)
    far_slabs = in_hbm(exchange(far_sent))

    chosen = positives.reshape(1, -1)
    chosen_others = others_positives
    places = [functools.partial(place_of, far, planes, ranks, refs, height) for far in range(2)]
    own_logits, own_stats, own = own_half(in_hbm(queries), near_slabs, chosen, places[0])
    other_logits, saved_logits, far_logits, stats, near_target, far_target, others, near_rows, far_rows = rest_half(
        own, others_inner, others_outer, near_slabs, far_slabs, chosen, chosen_others, own_stats, places
    )
    partner = lax.ppermute(stats, "z", across)
    sums, hit = early_grads(stats, near_target, far_target, other_logits, far_logits, near_rows, far_rows)
    own_logits, other_logits = in_hbm(own_logits), in_hbm(saved_logits)
    far_contrib, pieces, totals, loss = far_grads(
        own, others, far_logits, far_target, stats, partner, hit, far_slabs
    )
    pieces = in_hbm(pieces)
    other_part = other_grads(stats, totals, near_target, far_target, sums, hit, pieces)
    far_back = in_hbm(exchange(far_contrib).reshape(-1, width))
    kept, *given, own_grad = near_grads(
        own, others, near_target, totals, own_logits, other_logits, pieces, near_slabs, far_slabs, ranks
    )
    joined = join_cores(kept, [lax.ppermute(array, PLANE, [(i, i ^ 1) for i in range(slabs)]) for array in given])
    own_part = lax.ppermute(other_part, "z", across)
    far_sum = segment_rows(spread, [far_back])
    pair_sum = lax.ppermute(far_sum, "z", to_pair)
    near_back = [
        lax.ppermute(array, PLANE, [(i, i ^ (2 * g)) for i in range(slabs)]) if g else array
        for g, array in enumerate(joined)
    ]
    query_grad = add_parts(own_grad, own_part, BUSY, in_hbm(far_sum))
    near_sum = segment_rows(near_spread, near_back, in_hbm(query_grad))
    row_sum = add_parts(near_sum, pair_sum, 1 << 20)
    return loss.reshape(-1), query_grad, row_sum.reshape(passages.shape)


def solution(mesh):
    groups, members = mesh.devices.shape
    split = Mesh(mesh.devices.reshape(groups, PLANES, members // PLANES), ("group", "z", "rank"))
    rows = ("group", "z", "rank")
    return jax.shard_map(
        on_device,
        mesh=split,
        in_specs=(P(rows, None), P(rows, None, None), P(), P(rows)),
        out_specs=(P(rows), P(rows, None), P(rows, None, None)),
        check_vma=False,
    )
```

```python
import functools

import jax
import jax.numpy as jnp
from jax import lax
from jax.experimental import pallas as pl
from jax.experimental.pallas import tpu as pltpu
from jax.sharding import Mesh
from jax.sharding import PartitionSpec as P

SCALE = 0.8
PLANES = 4
CHUNKS = 1
BF16 = jnp.bfloat16
F32 = jnp.float32
BUSY = 1 << 37
PLANE = ("group", "rank")
ANY = pl.BlockSpec(memory_space=pl.ANY)
HBM = pl.BlockSpec(memory_space=pltpu.HBM)
VMEM = pl.BlockSpec(memory_space=pltpu.VMEM)
SMEM = pl.BlockSpec(memory_space=pltpu.SMEM)


def params():
    return pltpu.CompilerParams(vmem_limit_bytes=28 << 20)


def cost(flops, mib):
    return pl.CostEstimate(flops=flops, bytes_accessed=mib << 20, transcendentals=0)


def in_hbm(array):
    return pltpu.with_memory_space_constraint(array, pltpu.HBM)


def shape(dims, dtype):
    return jax.ShapeDtypeStruct(dims, dtype)


def after_kernel(*refs):
    del refs


def after(array, *others, where=VMEM):
    return pl.pallas_call(
        after_kernel,
        in_specs=[ANY] + [where] * len(others),
        out_specs=ANY,
        out_shape=shape(array.shape, array.dtype),
        input_output_aliases={0: 0},
        name="after",
    )(array, *others)


def copy_kernel(source_ref, out_ref, held, done):
    pieces = [pl.ds(i * (held.shape[0] // 4), held.shape[0] // 4) for i in range(4)]
    loads = [load(source_ref.at[p], held.at[p], done.at[0, i]) for i, p in enumerate(pieces)]
    stores = []
    for i, p in enumerate(pieces):
        loads[i].wait()
        stores.append(load(held.at[p], out_ref.at[p], done.at[1, i]))
    for store in stores:
        store.wait()


def copy_rows(array):
    return pl.pallas_call(
        copy_kernel,
        in_specs=[HBM],
        out_specs=HBM,
        out_shape=pltpu.HBM(array.shape, BF16),
        scratch_shapes=[pltpu.VMEM(array.shape, BF16), pltpu.SemaphoreType.DMA((2, 4))],
        compiler_params=params(),
        name="copy_rows",
        cost_estimate=cost(0, 2),
    )(array)


def gather_kernel(planes, ranks, ids, rows_ref, out_ref, made, left):
    slabs, depth, width = out_ref.shape
    height = rows_ref.shape[1]
    refs = ids.shape[0]
    z = lax.axis_index("z")

    def sent(slab):
        return pltpu.make_async_copy(made.at[slab], out_ref.at[slab], left.at[slab])

    def fill(slab, carry):
        for pick in range(2 * refs):
            there = z if pick < refs else planes - 1 - z
            owner = (slab // ranks * planes + there) * ranks + slab % ranks
            made[slab, pick * height : (pick + 1) * height, :] = rows_ref[ids[pick % refs, owner]]
        sent(slab).start()
        return carry

    def drain(slab, carry):
        sent(slab).wait()
        return carry

    lax.fori_loop(0, slabs, fill, 0)
    lax.fori_loop(0, slabs, drain, 0)


def gather_rows(ids, rows, slabs, planes, ranks, flops):
    blocks, height, width = rows.shape
    dims = (slabs, 2 * ids.shape[0] * height, width)
    return pl.pallas_call(
        functools.partial(gather_kernel, planes, ranks),
        in_specs=[SMEM, VMEM],
        out_specs=HBM,
        out_shape=pltpu.HBM(dims, BF16),
        scratch_shapes=[pltpu.VMEM(dims, BF16), pltpu.SemaphoreType.DMA((slabs,))],
        compiler_params=params(),
        name="gather_rows",
        cost_estimate=cost(flops, 4),
    )(ids, rows)


def select_kernel(spread_ref, rows_ref, out_ref, made, left):
    slabs, depth, width = out_ref.shape
    part = slabs // 2
    stores = []
    for c in range(2):
        some = slice(c * part, (c + 1) * part)
        lanes = slice(c * part * depth, (c + 1) * part * depth)
        product = lax.dot_general(
            spread_ref[:, lanes], rows_ref[...], (((0,), (0,)), ((), ())), preferred_element_type=F32
        )
        made[some] = product.astype(BF16).reshape(part, depth, width)
        some = pl.ds(c * part, part)
        stores.append(load(made.at[some], out_ref.at[some], left.at[c]))
    for store in stores:
        store.wait()


def select_rows(spread, rows, slabs):
    dims = (slabs, spread.shape[1] // slabs, rows.shape[1])
    return pl.pallas_call(
        select_kernel,
        in_specs=[VMEM, VMEM],
        out_specs=HBM,
        out_shape=pltpu.HBM(dims, BF16),
        scratch_shapes=[pltpu.VMEM(dims, BF16), pltpu.SemaphoreType.DMA((2,))],
        compiler_params=params(),
        name="select_rows",
        cost_estimate=cost(BUSY, 4),
    )(spread, rows)


def plane_place(ranks):
    return lax.axis_index("group") * ranks + lax.axis_index("rank")


def join_kernel(kept_ref, *refs):
    chips, depth, _ = kept_ref.shape
    given_refs = refs[:chips]
    *out_refs, held, arrived, left = refs[chips:]
    for g in range(chips):
        load(kept_ref.at[g], held.at[g, pl.ds(0, depth)], arrived.at[g, 0])
        load(given_refs[g], held.at[g, pl.ds(depth, depth)], arrived.at[g, 1])
    for g in range(chips):
        pltpu.make_async_copy(kept_ref.at[g], held.at[g, pl.ds(0, depth)], arrived.at[g, 0]).wait()
        pltpu.make_async_copy(given_refs[g], held.at[g, pl.ds(depth, depth)], arrived.at[g, 1]).wait()
        load(held.at[g], out_refs[g], left.at[g])
    for g in range(chips):
        pltpu.make_async_copy(held.at[g], out_refs[g], left.at[g]).wait()


def join_cores(kept, given):
    chips, depth, width = kept.shape
    return pl.pallas_call(
        join_kernel,
        in_specs=[HBM] + [ANY] * chips,
        out_specs=[HBM] * chips,
        out_shape=[pltpu.HBM((2 * depth, width), BF16)] * chips,
        scratch_shapes=[
            pltpu.VMEM((chips, 2 * depth, width), BF16),
            pltpu.SemaphoreType.DMA((chips, 2)),
            pltpu.SemaphoreType.DMA((chips,)),
        ],
        compiler_params=params(),
        name="join_cores",
        cost_estimate=cost(1 << 20, 4),
    )(kept, *given)


def segment_kernel(stripes, arrays, spread_ref, *refs):
    slab_refs = refs[:arrays]
    out_ref, held, result, arrived, left = refs[-5:]
    tile = out_ref.shape[1] // stripes
    depth = held.shape[1] // arrays
    columns = [pl.ds(t * tile, tile) for t in range(stripes)]
    loads = [
        Several(
            [
                load(ref.at[:, columns[t]], held.at[t, pl.ds(i * depth, depth)], arrived.at[t, i])
                for i, ref in enumerate(slab_refs)
            ]
        )
        for t in range(stripes)
    ]
    stores = []
    for t in range(stripes):
        loads[t].wait()
        total = jnp.dot(spread_ref[...], held[t], preferred_element_type=F32)
        if out_ref.dtype == F32:
            out_ref[:, t * tile : (t + 1) * tile] = total
        else:
            result[t] = total.astype(BF16)
            stores.append(load(result.at[t], out_ref.at[:, columns[t]], left.at[t]))
    for store in stores:
        store.wait()


class Several:
    def __init__(self, copies):
        self.copies = copies

    def wait(self):
        for copy in self.copies:
            copy.wait()


def segment_rows(spread, arrays, wait=None):
    stripes = 2
    rows, depth = spread.shape
    width = arrays[0].shape[-1]
    tile = width // stripes
    extra = [] if wait is None else [wait]
    return pl.pallas_call(
        functools.partial(segment_kernel, stripes, len(arrays)),
        in_specs=[VMEM] + [ANY] * (len(arrays) + len(extra)),
        out_specs=VMEM if extra else HBM,
        out_shape=shape((rows, width), F32) if extra else pltpu.HBM((rows, width), BF16),
        scratch_shapes=[
            pltpu.VMEM((stripes, depth, tile), BF16),
            pltpu.VMEM((stripes, rows, tile), BF16),
            pltpu.SemaphoreType.DMA((stripes, len(arrays))),
            pltpu.SemaphoreType.DMA((stripes,)),
        ],
        compiler_params=params(),
        name="segment_rows",
        cost_estimate=cost(BUSY if extra else 1 << 30, 4),
    )(spread, *arrays, *extra)


def candidates(slabs_ref, q, chunk):
    slabs, depth, width = slabs_ref.shape
    part, half = slabs // CHUNKS, depth // 2
    block = slabs_ref[chunk * part : (chunk + 1) * part, q * half : (q + 1) * half, :]
    return block.reshape(part * half, width)


def hits(rows, chunk, target_row):
    row = lax.broadcasted_iota(jnp.int32, (rows, target_row.shape[1]), 0)
    return row + chunk * rows == target_row


def joined(a, b):
    top = jnp.maximum(a[0], b[0])
    return top, a[1] * jnp.exp(a[0] - top) + b[1] * jnp.exp(b[0] - top), a[2] + b[2]


def stat_rows(ref, q):
    return [ref[4 * q + i : 4 * q + i + 1, :] for i in range(3)]


def chunk_rows(ref, chunk):
    rows = ref.shape[1] // CHUNKS
    return slice(chunk * rows, (chunk + 1) * rows)


def place_of(far, planes, ranks, refs, height, chosen):
    owner = chosen // height
    spot = (owner // (planes * ranks) * ranks + owner % ranks) * (refs * height) + chosen % height
    return jnp.where(owner // ranks % planes == lax.axis_index("z") ^ far, spot, -1)


def load(source, held, arrived):
    copy = pltpu.make_async_copy(source, held, arrived)
    copy.start()
    return copy


def part_of(size, chunk):
    return pl.ds(chunk * (size // CHUNKS), size // CHUNKS)


def load_chunks(source, held, arrived):
    parts = [part_of(source.shape[0], c) for c in range(CHUNKS)]
    return [load(source.at[part], held.at[part], arrived.at[c]) for c, part in enumerate(parts)]


def block_logits(block_ref, slab_part, target_row, put):
    stats = None
    for c in range(CHUNKS):
        block = lax.dot_general(slab_part(c), block_ref[...], (((1,), (1,)), ((), ())), preferred_element_type=F32)
        block = SCALE * block
        put(c, block)
        top = jnp.max(block, axis=0, keepdims=True)
        total = jnp.sum(jnp.exp(block - top), axis=0, keepdims=True)
        hit = hits(block.shape[0], c, target_row)
        pick = jnp.sum(jnp.where(hit, block, 0.0), axis=0, keepdims=True)
        here = (top, total, pick)
        stats = here if c == 0 else joined(stats, here)
    return stats


def put_stats(stats_ref, q, stats):
    for i in range(3):
        stats_ref[4 * q + i : 4 * q + i + 1, :] = stats[i]
    stats_ref[4 * q + 3 : 4 * q + 4, :] = jnp.zeros_like(stats[0])


def held_rows(held, chunk):
    slabs = held.shape[0] // CHUNKS
    return held[chunk * slabs : (chunk + 1) * slabs].reshape(slabs * held.shape[1], held.shape[2])


def row_chunk(rows, chunk):
    return slice(chunk * rows // CHUNKS, (chunk + 1) * rows // CHUNKS)


def put_targets(place, target_ref, chosen_ref, chosen_others_ref):
    target_ref[...] = jnp.full(target_ref.shape, -1, jnp.int32)
    target_ref[0:1, :] = place(chosen_ref[...])
    target_ref[1:2, :] = place(chosen_others_ref[...])


def own_kernel(place, queries_ref, slabs_ref, chosen_ref, logits_ref, stats_ref, kept_ref, held, made, arrived, came, left):
    half = slabs_ref.shape[1] // 2
    loads = load_chunks(slabs_ref.at[:, pl.ds(0, half)], held, arrived)
    load(queries_ref, kept_ref, came).wait()
    stores = []

    def slab_part(c):
        loads[c].wait()
        return held_rows(held, c)

    def put(c, block):
        part = part_of(logits_ref.shape[0], c)
        made[row_chunk(made.shape[0], c), :] = block
        stores.append(load(made.at[part], logits_ref.at[part], left.at[c]))

    stats = block_logits(kept_ref, slab_part, place(chosen_ref[...]), put)
    put_stats(stats_ref, 0, stats)
    put_stats(stats_ref, 1, stats)
    for store in stores:
        store.wait()


def own_half(queries, slabs, chosen, place):
    size, width = queries.shape
    rows = slabs.shape[0] * slabs.shape[1] // 2
    return pl.pallas_call(
        functools.partial(own_kernel, place),
        in_specs=[HBM, HBM, VMEM],
        out_specs=[HBM, VMEM, VMEM],
        out_shape=[pltpu.HBM((rows, size), F32), shape((8, size), F32), shape((size, width), BF16)],
        scratch_shapes=[
            pltpu.VMEM((slabs.shape[0], slabs.shape[1] // 2, width), BF16),
            pltpu.VMEM((rows, size), F32),
            pltpu.SemaphoreType.DMA((CHUNKS,)),
            pltpu.SemaphoreType.DMA,
            pltpu.SemaphoreType.DMA((CHUNKS,)),
        ],
        compiler_params=params(),
        name="own_half",
        cost_estimate=cost(BUSY, 4),
    )(queries, slabs, chosen)


def other_half_kernel(
    place, inner_ref, outer_ref, near_ref, chosen_ref,
    logits_ref, saved_ref, stats_ref, others_ref, near_rows, near_in, left, came,
):
    half = near_ref.shape[1] // 2
    z = lax.axis_index("z")
    inner = (z > 0) & (z < lax.axis_size("z") - 1)

    @pl.when(inner)
    def _():
        load(inner_ref, others_ref, came)

    @pl.when(jnp.logical_not(inner))
    def _():
        load(outer_ref, others_ref, came)

    whole = [pltpu.make_async_copy(outer_ref, others_ref, came)]
    near_load = load(near_ref.at[:, pl.ds(half, half)], near_rows, near_in)
    stores = []

    def put(c, block):
        logits_ref[...] = block
        stores.append(load(logits_ref, saved_ref, left))

    for copy in whole:
        copy.wait()
    near_load.wait()
    stats = block_logits(others_ref, lambda c: held_rows(near_rows, c), place(chosen_ref[...]), put)
    put_stats(stats_ref, 0, stats)
    put_stats(stats_ref, 1, stats)
    for store in stores:
        store.wait()


def other_half(inner, outer, near_slabs, chosen, place):
    size, width = inner.shape
    rows = near_slabs.shape[0] * near_slabs.shape[1] // 2
    part = (near_slabs.shape[0], near_slabs.shape[1] // 2, width)
    return pl.pallas_call(
        functools.partial(other_half_kernel, place),
        in_specs=[ANY] * 2 + [HBM, VMEM],
        out_specs=[VMEM, HBM] + [VMEM] * 3,
        out_shape=[
            shape((rows, size), F32),
            pltpu.HBM((rows, size), F32),
            shape((8, size), F32),
            shape((size, width), BF16),
            shape(part, BF16),
        ],
        scratch_shapes=[pltpu.SemaphoreType.DMA] * 3,
        compiler_params=params(),
        name="other_half",
        cost_estimate=cost(BUSY, 8),
    )(inner, outer, near_slabs, chosen)


def rest_kernel(
    near_place, far_place, queries_ref, others_ref, far_ref, chosen_ref, chosen_others_ref, own_stats_ref, other_stats_ref,
    far_logits_ref, stats_ref, near_target_ref, far_target_ref, far_rows, held, far_in, held_in,
):
    half = far_ref.shape[1] // 2
    held_loads = load_chunks(far_ref.at[:, pl.ds(0, half)], held, held_in)
    far_loads = load_chunks(far_ref.at[:, pl.ds(half, half)], far_rows, far_in)
    put_targets(near_place, near_target_ref, chosen_ref, chosen_others_ref)
    put_targets(far_place, far_target_ref, chosen_ref, chosen_others_ref)

    def part(loads, rows):
        def get(c):
            loads[c].wait()
            return held_rows(rows, c)

        return get

    def put_far(q):
        def put(c, block):
            far_logits_ref[q, chunk_rows(far_logits_ref, c), :] = block

        return put

    own = block_logits(queries_ref, part(held_loads, held), far_target_ref[0:1, :], put_far(0))
    put_stats(stats_ref, 0, joined(stat_rows(own_stats_ref, 0), own))
    far = block_logits(others_ref, part(far_loads, far_rows), far_target_ref[1:2, :], put_far(1))
    put_stats(stats_ref, 1, joined(stat_rows(other_stats_ref, 0), far))


def rest_half(queries, others, far_slabs, chosen, chosen_others, own_stats, other_stats, places):
    size, width = queries.shape
    rows = far_slabs.shape[0] * far_slabs.shape[1] // 2
    part = (far_slabs.shape[0], far_slabs.shape[1] // 2, width)
    chunk_sems = pltpu.SemaphoreType.DMA((CHUNKS,))
    return pl.pallas_call(
        functools.partial(rest_kernel, *places),
        in_specs=[VMEM] * 2 + [HBM] + [VMEM] * 4,
        out_specs=[VMEM] * 5,
        out_shape=[
            shape((2, rows, size), F32),
            shape((8, size), F32),
            shape((8, size), jnp.int32),
            shape((8, size), jnp.int32),
            shape(part, BF16),
        ],
        scratch_shapes=[pltpu.VMEM(part, BF16)] + [chunk_sems] * 2,
        compiler_params=params(),
        name="rest_half",
        cost_estimate=cost(3 << 29, 8),
    )(queries, others, far_slabs, chosen, chosen_others, own_stats, other_stats)


def log_totals(here_ref, there_ref):
    out = []
    for q in range(2):
        top, total, pick = joined(stat_rows(here_ref, q), stat_rows(there_ref, 1 - q))
        out.append((top + jnp.log(total), pick))
    return out


def dlogits(logits, log_total, chunk, target_row):
    hit = hits(logits.shape[0], chunk, target_row)
    return (jnp.exp(logits - log_total) - jnp.where(hit, 1.0, 0.0)).astype(BF16)


def send_contrib(made, out_ref, left, chunk, q, piece, block, complete):
    slabs, depth, width = out_ref.shape
    part, half = slabs // CHUNKS, depth // 2
    product = SCALE * jnp.dot(piece, block, preferred_element_type=F32)
    made[chunk, :, q * half : (q + 1) * half, :] = product.astype(BF16).reshape(part, half, width)
    if not complete:
        return []
    store = pltpu.make_async_copy(made.at[chunk], out_ref.at[pl.ds(chunk * part, part)], left.at[chunk])
    store.start()
    return [store]


def contrib_scratch(slabs):
    return [
        pltpu.VMEM((CHUNKS, slabs.shape[0] // CHUNKS) + slabs.shape[1:], BF16),
        pltpu.SemaphoreType.DMA((CHUNKS,)),
    ]


def load_share(q, logits_ref, near_ref, far_ref, logits, near, far, came):
    rows, slabs, half = logits_ref.shape[0], near_ref.shape[0], near_ref.shape[1] // 2
    picks = pl.ds(q * half, half)
    copies = []
    for c in range(CHUNKS):
        part, some = part_of(rows, c), part_of(slabs, c)
        copies.append(
            [
                load(far_ref.at[some, picks], far.at[some], came.at[0, c]),
                load(logits_ref.at[part], logits.at[part], came.at[1, c]),
                load(near_ref.at[some, picks], near.at[some], came.at[2, c]),
            ]
        )
    return copies


def query_share(copies, far_piece, near_piece, near, far, use):
    dims = (((0,), (0,)), ((), ()))
    slabs, half, width = near.shape
    total = None
    for c in range(CHUNKS):
        some = slice(c * slabs // CHUNKS, (c + 1) * slabs // CHUNKS)
        rows = slabs // CHUNKS * half
        piece = far_piece(c)
        copies[c][0].wait()
        share = lax.dot_general(piece, far[some].reshape(rows, width), dims, preferred_element_type=F32)
        copies[c][1].wait()
        piece = near_piece(c)
        copies[c][2].wait()
        share += lax.dot_general(piece, near[some].reshape(rows, width), dims, preferred_element_type=F32)
        total = share if c == 0 else total + share
        if use is not None:
            use(c, piece)
    return total


def share_scratch(logits, slabs):
    part = (slabs.shape[0], slabs.shape[1] // 2, slabs.shape[2])
    return [
        pltpu.VMEM(logits.shape, F32),
        pltpu.VMEM(part, BF16),
        pltpu.VMEM(part, BF16),
        pltpu.SemaphoreType.DMA((3, CHUNKS)),
    ]


def early_kernel(stats_ref, near_target_ref, far_target_ref, near_logits_ref, far_logits_ref, near_ref, far_ref, sums_ref, hit_ref):
    dims = (((0,), (0,)), ((), ()))
    top = stats_ref[4:5, :]
    rows = near_logits_ref.shape[0]
    for c in range(CHUNKS):
        part = row_chunk(rows, c)
        for i, (score, target_ref, slab_ref) in enumerate(
            ((near_logits_ref[part, :], near_target_ref, near_ref), (far_logits_ref[1, part, :], far_target_ref, far_ref))
        ):
            block = held_rows(slab_ref, c)
            weight = jnp.exp(score - top).astype(BF16)
            hit = jnp.where(hits(score.shape[0], c, target_ref[1:2, :]), 1.0, 0.0).astype(BF16)
            product = lax.dot_general(weight, block, dims, preferred_element_type=F32)
            picked = lax.dot_general(hit, block, dims, preferred_element_type=F32)
            if c == 0 and i == 0:
                sums_ref[...] = product
                hit_ref[...] = picked
            else:
                sums_ref[...] += product
                hit_ref[...] += picked


def early_grads(stats, near_target, far_target, near_logits, far_logits, near_rows, far_rows):
    size, width = near_logits.shape[1], near_rows.shape[2]
    return pl.pallas_call(
        early_kernel,
        in_specs=[VMEM] * 7,
        out_specs=[VMEM] * 2,
        out_shape=[shape((size, width), F32)] * 2,
        compiler_params=params(),
        name="early_grads",
        cost_estimate=cost(BUSY, 4),
    )(stats, near_target, far_target, near_logits, far_logits, near_rows, far_rows)


def other_kernel(here_ref, totals_ref, near_target_ref, far_target_ref, sums_ref, hit_ref, wait_ref, other_ref, made, left):
    del wait_ref
    total = totals_ref[1:2, :]
    top, _, pick = stat_rows(here_ref, 1)
    held = jnp.maximum(near_target_ref[1:2, :], far_target_ref[1:2, :]) >= 0
    scale = jnp.exp(top - total)
    counted = scale * jnp.exp(jnp.where(held, pick - top, 0.0)).astype(BF16).astype(F32)
    wanted = (jnp.exp(jnp.where(held, pick - total, 0.0)) - 1.0).astype(BF16).astype(F32)
    rows = [scale, jnp.where(held, wanted - counted, 0.0)]
    columns = jnp.transpose(jnp.concatenate(rows + [jnp.zeros_like(scale)] * 6, axis=0))
    stores = []
    size = made.shape[0] // 4
    for c in range(4):
        part = slice(c * size, (c + 1) * size)
        share = columns[part, 0:1] * sums_ref[part, :] + columns[part, 1:2] * hit_ref[part, :]
        made[part, :] = (SCALE * share).astype(BF16)
        some = pl.ds(c * size, size)
        stores.append(load(made.at[some], other_ref.at[some], left.at[c]))
    for store in stores:
        store.wait()


def other_grads(here, totals, near_target, far_target, sums, hit, wait):
    size, width = sums.shape
    return pl.pallas_call(
        other_kernel,
        in_specs=[VMEM] * 6 + [HBM],
        out_specs=HBM,
        out_shape=pltpu.HBM((size, width), BF16),
        scratch_shapes=[pltpu.VMEM((size, width), BF16), pltpu.SemaphoreType.DMA((4,))],
        compiler_params=params(),
        name="other_grads",
        cost_estimate=cost(1 << 20, 4),
    )(here, totals, near_target, far_target, sums, hit, wait)


def far_kernel(
    queries_ref, others_ref, logits_ref, target_ref, here_ref, there_ref, wait_ref,
    contrib_ref, pieces_ref, totals_ref, loss_ref, made, left, pieces, pieces_out,
):
    del wait_ref
    totals = log_totals(here_ref, there_ref)
    totals_ref[...] = jnp.zeros_like(totals_ref)
    for q in range(2):
        totals_ref[q : q + 1, :] = totals[q][0]
    loss_ref[...] = totals[0][0] - totals[0][1]
    slabs, depth, width = contrib_ref.shape
    half = depth // 2
    stores = []
    for q, block_ref in enumerate((queries_ref, others_ref)):
        piece = dlogits(logits_ref[q], totals[q][0], 0, target_ref[q : q + 1, :])
        if q == 0:
            pieces[...] = piece
            stores.append(load(pieces, pieces_ref, pieces_out))
        product = SCALE * jnp.dot(piece, block_ref[...], preferred_element_type=F32)
        made[q] = product.astype(BF16).reshape(slabs, half, width)
        stores.append(load(made.at[q], contrib_ref.at[:, pl.ds(q * half, half)], left.at[q]))
    for store in stores:
        store.wait()


def far_grads(queries, others, logits, target, here, there, wait, slabs):
    size = queries.shape[0]
    rows = logits.shape[1]
    count, depth, width = slabs.shape
    return pl.pallas_call(
        far_kernel,
        in_specs=[VMEM] * 7,
        out_specs=[HBM] * 2 + [VMEM] * 2,
        out_shape=[
            pltpu.HBM(slabs.shape, BF16),
            pltpu.HBM((rows, size), BF16),
            shape((8, size), F32),
            shape((1, size), F32),
        ],
        scratch_shapes=[
            pltpu.VMEM((2, count, depth // 2, width), BF16),
            pltpu.SemaphoreType.DMA((2,)),
            pltpu.VMEM((rows, size), BF16),
            pltpu.SemaphoreType.DMA,
        ],
        compiler_params=params(),
        name="far_grads",
        cost_estimate=cost(1 << 30, 4),
    )(queries, others, logits, target, here, there, wait)


def near_kernel(
    ranks, queries_ref, others_ref, target_ref, totals_ref, own_logits_ref, other_logits_ref, pieces_ref, near_ref, far_ref,
    kept_ref, *refs,
):
    *given_refs, own_ref, logits, near, far, came, pieces, begun, score, scored, own, own_out, made, left = refs
    first = load(pieces_ref, pieces, begun)
    copies = load_share(0, own_logits_ref, near_ref, far_ref, logits, near, far, came)
    other_scores = load(other_logits_ref, score, scored)
    slabs, depth, width = made.shape
    half = depth // 2

    def store_part(q, piece, block_ref):
        product = SCALE * jnp.dot(piece, block_ref[...], preferred_element_type=F32)
        made[:, q * half : (q + 1) * half, :] = product.astype(BF16).reshape(slabs, half, width)

    other_scores.wait()
    store_part(1, dlogits(score[...], totals_ref[1:2, :], 0, target_ref[1:2, :]), others_ref)
    first.wait()

    def far_piece(c):
        return pieces[row_chunk(logits.shape[0], c), :]

    def near_piece(c):
        return dlogits(logits[row_chunk(logits.shape[0], c), :], totals_ref[0:1, :], c, target_ref[0:1, :])

    def use(c, piece):
        store_part(0, piece, queries_ref)

    total = query_share(copies, far_piece, near_piece, near, far, use)
    place = plane_place(ranks)
    stores = []
    for s in range(slabs):
        out_ref = given_refs[s // 2] if s % 2 else kept_ref.at[s // 2]
        stores.append(load(made.at[place ^ s], out_ref, left.at[s]))
    own[...] = SCALE * total
    stores.append(load(own, own_ref, own_out))
    for store in stores:
        store.wait()


def near_grads(queries, others, target, totals, own_logits, other_logits, pieces, near_slabs, far_slabs, ranks):
    slabs, depth, width = near_slabs.shape
    kept = pltpu.HBM((slabs // 2, depth, width), BF16)
    given = [pltpu.HBM((depth, width), BF16)] * (slabs // 2)
    return pl.pallas_call(
        functools.partial(near_kernel, ranks),
        in_specs=[VMEM] * 4 + [HBM] * 5,
        out_specs=[HBM] * (2 + slabs // 2),
        out_shape=[kept, *given, pltpu.HBM(queries.shape, F32)],
        scratch_shapes=share_scratch(own_logits, near_slabs)
        + [pltpu.VMEM(pieces.shape, BF16), pltpu.SemaphoreType.DMA]
        + [pltpu.VMEM(own_logits.shape, F32), pltpu.SemaphoreType.DMA]
        + [pltpu.VMEM(queries.shape, F32), pltpu.SemaphoreType.DMA]
        + [pltpu.VMEM(near_slabs.shape, BF16), pltpu.SemaphoreType.DMA((slabs,))],
        compiler_params=params(),
        name="near_grads",
        cost_estimate=cost(2 << 30, 8),
    )(queries, others, target, totals, own_logits, other_logits, pieces, near_slabs, far_slabs)


def add_kernel(own_ref, part_ref, *refs):
    out_ref, own, part, made, own_in, part_in, left = refs[-7:]
    pieces = [pl.ds(i * (part.shape[0] // 4), part.shape[0] // 4) for i in range(4)]
    halves = [load(part_ref.at[p], part.at[p], part_in.at[i]) for i, p in enumerate(pieces)]
    if own.shape == part.shape:
        sums = [load(own_ref.at[p], own.at[p], own_in.at[i]) for i, p in enumerate(pieces)]
        own_ref = own
    stores = []
    for i, p in enumerate(pieces):
        halves[i].wait()
        if own_ref is own:
            sums[i].wait()
        rows = slice(p.start, p.start + p.size)
        made[rows, :] = (own_ref[rows, :] + part[rows, :].astype(F32)).astype(BF16)
        stores.append(load(made.at[p], out_ref.at[p], left.at[i]))
    for store in stores:
        store.wait()


def add_parts(own, part, hint, *waits):
    sems = pltpu.SemaphoreType.DMA((4,))
    return pl.pallas_call(
        add_kernel,
        in_specs=[HBM if waits else VMEM, ANY] + [ANY] * len(waits),
        out_specs=HBM,
        out_shape=pltpu.HBM(own.shape, BF16),
        scratch_shapes=[
            pltpu.VMEM(own.shape if waits else (8, 128), F32),
            pltpu.VMEM(own.shape, BF16),
            pltpu.VMEM(own.shape, BF16),
        ]
        + [sems] * 3,
        compiler_params=params(),
        name="add_parts",
        cost_estimate=cost(hint, 4),
    )(in_hbm(own) if waits else own, part, *waits)


def on_device(queries, passages, block_ids, positives):
    height, blocks, width = passages.shape
    refs = block_ids.shape[1]
    groups, planes, ranks = lax.axis_size("group"), lax.axis_size("z"), lax.axis_size("rank")
    slabs = groups * ranks
    z = lax.axis_index("z")
    to_pair = [(i, i ^ 1) for i in range(planes)]
    across = [(i, planes - 1 - i) for i in range(planes)]

    def exchange(slab_array):
        return lax.all_to_all(slab_array, PLANE, split_axis=0, concat_axis=0, tiled=True)

    ids = block_ids.T
    own_rows = jnp.transpose(passages, (1, 0, 2))
    near_slabs = in_hbm(exchange(gather_rows(ids, own_rows, slabs, planes, ranks, 0)))
    pair_rows = lax.ppermute(passages.reshape(height * blocks, width), "z", to_pair)
    inner = [pair for pair in across if 0 < pair[0] < planes - 1]
    outer = [pair for pair in across if pair not in inner]
    others_inner = lax.ppermute(queries, "z", inner)
    others_positives = lax.ppermute(positives, "z", across).reshape(1, -1)

    table = block_ids.reshape(groups, planes, ranks, refs)
    both = jnp.stack([jnp.take(table, z, axis=1), jnp.take(table, planes - 1 - z, axis=1)], axis=2)
    place = (jnp.arange(height, dtype=jnp.int32) * blocks + both.reshape(-1, 1)).reshape(1, -1)
    spread = (jnp.arange(height * blocks, dtype=jnp.int32)[:, None] == place).astype(BF16)
    by_shift = jnp.take(both.reshape(slabs, -1), plane_place(ranks) ^ jnp.arange(slabs), axis=0)
    near_place = (jnp.arange(height, dtype=jnp.int32) * blocks + by_shift.reshape(-1, 1)).reshape(1, -1)
    near_spread = (jnp.arange(height * blocks, dtype=jnp.int32)[:, None] == near_place).astype(BF16)
    far_sent = select_rows(spread, pair_rows, slabs)
    others_outer = lax.ppermute(after(copy_rows(in_hbm(queries)), in_hbm(far_sent), where=HBM), "z", outer)
    far_slabs = in_hbm(exchange(far_sent))

    chosen = positives.reshape(1, -1)
    chosen_others = others_positives
    places = [functools.partial(place_of, far, planes, ranks, refs, height) for far in range(2)]
    own_logits, own_stats, own = own_half(in_hbm(queries), near_slabs, chosen, places[0])
    other_logits, saved_logits, other_stats, others, near_rows = other_half(
        others_inner, others_outer, near_slabs, chosen_others, places[0]
    )
    far_logits, stats, near_target, far_target, far_rows = rest_half(
        own, others, far_slabs, chosen, chosen_others, own_stats, other_stats, places
    )
    partner = lax.ppermute(stats, "z", across)
    sums, hit = early_grads(stats, near_target, far_target, other_logits, far_logits, near_rows, far_rows)
    own_logits, other_logits = in_hbm(own_logits), in_hbm(saved_logits)
    far_contrib, pieces, totals, loss = far_grads(
        own, others, far_logits, far_target, stats, partner, hit, far_slabs
    )
    pieces = in_hbm(pieces)
    other_part = other_grads(stats, totals, near_target, far_target, sums, hit, pieces)
    far_back = in_hbm(exchange(far_contrib).reshape(-1, width))
    kept, *given, own_grad = near_grads(
        own, others, near_target, totals, own_logits, other_logits, pieces, near_slabs, far_slabs, ranks
    )
    joined = join_cores(kept, [lax.ppermute(array, PLANE, [(i, i ^ 1) for i in range(slabs)]) for array in given])
    own_part = lax.ppermute(other_part, "z", across)
    far_sum = segment_rows(spread, [far_back])
    pair_sum = lax.ppermute(far_sum, "z", to_pair)
    near_back = [
        lax.ppermute(array, PLANE, [(i, i ^ (2 * g)) for i in range(slabs)]) if g else array
        for g, array in enumerate(joined)
    ]
    query_grad = add_parts(own_grad, own_part, BUSY, in_hbm(far_sum))
    near_sum = segment_rows(near_spread, near_back, in_hbm(query_grad))
    row_sum = add_parts(near_sum, pair_sum, 1 << 20)
    return loss.reshape(-1), query_grad, row_sum.reshape(passages.shape)


def solution(mesh):
    groups, members = mesh.devices.shape
    split = Mesh(mesh.devices.reshape(groups, PLANES, members // PLANES), ("group", "z", "rank"))
    rows = ("group", "z", "rank")
    return jax.shard_map(
        on_device,
        mesh=split,
        in_specs=(P(rows, None), P(rows, None, None), P(), P(rows)),
        out_specs=(P(rows), P(rows, None), P(rows, None, None)),
        check_vma=False,
    )
```

```python
import functools

import jax
import jax.numpy as jnp
from jax import lax
from jax.experimental import pallas as pl
from jax.experimental.pallas import tpu as pltpu
from jax.sharding import Mesh
from jax.sharding import PartitionSpec as P

SCALE = 0.8
PLANES = 4
CHUNKS = 1
BF16 = jnp.bfloat16
F32 = jnp.float32
BUSY = 1 << 37
PLANE = ("group", "rank")
ANY = pl.BlockSpec(memory_space=pl.ANY)
HBM = pl.BlockSpec(memory_space=pltpu.HBM)
VMEM = pl.BlockSpec(memory_space=pltpu.VMEM)
SMEM = pl.BlockSpec(memory_space=pltpu.SMEM)


def params():
    return pltpu.CompilerParams(vmem_limit_bytes=28 << 20)


def cost(flops, mib):
    return pl.CostEstimate(flops=flops, bytes_accessed=mib << 20, transcendentals=0)


def in_hbm(array):
    return pltpu.with_memory_space_constraint(array, pltpu.HBM)


def shape(dims, dtype):
    return jax.ShapeDtypeStruct(dims, dtype)


def after_kernel(*refs):
    del refs


def after(array, *others, where=VMEM):
    return pl.pallas_call(
        after_kernel,
        in_specs=[ANY] + [where] * len(others),
        out_specs=ANY,
        out_shape=shape(array.shape, array.dtype),
        input_output_aliases={0: 0},
        name="after",
    )(array, *others)


def copy_kernel(source_ref, out_ref, held, done):
    pieces = [pl.ds(i * (held.shape[0] // 4), held.shape[0] // 4) for i in range(4)]
    loads = [load(source_ref.at[p], held.at[p], done.at[0, i]) for i, p in enumerate(pieces)]
    stores = []
    for i, p in enumerate(pieces):
        loads[i].wait()
        stores.append(load(held.at[p], out_ref.at[p], done.at[1, i]))
    for store in stores:
        store.wait()


def copy_rows(array):
    return pl.pallas_call(
        copy_kernel,
        in_specs=[HBM],
        out_specs=HBM,
        out_shape=pltpu.HBM(array.shape, BF16),
        scratch_shapes=[pltpu.VMEM(array.shape, BF16), pltpu.SemaphoreType.DMA((2, 4))],
        compiler_params=params(),
        name="copy_rows",
        cost_estimate=cost(0, 2),
    )(array)


def gather_kernel(planes, ranks, ids, rows_ref, out_ref, made, left):
    slabs, depth, width = out_ref.shape
    height = rows_ref.shape[1]
    refs = ids.shape[0]
    z = lax.axis_index("z")

    def sent(slab):
        return pltpu.make_async_copy(made.at[slab], out_ref.at[slab], left.at[slab])

    def fill(slab, carry):
        for pick in range(2 * refs):
            there = z if pick < refs else planes - 1 - z
            owner = (slab // ranks * planes + there) * ranks + slab % ranks
            made[slab, pick * height : (pick + 1) * height, :] = rows_ref[ids[pick % refs, owner]]
        sent(slab).start()
        return carry

    def drain(slab, carry):
        sent(slab).wait()
        return carry

    lax.fori_loop(0, slabs, fill, 0)
    lax.fori_loop(0, slabs, drain, 0)


def gather_rows(ids, rows, slabs, planes, ranks, flops):
    blocks, height, width = rows.shape
    dims = (slabs, 2 * ids.shape[0] * height, width)
    return pl.pallas_call(
        functools.partial(gather_kernel, planes, ranks),
        in_specs=[SMEM, VMEM],
        out_specs=HBM,
        out_shape=pltpu.HBM(dims, BF16),
        scratch_shapes=[pltpu.VMEM(dims, BF16), pltpu.SemaphoreType.DMA((slabs,))],
        compiler_params=params(),
        name="gather_rows",
        cost_estimate=cost(flops, 4),
    )(ids, rows)


def select_kernel(spread_ref, rows_ref, out_ref, made, left):
    slabs, depth, width = out_ref.shape
    part = slabs // 2
    stores = []
    for c in range(2):
        some = slice(c * part, (c + 1) * part)
        lanes = slice(c * part * depth, (c + 1) * part * depth)
        product = lax.dot_general(
            spread_ref[:, lanes], rows_ref[...], (((0,), (0,)), ((), ())), preferred_element_type=F32
        )
        made[some] = product.astype(BF16).reshape(part, depth, width)
        some = pl.ds(c * part, part)
        stores.append(load(made.at[some], out_ref.at[some], left.at[c]))
    for store in stores:
        store.wait()


def select_rows(spread, rows, slabs):
    dims = (slabs, spread.shape[1] // slabs, rows.shape[1])
    return pl.pallas_call(
        select_kernel,
        in_specs=[VMEM, VMEM],
        out_specs=HBM,
        out_shape=pltpu.HBM(dims, BF16),
        scratch_shapes=[pltpu.VMEM(dims, BF16), pltpu.SemaphoreType.DMA((2,))],
        compiler_params=params(),
        name="select_rows",
        cost_estimate=cost(BUSY, 4),
    )(spread, rows)


def plane_place(ranks):
    return lax.axis_index("group") * ranks + lax.axis_index("rank")


def join_kernel(kept_ref, *refs):
    chips, depth, _ = kept_ref.shape
    given_refs = refs[:chips]
    *out_refs, held, arrived, left = refs[chips:]
    for g in range(chips):
        load(kept_ref.at[g], held.at[g, pl.ds(0, depth)], arrived.at[g, 0])
        load(given_refs[g], held.at[g, pl.ds(depth, depth)], arrived.at[g, 1])
    for g in range(chips):
        pltpu.make_async_copy(kept_ref.at[g], held.at[g, pl.ds(0, depth)], arrived.at[g, 0]).wait()
        pltpu.make_async_copy(given_refs[g], held.at[g, pl.ds(depth, depth)], arrived.at[g, 1]).wait()
        load(held.at[g], out_refs[g], left.at[g])
    for g in range(chips):
        pltpu.make_async_copy(held.at[g], out_refs[g], left.at[g]).wait()


def join_cores(kept, given):
    chips, depth, width = kept.shape
    return pl.pallas_call(
        join_kernel,
        in_specs=[HBM] + [ANY] * chips,
        out_specs=[HBM] * chips,
        out_shape=[pltpu.HBM((2 * depth, width), BF16)] * chips,
        scratch_shapes=[
            pltpu.VMEM((chips, 2 * depth, width), BF16),
            pltpu.SemaphoreType.DMA((chips, 2)),
            pltpu.SemaphoreType.DMA((chips,)),
        ],
        compiler_params=params(),
        name="join_cores",
        cost_estimate=cost(1 << 20, 4),
    )(kept, *given)


def segment_kernel(stripes, arrays, spread_ref, *refs):
    slab_refs = refs[:arrays]
    out_ref, held, result, arrived, left = refs[-5:]
    tile = out_ref.shape[1] // stripes
    depth = held.shape[1] // arrays
    columns = [pl.ds(t * tile, tile) for t in range(stripes)]
    loads = [
        Several(
            [
                load(ref.at[:, columns[t]], held.at[t, pl.ds(i * depth, depth)], arrived.at[t, i])
                for i, ref in enumerate(slab_refs)
            ]
        )
        for t in range(stripes)
    ]
    stores = []
    for t in range(stripes):
        loads[t].wait()
        total = jnp.dot(spread_ref[...], held[t], preferred_element_type=F32)
        if out_ref.dtype == F32:
            out_ref[:, t * tile : (t + 1) * tile] = total
        else:
            result[t] = total.astype(BF16)
            stores.append(load(result.at[t], out_ref.at[:, columns[t]], left.at[t]))
    for store in stores:
        store.wait()


class Several:
    def __init__(self, copies):
        self.copies = copies

    def wait(self):
        for copy in self.copies:
            copy.wait()


def segment_rows(spread, arrays, wait=None):
    stripes = 1
    rows, depth = spread.shape
    width = arrays[0].shape[-1]
    tile = width // stripes
    extra = [] if wait is None else [wait]
    return pl.pallas_call(
        functools.partial(segment_kernel, stripes, len(arrays)),
        in_specs=[VMEM] + [ANY] * (len(arrays) + len(extra)),
        out_specs=VMEM if extra else HBM,
        out_shape=shape((rows, width), F32) if extra else pltpu.HBM((rows, width), BF16),
        scratch_shapes=[
            pltpu.VMEM((stripes, depth, tile), BF16),
            pltpu.VMEM((stripes, rows, tile), BF16),
            pltpu.SemaphoreType.DMA((stripes, len(arrays))),
            pltpu.SemaphoreType.DMA((stripes,)),
        ],
        compiler_params=params(),
        name="segment_rows",
        cost_estimate=cost(BUSY if extra else 1 << 30, 4),
    )(spread, *arrays, *extra)


def candidates(slabs_ref, q, chunk):
    slabs, depth, width = slabs_ref.shape
    part, half = slabs // CHUNKS, depth // 2
    block = slabs_ref[chunk * part : (chunk + 1) * part, q * half : (q + 1) * half, :]
    return block.reshape(part * half, width)


def hits(rows, chunk, target_row):
    row = lax.broadcasted_iota(jnp.int32, (rows, target_row.shape[1]), 0)
    return row + chunk * rows == target_row


def joined(a, b):
    top = jnp.maximum(a[0], b[0])
    return top, a[1] * jnp.exp(a[0] - top) + b[1] * jnp.exp(b[0] - top), a[2] + b[2]


def stat_rows(ref, q):
    return [ref[4 * q + i : 4 * q + i + 1, :] for i in range(3)]


def chunk_rows(ref, chunk):
    rows = ref.shape[1] // CHUNKS
    return slice(chunk * rows, (chunk + 1) * rows)


def place_of(far, planes, ranks, refs, height, chosen):
    owner = chosen // height
    spot = (owner // (planes * ranks) * ranks + owner % ranks) * (refs * height) + chosen % height
    return jnp.where(owner // ranks % planes == lax.axis_index("z") ^ far, spot, -1)


def load(source, held, arrived):
    copy = pltpu.make_async_copy(source, held, arrived)
    copy.start()
    return copy


def part_of(size, chunk):
    return pl.ds(chunk * (size // CHUNKS), size // CHUNKS)


def load_chunks(source, held, arrived):
    parts = [part_of(source.shape[0], c) for c in range(CHUNKS)]
    return [load(source.at[part], held.at[part], arrived.at[c]) for c, part in enumerate(parts)]


def block_logits(block_ref, slab_part, target_row, put):
    stats = None
    for c in range(CHUNKS):
        block = lax.dot_general(slab_part(c), block_ref[...], (((1,), (1,)), ((), ())), preferred_element_type=F32)
        block = SCALE * block
        put(c, block)
        top = jnp.max(block, axis=0, keepdims=True)
        total = jnp.sum(jnp.exp(block - top), axis=0, keepdims=True)
        hit = hits(block.shape[0], c, target_row)
        pick = jnp.sum(jnp.where(hit, block, 0.0), axis=0, keepdims=True)
        here = (top, total, pick)
        stats = here if c == 0 else joined(stats, here)
    return stats


def put_stats(stats_ref, q, stats):
    for i in range(3):
        stats_ref[4 * q + i : 4 * q + i + 1, :] = stats[i]
    stats_ref[4 * q + 3 : 4 * q + 4, :] = jnp.zeros_like(stats[0])


def held_rows(held, chunk):
    slabs = held.shape[0] // CHUNKS
    return held[chunk * slabs : (chunk + 1) * slabs].reshape(slabs * held.shape[1], held.shape[2])


def row_chunk(rows, chunk):
    return slice(chunk * rows // CHUNKS, (chunk + 1) * rows // CHUNKS)


def put_targets(place, target_ref, chosen_ref, chosen_others_ref):
    target_ref[...] = jnp.full(target_ref.shape, -1, jnp.int32)
    target_ref[0:1, :] = place(chosen_ref[...])
    target_ref[1:2, :] = place(chosen_others_ref[...])


def own_kernel(place, queries_ref, slabs_ref, chosen_ref, logits_ref, stats_ref, kept_ref, held, made, arrived, came, left):
    half = slabs_ref.shape[1] // 2
    loads = load_chunks(slabs_ref.at[:, pl.ds(0, half)], held, arrived)
    load(queries_ref, kept_ref, came).wait()
    stores = []

    def slab_part(c):
        loads[c].wait()
        return held_rows(held, c)

    def put(c, block):
        part = part_of(logits_ref.shape[0], c)
        made[row_chunk(made.shape[0], c), :] = block
        stores.append(load(made.at[part], logits_ref.at[part], left.at[c]))

    stats = block_logits(kept_ref, slab_part, place(chosen_ref[...]), put)
    put_stats(stats_ref, 0, stats)
    put_stats(stats_ref, 1, stats)
    for store in stores:
        store.wait()


def own_half(queries, slabs, chosen, place):
    size, width = queries.shape
    rows = slabs.shape[0] * slabs.shape[1] // 2
    return pl.pallas_call(
        functools.partial(own_kernel, place),
        in_specs=[HBM, HBM, VMEM],
        out_specs=[HBM, VMEM, VMEM],
        out_shape=[pltpu.HBM((rows, size), F32), shape((8, size), F32), shape((size, width), BF16)],
        scratch_shapes=[
            pltpu.VMEM((slabs.shape[0], slabs.shape[1] // 2, width), BF16),
            pltpu.VMEM((rows, size), F32),
            pltpu.SemaphoreType.DMA((CHUNKS,)),
            pltpu.SemaphoreType.DMA,
            pltpu.SemaphoreType.DMA((CHUNKS,)),
        ],
        compiler_params=params(),
        name="own_half",
        cost_estimate=cost(BUSY, 4),
    )(queries, slabs, chosen)


def other_half_kernel(
    place, inner_ref, outer_ref, near_ref, chosen_ref,
    logits_ref, saved_ref, stats_ref, others_ref, near_rows, near_in, left, came,
):
    half = near_ref.shape[1] // 2
    z = lax.axis_index("z")
    inner = (z > 0) & (z < lax.axis_size("z") - 1)

    @pl.when(inner)
    def _():
        load(inner_ref, others_ref, came)

    @pl.when(jnp.logical_not(inner))
    def _():
        load(outer_ref, others_ref, came)

    whole = [pltpu.make_async_copy(outer_ref, others_ref, came)]
    near_load = load(near_ref.at[:, pl.ds(half, half)], near_rows, near_in)
    stores = []

    def put(c, block):
        logits_ref[...] = block
        stores.append(load(logits_ref, saved_ref, left))

    for copy in whole:
        copy.wait()
    near_load.wait()
    stats = block_logits(others_ref, lambda c: held_rows(near_rows, c), place(chosen_ref[...]), put)
    put_stats(stats_ref, 0, stats)
    put_stats(stats_ref, 1, stats)
    for store in stores:
        store.wait()


def other_half(inner, outer, near_slabs, chosen, place):
    size, width = inner.shape
    rows = near_slabs.shape[0] * near_slabs.shape[1] // 2
    part = (near_slabs.shape[0], near_slabs.shape[1] // 2, width)
    return pl.pallas_call(
        functools.partial(other_half_kernel, place),
        in_specs=[ANY] * 2 + [HBM, VMEM],
        out_specs=[VMEM, HBM] + [VMEM] * 3,
        out_shape=[
            shape((rows, size), F32),
            pltpu.HBM((rows, size), F32),
            shape((8, size), F32),
            shape((size, width), BF16),
            shape(part, BF16),
        ],
        scratch_shapes=[pltpu.SemaphoreType.DMA] * 3,
        compiler_params=params(),
        name="other_half",
        cost_estimate=cost(BUSY, 8),
    )(inner, outer, near_slabs, chosen)


def rest_kernel(
    near_place, far_place, queries_ref, others_ref, far_ref, chosen_ref, chosen_others_ref, own_stats_ref, other_stats_ref,
    far_logits_ref, stats_ref, near_target_ref, far_target_ref, far_rows, held, far_in, held_in,
):
    half = far_ref.shape[1] // 2
    held_loads = load_chunks(far_ref.at[:, pl.ds(0, half)], held, held_in)
    far_loads = load_chunks(far_ref.at[:, pl.ds(half, half)], far_rows, far_in)
    put_targets(near_place, near_target_ref, chosen_ref, chosen_others_ref)
    put_targets(far_place, far_target_ref, chosen_ref, chosen_others_ref)

    def part(loads, rows):
        def get(c):
            loads[c].wait()
            return held_rows(rows, c)

        return get

    def put_far(q):
        def put(c, block):
            far_logits_ref[q, chunk_rows(far_logits_ref, c), :] = block

        return put

    own = block_logits(queries_ref, part(held_loads, held), far_target_ref[0:1, :], put_far(0))
    put_stats(stats_ref, 0, joined(stat_rows(own_stats_ref, 0), own))
    far = block_logits(others_ref, part(far_loads, far_rows), far_target_ref[1:2, :], put_far(1))
    put_stats(stats_ref, 1, joined(stat_rows(other_stats_ref, 0), far))


def rest_half(queries, others, far_slabs, chosen, chosen_others, own_stats, other_stats, places):
    size, width = queries.shape
    rows = far_slabs.shape[0] * far_slabs.shape[1] // 2
    part = (far_slabs.shape[0], far_slabs.shape[1] // 2, width)
    chunk_sems = pltpu.SemaphoreType.DMA((CHUNKS,))
    return pl.pallas_call(
        functools.partial(rest_kernel, *places),
        in_specs=[VMEM] * 2 + [HBM] + [VMEM] * 4,
        out_specs=[VMEM] * 5,
        out_shape=[
            shape((2, rows, size), F32),
            shape((8, size), F32),
            shape((8, size), jnp.int32),
            shape((8, size), jnp.int32),
            shape(part, BF16),
        ],
        scratch_shapes=[pltpu.VMEM(part, BF16)] + [chunk_sems] * 2,
        compiler_params=params(),
        name="rest_half",
        cost_estimate=cost(3 << 29, 8),
    )(queries, others, far_slabs, chosen, chosen_others, own_stats, other_stats)


def log_totals(here_ref, there_ref):
    out = []
    for q in range(2):
        top, total, pick = joined(stat_rows(here_ref, q), stat_rows(there_ref, 1 - q))
        out.append((top + jnp.log(total), pick))
    return out


def dlogits(logits, log_total, chunk, target_row):
    hit = hits(logits.shape[0], chunk, target_row)
    return (jnp.exp(logits - log_total) - jnp.where(hit, 1.0, 0.0)).astype(BF16)


def send_contrib(made, out_ref, left, chunk, q, piece, block, complete):
    slabs, depth, width = out_ref.shape
    part, half = slabs // CHUNKS, depth // 2
    product = SCALE * jnp.dot(piece, block, preferred_element_type=F32)
    made[chunk, :, q * half : (q + 1) * half, :] = product.astype(BF16).reshape(part, half, width)
    if not complete:
        return []
    store = pltpu.make_async_copy(made.at[chunk], out_ref.at[pl.ds(chunk * part, part)], left.at[chunk])
    store.start()
    return [store]


def contrib_scratch(slabs):
    return [
        pltpu.VMEM((CHUNKS, slabs.shape[0] // CHUNKS) + slabs.shape[1:], BF16),
        pltpu.SemaphoreType.DMA((CHUNKS,)),
    ]


def load_share(q, logits_ref, near_ref, far_ref, logits, near, far, came):
    rows, slabs, half = logits_ref.shape[0], near_ref.shape[0], near_ref.shape[1] // 2
    picks = pl.ds(q * half, half)
    copies = []
    for c in range(CHUNKS):
        part, some = part_of(rows, c), part_of(slabs, c)
        copies.append(
            [
                load(far_ref.at[some, picks], far.at[some], came.at[0, c]),
                load(logits_ref.at[part], logits.at[part], came.at[1, c]),
                load(near_ref.at[some, picks], near.at[some], came.at[2, c]),
            ]
        )
    return copies


def query_share(copies, far_piece, near_piece, near, far, use):
    dims = (((0,), (0,)), ((), ()))
    slabs, half, width = near.shape
    total = None
    for c in range(CHUNKS):
        some = slice(c * slabs // CHUNKS, (c + 1) * slabs // CHUNKS)
        rows = slabs // CHUNKS * half
        piece = far_piece(c)
        copies[c][0].wait()
        share = lax.dot_general(piece, far[some].reshape(rows, width), dims, preferred_element_type=F32)
        copies[c][1].wait()
        piece = near_piece(c)
        copies[c][2].wait()
        share += lax.dot_general(piece, near[some].reshape(rows, width), dims, preferred_element_type=F32)
        total = share if c == 0 else total + share
        if use is not None:
            use(c, piece)
    return total


def share_scratch(logits, slabs):
    part = (slabs.shape[0], slabs.shape[1] // 2, slabs.shape[2])
    return [
        pltpu.VMEM(logits.shape, F32),
        pltpu.VMEM(part, BF16),
        pltpu.VMEM(part, BF16),
        pltpu.SemaphoreType.DMA((3, CHUNKS)),
    ]


def early_kernel(stats_ref, near_target_ref, far_target_ref, near_logits_ref, far_logits_ref, near_ref, far_ref, sums_ref, hit_ref):
    dims = (((0,), (0,)), ((), ()))
    top = stats_ref[4:5, :]
    rows = near_logits_ref.shape[0]
    for c in range(CHUNKS):
        part = row_chunk(rows, c)
        for i, (score, target_ref, slab_ref) in enumerate(
            ((near_logits_ref[part, :], near_target_ref, near_ref), (far_logits_ref[1, part, :], far_target_ref, far_ref))
        ):
            block = held_rows(slab_ref, c)
            weight = jnp.exp(score - top).astype(BF16)
            hit = jnp.where(hits(score.shape[0], c, target_ref[1:2, :]), 1.0, 0.0).astype(BF16)
            product = lax.dot_general(weight, block, dims, preferred_element_type=F32)
            picked = lax.dot_general(hit, block, dims, preferred_element_type=F32)
            if c == 0 and i == 0:
                sums_ref[...] = product
                hit_ref[...] = picked
            else:
                sums_ref[...] += product
                hit_ref[...] += picked


def early_grads(stats, near_target, far_target, near_logits, far_logits, near_rows, far_rows):
    size, width = near_logits.shape[1], near_rows.shape[2]
    return pl.pallas_call(
        early_kernel,
        in_specs=[VMEM] * 7,
        out_specs=[VMEM] * 2,
        out_shape=[shape((size, width), F32)] * 2,
        compiler_params=params(),
        name="early_grads",
        cost_estimate=cost(BUSY, 4),
    )(stats, near_target, far_target, near_logits, far_logits, near_rows, far_rows)


def other_kernel(here_ref, totals_ref, near_target_ref, far_target_ref, sums_ref, hit_ref, wait_ref, other_ref, made, left):
    del wait_ref
    total = totals_ref[1:2, :]
    top, _, pick = stat_rows(here_ref, 1)
    held = jnp.maximum(near_target_ref[1:2, :], far_target_ref[1:2, :]) >= 0
    scale = jnp.exp(top - total)
    counted = scale * jnp.exp(jnp.where(held, pick - top, 0.0)).astype(BF16).astype(F32)
    wanted = (jnp.exp(jnp.where(held, pick - total, 0.0)) - 1.0).astype(BF16).astype(F32)
    rows = [scale, jnp.where(held, wanted - counted, 0.0)]
    columns = jnp.transpose(jnp.concatenate(rows + [jnp.zeros_like(scale)] * 6, axis=0))
    stores = []
    size = made.shape[0] // 4
    for c in range(4):
        part = slice(c * size, (c + 1) * size)
        share = columns[part, 0:1] * sums_ref[part, :] + columns[part, 1:2] * hit_ref[part, :]
        made[part, :] = (SCALE * share).astype(BF16)
        some = pl.ds(c * size, size)
        stores.append(load(made.at[some], other_ref.at[some], left.at[c]))
    for store in stores:
        store.wait()


def other_grads(here, totals, near_target, far_target, sums, hit, wait):
    size, width = sums.shape
    return pl.pallas_call(
        other_kernel,
        in_specs=[VMEM] * 6 + [HBM],
        out_specs=HBM,
        out_shape=pltpu.HBM((size, width), BF16),
        scratch_shapes=[pltpu.VMEM((size, width), BF16), pltpu.SemaphoreType.DMA((4,))],
        compiler_params=params(),
        name="other_grads",
        cost_estimate=cost(1 << 20, 4),
    )(here, totals, near_target, far_target, sums, hit, wait)


def far_kernel(
    queries_ref, others_ref, logits_ref, target_ref, here_ref, there_ref, wait_ref,
    contrib_ref, pieces_ref, totals_ref, loss_ref, made, left, pieces, pieces_out,
):
    del wait_ref
    totals = log_totals(here_ref, there_ref)
    totals_ref[...] = jnp.zeros_like(totals_ref)
    for q in range(2):
        totals_ref[q : q + 1, :] = totals[q][0]
    loss_ref[...] = totals[0][0] - totals[0][1]
    slabs, depth, width = contrib_ref.shape
    half = depth // 2
    stores = []
    for q, block_ref in enumerate((queries_ref, others_ref)):
        piece = dlogits(logits_ref[q], totals[q][0], 0, target_ref[q : q + 1, :])
        if q == 0:
            pieces[...] = piece
            stores.append(load(pieces, pieces_ref, pieces_out))
        product = SCALE * jnp.dot(piece, block_ref[...], preferred_element_type=F32)
        made[q] = product.astype(BF16).reshape(slabs, half, width)
        stores.append(load(made.at[q], contrib_ref.at[:, pl.ds(q * half, half)], left.at[q]))
    for store in stores:
        store.wait()


def far_grads(queries, others, logits, target, here, there, wait, slabs):
    size = queries.shape[0]
    rows = logits.shape[1]
    count, depth, width = slabs.shape
    return pl.pallas_call(
        far_kernel,
        in_specs=[VMEM] * 7,
        out_specs=[HBM] * 2 + [VMEM] * 2,
        out_shape=[
            pltpu.HBM(slabs.shape, BF16),
            pltpu.HBM((rows, size), BF16),
            shape((8, size), F32),
            shape((1, size), F32),
        ],
        scratch_shapes=[
            pltpu.VMEM((2, count, depth // 2, width), BF16),
            pltpu.SemaphoreType.DMA((2,)),
            pltpu.VMEM((rows, size), BF16),
            pltpu.SemaphoreType.DMA,
        ],
        compiler_params=params(),
        name="far_grads",
        cost_estimate=cost(1 << 30, 4),
    )(queries, others, logits, target, here, there, wait)


def near_kernel(
    ranks, queries_ref, others_ref, target_ref, totals_ref, own_logits_ref, other_logits_ref, pieces_ref, near_ref, far_ref,
    kept_ref, *refs,
):
    *given_refs, own_ref, logits, near, far, came, pieces, begun, score, scored, own, own_out, made, left = refs
    first = load(pieces_ref, pieces, begun)
    copies = load_share(0, own_logits_ref, near_ref, far_ref, logits, near, far, came)
    other_scores = load(other_logits_ref, score, scored)
    slabs, depth, width = made.shape
    half = depth // 2

    def store_part(q, piece, block_ref):
        product = SCALE * jnp.dot(piece, block_ref[...], preferred_element_type=F32)
        made[:, q * half : (q + 1) * half, :] = product.astype(BF16).reshape(slabs, half, width)

    other_scores.wait()
    store_part(1, dlogits(score[...], totals_ref[1:2, :], 0, target_ref[1:2, :]), others_ref)
    first.wait()

    def far_piece(c):
        return pieces[row_chunk(logits.shape[0], c), :]

    def near_piece(c):
        return dlogits(logits[row_chunk(logits.shape[0], c), :], totals_ref[0:1, :], c, target_ref[0:1, :])

    def use(c, piece):
        store_part(0, piece, queries_ref)

    total = query_share(copies, far_piece, near_piece, near, far, use)
    place = plane_place(ranks)
    stores = []
    for s in range(slabs):
        out_ref = given_refs[s // 2] if s % 2 else kept_ref.at[s // 2]
        stores.append(load(made.at[place ^ s], out_ref, left.at[s]))
    own[...] = SCALE * total
    stores.append(load(own, own_ref, own_out))
    for store in stores:
        store.wait()


def near_grads(queries, others, target, totals, own_logits, other_logits, pieces, near_slabs, far_slabs, ranks):
    slabs, depth, width = near_slabs.shape
    kept = pltpu.HBM((slabs // 2, depth, width), BF16)
    given = [pltpu.HBM((depth, width), BF16)] * (slabs // 2)
    return pl.pallas_call(
        functools.partial(near_kernel, ranks),
        in_specs=[VMEM] * 4 + [HBM] * 5,
        out_specs=[HBM] * (2 + slabs // 2),
        out_shape=[kept, *given, pltpu.HBM(queries.shape, F32)],
        scratch_shapes=share_scratch(own_logits, near_slabs)
        + [pltpu.VMEM(pieces.shape, BF16), pltpu.SemaphoreType.DMA]
        + [pltpu.VMEM(own_logits.shape, F32), pltpu.SemaphoreType.DMA]
        + [pltpu.VMEM(queries.shape, F32), pltpu.SemaphoreType.DMA]
        + [pltpu.VMEM(near_slabs.shape, BF16), pltpu.SemaphoreType.DMA((slabs,))],
        compiler_params=params(),
        name="near_grads",
        cost_estimate=cost(2 << 30, 8),
    )(queries, others, target, totals, own_logits, other_logits, pieces, near_slabs, far_slabs)


def add_kernel(own_ref, part_ref, *refs):
    out_ref, own, part, made, own_in, part_in, left = refs[-7:]
    pieces = [pl.ds(i * (part.shape[0] // 4), part.shape[0] // 4) for i in range(4)]
    halves = [load(part_ref.at[p], part.at[p], part_in.at[i]) for i, p in enumerate(pieces)]
    if own.shape == part.shape:
        sums = [load(own_ref.at[p], own.at[p], own_in.at[i]) for i, p in enumerate(pieces)]
        own_ref = own
    stores = []
    for i, p in enumerate(pieces):
        halves[i].wait()
        if own_ref is own:
            sums[i].wait()
        rows = slice(p.start, p.start + p.size)
        made[rows, :] = (own_ref[rows, :] + part[rows, :].astype(F32)).astype(BF16)
        stores.append(load(made.at[p], out_ref.at[p], left.at[i]))
    for store in stores:
        store.wait()


def add_parts(own, part, hint, *waits):
    sems = pltpu.SemaphoreType.DMA((4,))
    return pl.pallas_call(
        add_kernel,
        in_specs=[HBM if waits else VMEM, ANY] + [ANY] * len(waits),
        out_specs=HBM,
        out_shape=pltpu.HBM(own.shape, BF16),
        scratch_shapes=[
            pltpu.VMEM(own.shape if waits else (8, 128), F32),
            pltpu.VMEM(own.shape, BF16),
            pltpu.VMEM(own.shape, BF16),
        ]
        + [sems] * 3,
        compiler_params=params(),
        name="add_parts",
        cost_estimate=cost(hint, 4),
    )(in_hbm(own) if waits else own, part, *waits)


def on_device(queries, passages, block_ids, positives):
    height, blocks, width = passages.shape
    refs = block_ids.shape[1]
    groups, planes, ranks = lax.axis_size("group"), lax.axis_size("z"), lax.axis_size("rank")
    slabs = groups * ranks
    z = lax.axis_index("z")
    to_pair = [(i, i ^ 1) for i in range(planes)]
    across = [(i, planes - 1 - i) for i in range(planes)]

    def exchange(slab_array):
        return lax.all_to_all(slab_array, PLANE, split_axis=0, concat_axis=0, tiled=True)

    ids = block_ids.T
    own_rows = jnp.transpose(passages, (1, 0, 2))
    near_slabs = in_hbm(exchange(gather_rows(ids, own_rows, slabs, planes, ranks, 0)))
    pair_rows = lax.ppermute(passages.reshape(height * blocks, width), "z", to_pair)
    inner = [pair for pair in across if 0 < pair[0] < planes - 1]
    outer = [pair for pair in across if pair not in inner]
    others_inner = lax.ppermute(queries, "z", inner)
    others_positives = lax.ppermute(positives, "z", across).reshape(1, -1)

    table = block_ids.reshape(groups, planes, ranks, refs)
    both = jnp.stack([jnp.take(table, z, axis=1), jnp.take(table, planes - 1 - z, axis=1)], axis=2)
    place = (jnp.arange(height, dtype=jnp.int32) * blocks + both.reshape(-1, 1)).reshape(1, -1)
    spread = (jnp.arange(height * blocks, dtype=jnp.int32)[:, None] == place).astype(BF16)
    by_shift = jnp.take(both.reshape(slabs, -1), plane_place(ranks) ^ jnp.arange(slabs), axis=0)
    near_place = (jnp.arange(height, dtype=jnp.int32) * blocks + by_shift.reshape(-1, 1)).reshape(1, -1)
    near_spread = (jnp.arange(height * blocks, dtype=jnp.int32)[:, None] == near_place).astype(BF16)
    far_sent = select_rows(spread, pair_rows, slabs)
    others_outer = lax.ppermute(after(copy_rows(in_hbm(queries)), in_hbm(far_sent), where=HBM), "z", outer)
    far_slabs = in_hbm(exchange(far_sent))

    chosen = positives.reshape(1, -1)
    chosen_others = others_positives
    places = [functools.partial(place_of, far, planes, ranks, refs, height) for far in range(2)]
    own_logits, own_stats, own = own_half(in_hbm(queries), near_slabs, chosen, places[0])
    other_logits, saved_logits, other_stats, others, near_rows = other_half(
        others_inner, others_outer, near_slabs, chosen_others, places[0]
    )
    far_logits, stats, near_target, far_target, far_rows = rest_half(
        own, others, far_slabs, chosen, chosen_others, own_stats, other_stats, places
    )
    partner = lax.ppermute(stats, "z", across)
    sums, hit = early_grads(stats, near_target, far_target, other_logits, far_logits, near_rows, far_rows)
    own_logits, other_logits = in_hbm(own_logits), in_hbm(saved_logits)
    far_contrib, pieces, totals, loss = far_grads(
        own, others, far_logits, far_target, stats, partner, hit, far_slabs
    )
    pieces = in_hbm(pieces)
    other_part = other_grads(stats, totals, near_target, far_target, sums, hit, pieces)
    far_back = in_hbm(exchange(far_contrib).reshape(-1, width))
    kept, *given, own_grad = near_grads(
        own, others, near_target, totals, own_logits, other_logits, pieces, near_slabs, far_slabs, ranks
    )
    joined = join_cores(kept, [lax.ppermute(array, PLANE, [(i, i ^ 1) for i in range(slabs)]) for array in given])
    own_part = lax.ppermute(other_part, "z", across)
    far_sum = segment_rows(spread, [far_back])
    pair_sum = lax.ppermute(far_sum, "z", to_pair)
    near_back = [
        lax.ppermute(array, PLANE, [(i, i ^ (2 * g)) for i in range(slabs)]) if g else array
        for g, array in enumerate(joined)
    ]
    query_grad = add_parts(own_grad, own_part, BUSY, in_hbm(far_sum))
    near_sum = segment_rows(near_spread, near_back, in_hbm(query_grad))
    row_sum = add_parts(near_sum, pair_sum, 1 << 20)
    return loss.reshape(-1), query_grad, row_sum.reshape(passages.shape)


def solution(mesh):
    groups, members = mesh.devices.shape
    split = Mesh(mesh.devices.reshape(groups, PLANES, members // PLANES), ("group", "z", "rank"))
    rows = ("group", "z", "rank")
    return jax.shard_map(
        on_device,
        mesh=split,
        in_specs=(P(rows, None), P(rows, None, None), P(), P(rows)),
        out_specs=(P(rows), P(rows, None), P(rows, None, None)),
        check_vma=False,
    )
```
